256 devices in a mesh: tower: 2 (over core), dp: 128 (over z, x, y).
Axes of the slice: x: 4, y: 4, z: 8, core: 2. Of those that a mesh axis runs over, the one named last changes fastest.
Arguments:
- tokens: bfloat16 [65536, 1280], P(('tower', 'dp')), may hold values from -6 to 6
- norm_gain: bfloat16 [1280], replicated, may hold values from 0.5 to 1.5
- router: bfloat16 [1280, 32], replicated, may hold values from -0.15625 to 0.15625
- expert_ids: int32 [65536, 1], P(('tower', 'dp')), may hold values from 0 to 31; in each aligned block of 256 rows (0 to 255, 256 to 511, ...) at most 12 rows name the same one
- up_weights: bfloat16 [1280, 81920], P(None, 'dp'), may hold values from -0.15625 to 0.15625
- down_weights: bfloat16 [81920, 1280], P('dp'), may hold values from -0.125 to 0.125
- cotangent: bfloat16 [65536, 1280], P(('tower', 'dp')), may hold values from -6 to 6
- embeds: bfloat16 [2, 2048, 1024], P('tower', 'dp'), may hold values from -400 to 400
- logit_scale_log: float32 [], replicated, may hold values from 0.7 to 1.6
- pairwise_logit_bias: float32 [], replicated, may hold values from -3 to -1
Outputs:
- tokens_grad: bfloat16 [65536, 1280], P(('tower', 'dp'))
- router_grad: float32 [1280, 32], replicated
- down_grad: float32 [81920, 1280], P('dp')
- embed_grads: float32 [2, 2048, 1024], P('tower', 'dp')
The draws below stay inside these ranges and needn't reach their ends.
Inputs may be any that keep to these rules, and one draw needn't show every extreme that they name: `expert_ids`: within the image tokens of one device (aligned blocks of 256 rows), at most 12 name one expert, and in some block some expert is named by exactly 12 of them.
All inputs are finite; a program needn't handle non-finite values.
Results may differ from the reference program's by a relative error of at most 0.0067.
Values may be sent and summed in bfloat16 or wider, within the bound.
No kernel may reach another device: no remote copies, remote signals or barrier semaphores. Data moves between devices by JAX's collectives and lax.ppermute only.
A program may use at most 128 MiB of HBM per device.

```python
import math
import jax
import jax.numpy as jnp
import numpy as np
from jax import lax

D = 1280
FF = 2560
SHARDS = 4
E = 1024
TOK_DEV = 256
EXPERTS = 32
CAP = 12
IMG_TOKENS = 65536
PAIRS = 2048
N_TOWER = 2
N_DP = 128


def draw_embeds(key, part):
    key = jax.random.fold_in(key, 11)
    row_key, col_key, base_key = jax.random.split(key, 3)
    shape_all = (2, PAIRS, E)
    row_scale = jnp.exp(jax.random.uniform(row_key, (2, PAIRS, 1), jnp.float32, 0.0, math.log(10.0)))
    col_scale = jnp.exp(jax.random.uniform(col_key, (1, 1, E), jnp.float32, 0.0, math.log(10.0)))
    base = jnp.clip(jax.random.normal(base_key, shape_all, jnp.float32), -4.0, 4.0)
    return (base * row_scale * col_scale).astype(jnp.bfloat16)


def block_levels(rng, extent, pieces, least, top_value):
    level = 1.0
    for axis_at, shards_of in pieces:
        heights = jax.random.uniform(jax.random.fold_in(jax.random.fold_in(rng, 6), axis_at), (shards_of,), jnp.float32, least / len(pieces), top_value / len(pieces))
        level = level * jnp.repeat(jnp.exp(heights), extent[axis_at] // shards_of).reshape((-1,) + (1,) * (len(extent) - 1 - axis_at))
    return level


def shared_out(key, own, number, rows, amount, top, most, skew):
    ranking = jax.random.permutation(key, amount)
    heavy_load, common = shares(amount, rows * top, most, skew, True), shares(amount, rows * top, most, skew, False)
    places = jnp.arange(amount)

    def named(sizes, offset_by):
        used = int((sizes > 0).sum())
        fixed = max(1, used // 4)
        shifted = fixed + (places - fixed + offset_by * (used - fixed)) % max(1, amount - fixed)
        return jnp.zeros((amount,), jnp.int32).at[ranking[jnp.where(places < fixed, places, shifted)]].set(jnp.asarray(sizes, jnp.int32))

    sizes = jnp.where(number % 4 == 0, named(heavy_load, number // 4), named(common, number - number // 4 - 1))
    mixed = jax.random.permutation(jax.random.fold_in(own, 3), amount)
    source_of, sink = mixed[0:amount // 2 * 2:2], mixed[1:amount // 2 * 2:2]
    slack = jnp.minimum(sizes[source_of] - 1, most - sizes[sink]) // 2
    slack = jnp.where((source_of == ranking[0]) | (sink == ranking[0]) | (sizes[sink] == 0), 0, jnp.maximum(slack, 0))
    shifted = jax.random.randint(jax.random.fold_in(own, 4), (amount // 2,), 0, 1 << 20) % (slack + 1)
    sizes = sizes.at[source_of].add(-shifted).at[sink].add(shifted)
    members = jnp.searchsorted(jnp.cumsum(sizes), jnp.arange(rows * top), side="right").astype(jnp.int32)
    grid = members.reshape(top, rows).T
    grid = grid[jax.random.permutation(jax.random.fold_in(own, 1), rows)]
    offset_by = jax.random.randint(jax.random.fold_in(own, 2), (rows, 1), 0, top)
    return jnp.take_along_axis(grid, (jnp.arange(top)[None, :] + offset_by) % top, axis=1)


def shares(amount, total, bound, slope, full):
    portions = [(1 << 20) // math.isqrt(rank ** slope) + 1 for rank in range(1, amount + 1)]
    largest = bound if full else min(bound, max(-(-total // amount), total * portions[0] // sum(portions)))
    least = 1 if total - largest >= amount - 1 else 0
    counts, spare = [largest] + [least] * (amount - 1), total - largest - least * (amount - 1)
    while spare > 0:
        candidates = [i for i in range(1, amount) if counts[i] < largest] or [i for i in range(1, amount) if counts[i] < bound]
        pool, budget = sum([portions[i] for i in candidates]), spare
        for i in candidates:
            addition = min(bound - counts[i], max(1, budget * portions[i] // pool), spare)
            counts[i] = counts[i] + addition
            spare = spare - addition
    return np.array(counts)


def gaussian(own_key, dims, width, bound, cuts=(), held_as=jnp.bfloat16):
    loudness = block_levels(own_key, dims, cuts, -0.22, 0.18) if cuts else 1.0
    values = jax.random.normal(own_key, dims, jnp.float32) * width * loudness
    return jnp.minimum(jnp.maximum(values, -bound), bound).astype(held_as)


def setup_inputs(seed: int = 0) -> dict:
    splits = jax.random.split(jax.random.key(seed), 11)
    tokens = gaussian(splits[0], (IMG_TOKENS, D), 1.0, 6.0, ((0, 256),))
    norm_gain = jnp.clip(1.0 + 0.1 * jax.random.normal(splits[1], (D,), jnp.float32), 0.5, 1.5).astype(jnp.bfloat16)
    router = gaussian(splits[2], (D, EXPERTS), D ** -0.5, 0.15625)
    expert_ids_keys = jax.random.split(jax.random.fold_in(splits[3], 1), IMG_TOKENS // TOK_DEV)
    expert_ids_turns = jax.random.permutation(jax.random.fold_in(splits[3], 3), IMG_TOKENS // TOK_DEV)
    expert_ids = jax.vmap(lambda own, number: shared_out(jax.random.fold_in(splits[3], 2), own, number, TOK_DEV, EXPERTS, 1, CAP, 2))(expert_ids_keys, expert_ids_turns).reshape((IMG_TOKENS, 1))
    up_weights = gaussian(splits[4], (D, EXPERTS * FF), D ** -0.5, 0.15625, ((1, 128),))
    down_weights = gaussian(splits[5], (EXPERTS * FF, D), FF ** -0.5, 0.125, ((0, 128),))
    cotangent = gaussian(splits[6], (IMG_TOKENS, D), 1.0, 6.0, ((0, 256),))
    embeds = draw_embeds(jax.random.fold_in(splits[10], 71), 0)
    logit_scale_log = jnp.clip(jax.random.uniform(splits[8], (), jnp.float32, 0.7, 1.6), 0.7, 1.6)
    pairwise_logit_bias = jnp.clip(jax.random.uniform(splits[9], (), jnp.float32, -3.0, -1.0), -3.0, -1.0)
    return dict(tokens=tokens, norm_gain=norm_gain, router=router, expert_ids=expert_ids, up_weights=up_weights, down_weights=down_weights, cotangent=cotangent, embeds=embeds, logit_scale_log=logit_scale_log, pairwise_logit_bias=pairwise_logit_bias)


epsilon = 1e-06
gelu_root = 0.7978845608028654
gelu_cubic = 0.044715

def layer_norm(values, scale_vec):
    center = values - lax.optimization_barrier(jnp.mean(values, axis=-1, keepdims=True))
    spread = lax.optimization_barrier(jnp.mean(center * center, axis=-1, keepdims=True))
    return center * lax.rsqrt(spread + epsilon) * scale_vec.astype(jnp.float32)

def gelu_tanh(values):
    inner = gelu_root * (values + gelu_cubic * values * values * values)
    return 0.5 * values * (1.0 + jnp.tanh(inner))

def gelu_slope(values):
    inner = gelu_root * (values + gelu_cubic * values * values * values)
    tangent = jnp.tanh(inner)
    return 0.5 * (1.0 + tangent) + 0.5 * values * (1.0 - tangent * tangent) * gelu_root * (1.0 + 3.0 * gelu_cubic * values * values)

def shard_sum(left, right):
    product = jnp.einsum('rsf,sfd->rsd', left.astype(jnp.float32), right.astype(jnp.float32))
    rounded = lax.optimization_barrier(product.astype(jnp.bfloat16))
    return lax.optimization_barrier(jnp.sum(rounded.astype(jnp.float32), axis=1))

def reference(tokens, norm_gain, router, expert_ids, up_weights, down_weights, cotangent, embeds, logit_scale_log, pairwise_logit_bias):
    devices_all = N_TOWER * N_DP
    total_rows = tokens.shape[0]
    model_width = tokens.shape[1]
    shard_width = FF // SHARDS
    tokens_f32 = tokens.astype(jnp.float32)
    normed_f32, norm_back = jax.vjp(lambda values: layer_norm(values, norm_gain), tokens_f32)
    normed = normed_f32.astype(jnp.bfloat16)
    logits = jnp.dot(normed, router, preferred_element_type=jnp.float32)
    choices_ids = expert_ids[:, 0].astype(jnp.int32)
    onehot_f32 = (choices_ids[:, None] == jnp.arange(EXPERTS, dtype=jnp.int32)[None, :]).astype(jnp.float32)
    gates = jax.nn.sigmoid(lax.optimization_barrier(jnp.sum(logits * onehot_f32, axis=1)))
    block_hot = (choices_ids[:, None] == jnp.arange(EXPERTS, dtype=jnp.int32)[None, :]).astype(jnp.int32)
    block_hot = block_hot.reshape(devices_all, TOK_DEV, EXPERTS)
    slot_rank = lax.optimization_barrier(jnp.sum(jnp.cumsum(block_hot, axis=1) * block_hot, axis=2)).reshape(total_rows) - 1
    owner_block = jnp.arange(total_rows, dtype=jnp.int32) // TOK_DEV
    slot_column = (owner_block * CAP + slot_rank).astype(jnp.int32)
    slot_table = jnp.full((EXPERTS, devices_all * CAP), total_rows, dtype=jnp.int32)
    slot_table = slot_table.at[choices_ids, slot_column].set(jnp.arange(total_rows, dtype=jnp.int32))
    cotan_f32 = cotangent.astype(jnp.float32)
    output_grad = (gates[:, None] * cotan_f32).astype(jnp.bfloat16)
    zero_row = jnp.zeros((1, model_width), jnp.bfloat16)
    normed_pad = jnp.concatenate([normed, zero_row], axis=0)
    output_pad = jnp.concatenate([output_grad, zero_row], axis=0)

    def one_expert(expert_index):
        row_index = slot_table[expert_index]
        slot_rows = normed_pad[row_index]
        slot_grad = output_pad[row_index]
        up_block = lax.dynamic_slice_in_dim(up_weights, expert_index * FF, FF, 1)
        down_block = lax.dynamic_slice_in_dim(down_weights, expert_index * FF, FF, 0)
        preact = jnp.dot(slot_rows, up_block, preferred_element_type=jnp.float32)
        activated = gelu_tanh(preact).astype(jnp.bfloat16)
        rows_count = activated.shape[0]
        expert_out = shard_sum(activated.reshape(rows_count, SHARDS, shard_width), down_block.reshape(SHARDS, shard_width, model_width))
        hidden_grad = jnp.dot(slot_grad, down_block.T, preferred_element_type=jnp.float32)
        preact_grad = (hidden_grad * gelu_slope(preact)).astype(jnp.bfloat16)
        input_out = shard_sum(preact_grad.reshape(rows_count, SHARDS, shard_width), up_block.T.reshape(SHARDS, shard_width, model_width))
        down_part = lax.dot_general(activated, slot_grad, (((0,), (0,)), ((), ())), preferred_element_type=jnp.float32)
        return (expert_out, input_out, down_part)
    expert_all, input_all, down_all = lax.map(one_expert, jnp.arange(EXPERTS, dtype=jnp.int32))
    expert_rows = expert_all[choices_ids, slot_column]
    input_rows = input_all[choices_ids, slot_column]
    gate_grad = lax.optimization_barrier(jnp.sum(cotan_f32 * expert_rows, axis=1))
    logit_grad = gate_grad * gates * (1.0 - gates)
    router_cols = router.astype(jnp.float32).T[choices_ids]
    normed_grad = input_rows + logit_grad[:, None] * router_cols
    tokens_grad = (cotan_f32 + norm_back(normed_grad)[0]).astype(jnp.bfloat16)
    router_grad = lax.dot_general(normed.astype(jnp.float32), onehot_f32 * logit_grad[:, None], (((0,), (0,)), ((), ())), precision=lax.Precision.HIGHEST, preferred_element_type=jnp.float32)
    down_grad = down_all.reshape(EXPERTS * FF, model_width)
    embed_f32 = embeds.astype(jnp.float32)
    member_index = (embed_f32 * lax.rsqrt(lax.optimization_barrier(jnp.sum(embed_f32 * embed_f32, axis=-1, keepdims=True)) + epsilon)).astype(jnp.bfloat16)
    softness_factor = jnp.exp(logit_scale_log)
    pair_scores = softness_factor * jnp.dot(member_index[0], member_index[1].T, preferred_element_type=jnp.float32) + pairwise_logit_bias
    pair_labels = jnp.where(jnp.eye(pair_scores.shape[0], dtype=jnp.bool_), 1.0, -1.0).astype(jnp.float32)
    panel_weights = (-pair_labels * jax.nn.sigmoid(-pair_labels * pair_scores) * softness_factor).astype(jnp.bfloat16)
    image_grad = jnp.dot(panel_weights, member_index[1], preferred_element_type=jnp.float32)
    text_grad = jnp.dot(panel_weights.T, member_index[0], preferred_element_type=jnp.float32)
    embed_grads = jnp.stack([image_grad, text_grad], axis=0)
    return (tokens_grad, router_grad, down_grad, embed_grads)
```

```python
import jax
import jax.numpy as jnp
from jax import lax
from jax.sharding import Mesh, PartitionSpec as P

epsilon = 1e-06
gelu_root = 0.7978845608028654
gelu_cubic = 0.044715

line = 4
columns = 4


def shifted(block, axis, step):
    count = lax.axis_size(axis)
    return lax.ppermute(block, axis, [(i, (i + step) % count) for i in range(count)])


def exchanged(block, axis, bit):
    count = lax.axis_size(axis)
    return lax.ppermute(block, axis, [(i, i ^ bit) for i in range(count)])


def product(left, right):
    return jnp.dot(left, right, preferred_element_type=jnp.float32)


def contract_rows(left, right):
    return lax.dot_general(
        left, right, (((0,), (0,)), ((), ())), preferred_element_type=jnp.float32
    )


def contracted_columns(left, right):
    return lax.dot_general(
        left, right, (((1,), (1,)), ((), ())), preferred_element_type=jnp.float32
    )


def gelu_pair(values):
    inner = gelu_root * (values + gelu_cubic * values * values * values)
    tangent = jnp.tanh(inner)
    slope = 0.5 * (1.0 + tangent) + 0.5 * values * (1.0 - tangent * tangent) * gelu_root * (
        1.0 + 3.0 * gelu_cubic * values * values
    )
    return 0.5 * values * (1.0 + tangent), slope


def pair_loss(embeds, logit_scale_log, pairwise_logit_bias, dp_index):
    own_rows = embeds[0].astype(jnp.float32)
    local_member = (
        own_rows * lax.rsqrt(jnp.sum(own_rows * own_rows, axis=-1, keepdims=True) + epsilon)
    ).astype(jnp.bfloat16)
    other_unit = exchanged(local_member, "tower", 1)
    softness_factor = jnp.exp(logit_scale_log)
    pair_rows = local_member.shape[0]
    row_global = dp_index * pair_rows + jnp.arange(pair_rows, dtype=jnp.int32)
    panel_rows = lax.all_gather(other_unit, ("z", "x", "y"), axis=0, tiled=True)
    pair_scores = (
        softness_factor * contracted_columns(local_member, panel_rows) + pairwise_logit_bias
    )
    col_global = jnp.arange(panel_rows.shape[0], dtype=jnp.int32)
    pair_labels = jnp.where(row_global[:, None] == col_global[None, :], 1.0, -1.0).astype(
        jnp.float32
    )
    panel_weights = (
        -pair_labels * jax.nn.sigmoid(-pair_labels * pair_scores) * softness_factor
    ).astype(jnp.bfloat16)
    return product(panel_weights, panel_rows)


def body(
    tokens,
    norm_gain,
    router,
    expert_ids,
    up_weights,
    down_weights,
    cotangent,
    embeds,
    logit_scale_log,
    pairwise_logit_bias,
):
    token_total, width = tokens.shape
    experts = router.shape[1]
    capacity = 3 * token_total // (2 * experts)
    half = width // 2
    slots = experts * capacity
    tower = lax.axis_index("tower")
    expert = lax.axis_index("z") * columns + lax.axis_index("x")
    dp_index = expert * line + lax.axis_index("y")
    bf16, f32 = jnp.bfloat16, jnp.float32

    def first_half(values, axis):
        return lax.dynamic_slice_in_dim(values, tower * half, half, axis)

    def second_half(values, axis):
        return lax.dynamic_slice_in_dim(values, (1 - tower) * half, half, axis)

    up_own = (first_half(up_weights, 0), second_half(up_weights, 0))
    down_own = (first_half(down_weights, 1), second_half(down_weights, 1))
    up_before = shifted(up_own[0], "y", 1)
    up_after = shifted(up_own[0], "y", -1)
    down_before = shifted(down_own[0], "y", 1)
    down_after = shifted(down_own[0], "y", -1)
    up_across = shifted(up_before, "y", 1)
    down_across = shifted(down_after, "y", -1)

    def both(piece):
        return piece, exchanged(piece, "tower", 1)

    choices = expert_ids[:, 0]
    onehot = choices[:, None] == jnp.arange(experts, dtype=jnp.int32)[None, :]
    row_ids = jnp.arange(token_total, dtype=jnp.int32)
    lower_tri = (row_ids[:, None] >= row_ids[None, :]).astype(bf16)
    running = product(lower_tri, onehot.astype(bf16))
    slot_rank = jnp.sum(running * onehot.astype(f32), axis=1).astype(jnp.int32) - 1
    low_row = choices * (2 * capacity) + slot_rank + capacity * tower
    high_row = choices * (2 * capacity) + slot_rank + capacity * (1 - tower)
    sent_ids = jnp.arange(2 * slots, dtype=jnp.int32)[None, :]
    low_place = (low_row[:, None] == sent_ids).astype(bf16)
    high_place = (high_row[:, None] == sent_ids).astype(bf16)

    slot_ids = jnp.arange(slots, dtype=jnp.int32)
    slot_first = slot_ids // capacity * (2 * capacity) + slot_ids % capacity
    take_first = (slot_first[:, None] == sent_ids).astype(bf16)
    take_second = (slot_first[:, None] + capacity == sent_ids).astype(bf16)

    def to_experts(values):
        rows = contract_rows(low_place, values[:, :half]) + contract_rows(
            high_place, values[:, half:]
        )
        received = lax.all_to_all(
            rows.astype(bf16).reshape(experts, 2 * capacity, half),
            ("z", "x"),
            split_axis=0,
            concat_axis=0,
            tiled=True,
        ).reshape(2 * slots, half)
        return product(take_first, received), product(take_second, received)

    token_first, token_second = to_experts(tokens)
    cotan_first, cotan_second = to_experts(cotangent)

    def features(values):
        values = values.astype(f32)[None, :]
        return first_half(values, 1), second_half(values, 1)

    gain_first, gain_second = features(norm_gain)
    column = lax.dynamic_slice_in_dim(router, expert, 1, 1)[:, 0]
    column_first, column_second = features(column)

    def feature_mean(first, second):
        total = jnp.sum(first, axis=1, keepdims=True) + jnp.sum(second, axis=1, keepdims=True)
        return total / width

    mean = feature_mean(token_first, token_second)
    center_first, center_second = token_first - mean, token_second - mean
    spread = feature_mean(center_first * center_first, center_second * center_second)
    root = lax.rsqrt(spread + epsilon)
    unit_first, unit_second = center_first * root, center_second * root
    normed_first = (unit_first * gain_first).astype(bf16)
    normed_second = (unit_second * gain_second).astype(bf16)
    logits = jnp.sum(normed_first.astype(f32) * column_first, axis=1, keepdims=True) + jnp.sum(
        normed_second.astype(f32) * column_second, axis=1, keepdims=True
    )
    gates = jax.nn.sigmoid(logits)
    output_first = (gates * cotan_first).astype(bf16)
    output_second = (gates * cotan_second).astype(bf16)

    def shard(up_pair, down_pair):
        preact = product(normed_first, up_pair[0]) + product(normed_second, up_pair[1])
        hidden_grad = contracted_columns(output_first, down_pair[0]) + contracted_columns(
            output_second, down_pair[1]
        )
        gelu, slope = gelu_pair(preact)
        activated = gelu.astype(bf16)
        preact_grad = (hidden_grad * slope).astype(bf16)
        gated = jnp.sum(activated.astype(f32) * hidden_grad, axis=1, keepdims=True)
        input_first = contracted_columns(preact_grad, up_pair[0])
        input_second = contracted_columns(preact_grad, up_pair[1])
        down_first = contract_rows(activated, output_first)
        down_second = contract_rows(activated, output_second).astype(bf16)
        down_sum = down_first + exchanged(down_second, "tower", 1).astype(f32)
        return gated, input_first, input_second, down_sum

    own = shard(up_own, down_own)
    before = shard(both(up_before), both(down_before))
    after = shard(both(up_after), both(down_after))
    across = shard(both(up_across), both(down_across))

    gated, input_first, input_second = (
        own[k] + before[k] + after[k] + across[k] for k in range(3)
    )
    logit_grad = gated * (1.0 - gates)
    grad_first = (input_first + logit_grad * column_first) * gain_first
    grad_second = (input_second + logit_grad * column_second) * gain_second
    grad_mean = feature_mean(grad_first, grad_second)
    grad_unit = feature_mean(grad_first * unit_first, grad_second * unit_second)
    back_first = cotan_first + root * (grad_first - grad_mean - unit_first * grad_unit)
    back_second = cotan_second + root * (grad_second - grad_mean - unit_second * grad_unit)
    back_rows = contract_rows(take_first, back_first.astype(bf16)) + contract_rows(
        take_second, back_second.astype(bf16)
    )
    returned = lax.all_to_all(
        back_rows.astype(bf16).reshape(experts, 2 * capacity, half),
        ("z", "x"),
        split_axis=0,
        concat_axis=0,
        tiled=True,
    ).reshape(2 * slots, half)
    tokens_grad = jnp.concatenate(
        [product(low_place, returned), product(high_place, returned)], axis=1
    ).astype(bf16)

    router_first = jnp.sum(normed_first.astype(f32) * logit_grad, axis=0)
    router_second = jnp.sum(normed_second.astype(f32) * logit_grad, axis=0)
    router_column = jnp.where(
        tower == 0,
        jnp.concatenate([router_first, router_second]),
        jnp.concatenate([router_second, router_first]),
    ).reshape(-1, 128)
    router_column = router_column + exchanged(router_column, "tower", 1)
    router_column = router_column + exchanged(router_column, "y", 1)
    router_column = router_column + exchanged(router_column, "y", 2)
    router_columns = lax.all_to_all(
        jnp.broadcast_to(router_column[None], (experts,) + router_column.shape),
        ("z", "x"),
        split_axis=0,
        concat_axis=0,
        tiled=True,
    )
    router_grad = router_columns.reshape(experts, width).T

    down_half = (
        own[3]
        + shifted(before[3].astype(bf16), "y", -1).astype(f32)
        + shifted(after[3].astype(bf16), "y", 1).astype(f32)
        + shifted(across[3].astype(bf16), "y", 2).astype(f32)
    )
    down_other = exchanged(down_half, "tower", 1)
    down_grad = jnp.where(
        tower == 0,
        jnp.concatenate([down_half, down_other], axis=1),
        jnp.concatenate([down_other, down_half], axis=1),
    )
    embed_grads = pair_loss(embeds, logit_scale_log, pairwise_logit_bias, dp_index)
    return (tokens_grad, router_grad, down_grad, embed_grads[None])


def solution(mesh):
    towers, chips = mesh.devices.shape
    grid = Mesh(
        mesh.devices.reshape(towers, chips // (columns * line), columns, line),
        ("tower", "z", "x", "y"),
    )
    dp = ("z", "x", "y")
    rows = P(("tower",) + dp, None)
    placed = (
        rows,
        P(),
        P(),
        rows,
        P(None, dp),
        P(dp, None),
        rows,
        P("tower", dp, None),
        P(),
        P(),
    )
    return jax.shard_map(
        body,
        mesh=grid,
        in_specs=placed,
        out_specs=(rows, P(), P(dp, None), P("tower", dp, None)),
        check_vma=False,
    )
```

```python
import functools

import jax
import jax.numpy as jnp
from jax import lax
from jax.experimental import pallas as pl
from jax.experimental.pallas import tpu as pltpu
from jax.sharding import Mesh, PartitionSpec as P

epsilon = 1e-06
gelu_root = 0.7978845608028654
gelu_cubic = 0.044715

line = 4
columns = 4


def shifted(block, axis, step):
    count = lax.axis_size(axis)
    return lax.ppermute(block, axis, [(i, (i + step) % count) for i in range(count)])


def exchanged(block, axis, bit):
    count = lax.axis_size(axis)
    return lax.ppermute(block, axis, [(i, i ^ bit) for i in range(count)])


def exchanged_pair(block, bit):
    count = lax.axis_size("y")
    return lax.ppermute(
        block, ("tower", "y"), [(i, i ^ (bit + count)) for i in range(2 * count)]
    )


def product(left, right):
    return jnp.dot(left, right, preferred_element_type=jnp.float32)


def contract_rows(left, right):
    return lax.dot_general(
        left, right, (((0,), (0,)), ((), ())), preferred_element_type=jnp.float32
    )


def contracted_columns(left, right):
    return lax.dot_general(
        left, right, (((1,), (1,)), ((), ())), preferred_element_type=jnp.float32
    )


def gelu_pair(values):
    inner = gelu_root * (values + gelu_cubic * values * values * values)
    tangent = jnp.tanh(inner)
    slope = 0.5 * (1.0 + tangent) + 0.5 * values * (1.0 - tangent * tangent) * gelu_root * (
        1.0 + 3.0 * gelu_cubic * values * values
    )
    return 0.5 * values * (1.0 + tangent), slope


def local_call(kernel, out_shape, operands, vmem, flops=1, **options):
    return pl.pallas_call(
        kernel,
        out_shape=out_shape,
        compiler_params=pltpu.CompilerParams(vmem_limit_bytes=vmem << 20),
        cost_estimate=pl.CostEstimate(flops=flops, bytes_accessed=1, transcendentals=0),
        **options,
    )(*operands)


def shape_of(shape, dtype):
    return jax.ShapeDtypeStruct(shape, dtype)


def slot_kernel(low_ref, high_ref, values_ref, rows_ref):
    count, half = rows_ref.shape
    ids = lax.broadcasted_iota(jnp.int32, (count, values_ref.shape[0]), 0)
    low_place = (ids == low_ref[...]).astype(jnp.bfloat16)
    high_place = (ids == high_ref[...]).astype(jnp.bfloat16)
    rows = product(low_place, values_ref[:, :half]) + product(high_place, values_ref[:, half:])
    rows_ref[...] = rows.astype(jnp.bfloat16)


def token_kernel(low_ref, high_ref, rows_ref, values_ref):
    count, half = rows_ref.shape
    ids = lax.broadcasted_iota(jnp.int32, (values_ref.shape[0], count), 1)
    rows = rows_ref[...]
    low_place = (ids == low_ref[...]).astype(jnp.bfloat16)
    high_place = (ids == high_ref[...]).astype(jnp.bfloat16)
    values_ref[:, :half] = product(low_place, rows).astype(jnp.bfloat16)
    values_ref[:, half:] = product(high_place, rows).astype(jnp.bfloat16)


def half_row(slot, capacity):
    return slot + capacity * (slot // capacity)


def taken(rows, row_of_slot, shift):
    slots, count = row_of_slot.shape[0], rows.shape[0]
    ids = lax.broadcasted_iota(jnp.int32, (slots, count), 1)
    return product((ids == row_of_slot + shift).astype(jnp.bfloat16), rows)


def feature_mean(first, second, width):
    total = jnp.sum(first, axis=1, keepdims=True) + jnp.sum(second, axis=1, keepdims=True)
    return total / width


def norm_kernel(
    capacity, rows_ref, slot_ref, gain_ref, column_ref, normed_ref, unit_ref, root_ref, gate_ref
):
    half = rows_ref.shape[1]
    width = 2 * half
    rows, row_of_slot = rows_ref[...], slot_ref[...]
    first, second = taken(rows, row_of_slot, 0), taken(rows, row_of_slot, capacity)
    mean = feature_mean(first, second, width)
    first, second = first - mean, second - mean
    root = lax.rsqrt(feature_mean(first * first, second * second, width) + epsilon)
    first, second = first * root, second * root
    unit_ref[:, :half] = first
    unit_ref[:, half:] = second
    root_ref[...] = root
    first = (first * gain_ref[0:1]).astype(jnp.bfloat16)
    second = (second * gain_ref[1:2]).astype(jnp.bfloat16)
    normed_ref[:, :half] = first
    normed_ref[:, half:] = second
    logits = jnp.sum(first.astype(jnp.float32) * column_ref[0:1], axis=1, keepdims=True) + jnp.sum(
        second.astype(jnp.float32) * column_ref[1:2], axis=1, keepdims=True
    )
    gate_ref[...] = jax.nn.sigmoid(logits)


def preact_kernel(normed_ref, first_ref, second_ref, preact_ref, turned_ref):
    half = first_ref.shape[0]
    preact = product(normed_ref[:, :half], first_ref[...]) + product(
        normed_ref[:, half:], second_ref[...]
    )
    preact_ref[...] = preact
    gelu, _ = gelu_pair(preact)
    turned_ref[...] = gelu.T.astype(jnp.bfloat16)


def gate_kernel(capacity, rows_ref, slot_ref, gate_ref, cotan_ref, output_ref):
    half = rows_ref.shape[1]
    rows, row_of_slot, gates = rows_ref[...], slot_ref[...], gate_ref[...]
    for part in range(2):
        values = taken(rows, row_of_slot, part * capacity)
        cotan_ref[:, part * half : (part + 1) * half] = values.astype(jnp.bfloat16)
        output_ref[:, part * half : (part + 1) * half] = (gates * values).astype(jnp.bfloat16)


def down_kernel(turned_ref, output_ref, first_ref, second_ref):
    half = first_ref.shape[1]
    turned = turned_ref[...]
    first_ref[...] = product(turned, output_ref[:, :half])
    second_ref[...] = product(turned, output_ref[:, half:]).astype(jnp.bfloat16)


def hidden_kernel(
    shards, output_ref, normed_ref, gate_ref, *refs
):
    pieces, refs = refs[: 3 * shards], refs[3 * shards :]
    grad_ref, logit_ref, router_ref, weights, preacts, sems = refs
    half = weights.shape[3]
    copies = []
    for shard in range(shards):
        own = pieces[3 * shard : 3 * shard + 3]
        into = [preacts.at[shard]] + [weights.at[shard, k] for k in range(2)]
        copies.append(
            [pltpu.make_async_copy(own[k], into[k], sems.at[shard, k]) for k in range(3)]
        )
    for group in copies:
        for copy in group:
            copy.start()
    gated = None
    for shard in range(shards):
        for copy in copies[shard]:
            copy.wait()
        hidden_grad = contracted_columns(
            output_ref[:, :half], weights[shard, 0]
        ) + contracted_columns(output_ref[:, half:], weights[shard, 1])
        gelu, slope = gelu_pair(preacts[shard])
        term = jnp.sum(
            gelu.astype(jnp.bfloat16).astype(jnp.float32) * hidden_grad, axis=1, keepdims=True
        )
        gated = term if gated is None else gated + term
        grad_ref[shard] = (hidden_grad * slope).astype(jnp.bfloat16)
    logit_grad = gated * (1.0 - gate_ref[...])
    logit_ref[...] = logit_grad
    router_ref[0:1, :] = jnp.sum(
        normed_ref[:, :half].astype(jnp.float32) * logit_grad, axis=0, keepdims=True
    )
    router_ref[1:2, :] = jnp.sum(
        normed_ref[:, half:].astype(jnp.float32) * logit_grad, axis=0, keepdims=True
    )


def back_kernel(
    capacity,
    shards,
    grad_ref,
    logit_ref,
    cotan_ref,
    unit_ref,
    root_ref,
    slot_ref,
    gain_ref,
    column_ref,
    *refs,
):
    pieces, refs = refs[: 2 * shards], refs[2 * shards :]
    rows_ref, weights, first_sum, second_sum, sems = refs
    count, half = rows_ref.shape
    width = 2 * half
    copies = [
        [
            pltpu.make_async_copy(pieces[2 * shard + k], weights.at[shard, k], sems.at[shard, k])
            for k in range(2)
        ]
        for shard in range(shards)
    ]
    for group in copies:
        for copy in group:
            copy.start()
    for shard in range(shards):
        for copy in copies[shard]:
            copy.wait()
        first = contracted_columns(grad_ref[shard], weights[shard, 0])
        second = contracted_columns(grad_ref[shard], weights[shard, 1])
        if shard == 0:
            first_sum[...], second_sum[...] = first, second
        else:
            first_sum[...] += first
            second_sum[...] += second
    logit_grad = logit_ref[...]
    gain_first, gain_second = gain_ref[0:1], gain_ref[1:2]
    first = (first_sum[...] + logit_grad * column_ref[0:1]) * gain_first
    second = (second_sum[...] + logit_grad * column_ref[1:2]) * gain_second
    unit_first, unit_second = unit_ref[:, :half], unit_ref[:, half:]
    grad_mean = feature_mean(first, second, width)
    grad_unit = feature_mean(first * unit_first, second * unit_second, width)
    root = root_ref[...]
    first = cotan_ref[:, :half].astype(jnp.float32) + root * (
        first - grad_mean - unit_first * grad_unit
    )
    second = cotan_ref[:, half:].astype(jnp.float32) + root * (
        second - grad_mean - unit_second * grad_unit
    )
    ids = lax.broadcasted_iota(jnp.int32, (count, slot_ref.shape[1]), 0)
    rows = product(
        (ids == slot_ref[...]).astype(jnp.bfloat16), first.astype(jnp.bfloat16)
    ) + product(
        (ids == slot_ref[...] + capacity).astype(jnp.bfloat16), second.astype(jnp.bfloat16)
    )
    rows_ref[...] = rows.astype(jnp.bfloat16)


pair_y_bits, pair_x_bits, pair_z_bits = (2, 1), (2, 1), (4, 2, 1)


def pair_rows(embeds):
    own_rows = embeds[0].astype(jnp.float32)
    member = (
        own_rows * lax.rsqrt(jnp.sum(own_rows * own_rows, axis=-1, keepdims=True) + epsilon)
    ).astype(jnp.bfloat16)

    def collected(block, axis, bits):
        for bit in bits:
            block = jnp.concatenate([block, exchanged(block, axis, bit)], axis=0)
        return block

    line_rows = collected(exchanged(member, "tower", 1), "z", pair_z_bits)
    plane_rows = collected(collected(member, "y", pair_y_bits), "x", pair_x_bits)
    return plane_rows, line_rows


def pair_grads(plane_rows, line_rows, row_count, logit_scale_log, pairwise_logit_bias, dp_index):
    def row_ids(bits):
        blocks = dp_index[None]
        for bit in bits:
            blocks = jnp.concatenate([blocks, blocks ^ bit])
        return (blocks[:, None] * row_count + jnp.arange(row_count, dtype=jnp.int32)).reshape(-1)

    line_ids = row_ids([bit * line * columns for bit in pair_z_bits])
    plane_ids = row_ids(list(pair_y_bits) + [bit * line for bit in pair_x_bits])
    softness_factor = jnp.exp(logit_scale_log)
    pair_scores = (
        softness_factor * contracted_columns(plane_rows, line_rows) + pairwise_logit_bias
    )
    pair_labels = jnp.where(plane_ids[:, None] == line_ids[None, :], 1.0, -1.0).astype(
        jnp.float32
    )
    panel_weights = (
        -pair_labels * jax.nn.sigmoid(-pair_labels * pair_scores) * softness_factor
    ).astype(jnp.bfloat16)
    grads = product(panel_weights, line_rows)
    for axis, bits in (("x", pair_x_bits), ("y", pair_y_bits)):
        for bit in reversed(bits):
            kept = grads.shape[0] // 2
            grads = grads[:kept] + exchanged(grads[kept:], axis, bit)
    return grads


def body(
    tokens,
    norm_gain,
    router,
    expert_ids,
    up_weights,
    down_weights,
    cotangent,
    embeds,
    logit_scale_log,
    pairwise_logit_bias,
):
    token_total, width = tokens.shape
    hidden = up_weights.shape[1]
    experts = router.shape[1]
    capacity = 3 * token_total // (2 * experts)
    half = width // 2
    slots = experts * capacity
    tower = lax.axis_index("tower")
    expert = lax.axis_index("z") * columns + lax.axis_index("x")
    dp_index = expert * line + lax.axis_index("y")
    bf16, f32 = jnp.bfloat16, jnp.float32

    def halves(values, axis):
        return (
            lax.dynamic_slice_in_dim(values, tower * half, half, axis),
            lax.dynamic_slice_in_dim(values, (1 - tower) * half, half, axis),
        )

    up_own, down_own = halves(up_weights, 0), halves(down_weights, 1)
    up_before = shifted(up_own[0], "y", 1)
    up_after = shifted(up_own[0], "y", -1)
    down_before = shifted(down_own[0], "y", 1)
    down_after = shifted(down_own[0], "y", -1)
    up_across = shifted(up_before, "y", 1)
    down_across = shifted(down_after, "y", -1)

    choices = expert_ids[:, 0]
    onehot = choices[:, None] == jnp.arange(experts, dtype=jnp.int32)[None, :]
    row_ids = jnp.arange(token_total, dtype=jnp.int32)
    lower_tri = (row_ids[:, None] >= row_ids[None, :]).astype(bf16)
    running = product(lower_tri, onehot.astype(bf16))
    slot_rank = jnp.sum(running * onehot.astype(f32), axis=1).astype(jnp.int32) - 1
    low_row = choices * (2 * capacity) + slot_rank + capacity * tower
    high_row = choices * (2 * capacity) + slot_rank + capacity * (1 - tower)
    row_of_slot = half_row(jnp.arange(slots, dtype=jnp.int32), capacity)

    def slot_rows(values):
        return local_call(
            slot_kernel,
            [shape_of((2 * slots, half), bf16)],
            (low_row[None, :], high_row[None, :], values),
            24,
        )[0]

    def spread(rows):
        return lax.all_to_all(
            rows.reshape(experts, 2 * capacity, half),
            ("z", "x"),
            split_axis=0,
            concat_axis=0,
            tiled=True,
        ).reshape(2 * slots, half)

    def both(piece):
        return piece, exchanged(piece, "tower", 1)

    token_rows = spread(slot_rows(tokens))
    cotan_rows, token_rows = lax.optimization_barrier((slot_rows(cotangent), token_rows))
    cotan_rows = spread(cotan_rows)
    ups = [up_own] + [both(piece) for piece in (up_before, up_after, up_across)]
    downs = [down_own] + [both(piece) for piece in (down_before, down_after, down_across)]

    def features(values):
        return jnp.concatenate(halves(values.astype(f32)[None, :], 1), axis=0)

    gain = features(norm_gain)
    column = features(lax.dynamic_slice_in_dim(router, expert, 1, 1)[:, 0])
    normed, unit, root, gates = local_call(
        functools.partial(norm_kernel, capacity),
        [
            shape_of((slots, width), bf16),
            shape_of((slots, width), f32),
            shape_of((slots, 1), f32),
            shape_of((slots, 1), f32),
        ],
        (token_rows, row_of_slot[:, None], gain, column),
        24,
    )
    fronts = [
        local_call(
            preact_kernel,
            [shape_of((slots, hidden), f32), shape_of((hidden, slots), bf16)],
            (normed,) + up_pair,
            24,
        )
        for up_pair in ups
    ]
    pair_blocks = pair_rows(embeds)
    cotan_rows, downs, fronts, pair_blocks = lax.optimization_barrier(
        (cotan_rows, downs, fronts, pair_blocks)
    )
    cotan, output = local_call(
        functools.partial(gate_kernel, capacity),
        [shape_of((slots, width), bf16)] * 2,
        (cotan_rows, row_of_slot[:, None], gates),
        24,
    )

    def down_terms(front):
        first, second = local_call(
            down_kernel,
            [shape_of((hidden, half), f32), shape_of((hidden, half), bf16)],
            (front[1], output),
            24,
        )
        return first + exchanged(second, "tower", 1).astype(f32)

    down_before, down_after, down_across = (
        down_terms(front).astype(bf16) for front in fronts[1:]
    )
    output, down_before, down_after, down_across = lax.optimization_barrier(
        (output, down_before, down_after, down_across)
    )
    whole, apart = pl.BlockSpec(memory_space=pltpu.VMEM), pl.BlockSpec(memory_space=pl.ANY)
    shards = len(fronts)
    hidden_pieces, back_pieces = [], []
    for front, up_pair, down_pair in zip(fronts, ups, downs):
        hidden_pieces += [front[0], *down_pair]
        back_pieces += [*up_pair]
    preact_grad, logit_grad, router_halves = local_call(
        functools.partial(hidden_kernel, shards),
        [
            shape_of((shards, slots, hidden), bf16),
            shape_of((slots, 1), f32),
            shape_of((2, half), f32),
        ],
        (output, normed, gates, *hidden_pieces),
        40,
        in_specs=[whole] * 3 + [apart] * len(hidden_pieces),
        scratch_shapes=[
            pltpu.VMEM((shards, 2, hidden, half), bf16),
            pltpu.VMEM((shards, slots, hidden), f32),
            pltpu.SemaphoreType.DMA((shards, 3)),
        ],
    )
    back_rows = local_call(
        functools.partial(back_kernel, capacity, shards),
        [shape_of((2 * slots, half), bf16)],
        (
            preact_grad,
            logit_grad,
            cotan,
            unit,
            root,
            row_of_slot[None, :],
            gain,
            column,
            *back_pieces,
        ),
        40,
        2 * shards * slots * width * hidden,
        in_specs=[whole] * 8 + [apart] * len(back_pieces),
        scratch_shapes=[
            pltpu.VMEM((shards, 2, half, hidden), bf16),
            pltpu.VMEM((slots, half), f32),
            pltpu.VMEM((slots, half), f32),
            pltpu.SemaphoreType.DMA((shards, 2)),
        ],
    )[0]
    returned = spread(back_rows)
    tokens_grad = local_call(
        token_kernel,
        [shape_of((token_total, width), bf16)],
        (low_row[:, None], high_row[:, None], returned),
        24,
    )[0]

    router_column = jnp.where(
        tower == 0, router_halves, jnp.concatenate([router_halves[1:], router_halves[:1]])
    ).reshape(-1, 128)
    pairs = [
        (other_tower + own)
        for own, other_tower in (
            (router_column if bit == 0 else exchanged(router_column, "y", bit),
             exchanged_pair(router_column, bit))
            for bit in range(line)
        )
    ]
    router_column = ((pairs[0] + pairs[1]) + (pairs[2] + pairs[3]))[None]
    over_x = jnp.concatenate(
        [router_column] + [exchanged(router_column, "x", bit) for bit in range(1, columns)]
    )
    planes = experts // columns
    over_zx = jnp.concatenate(
        [over_x] + [exchanged(over_x, "z", bit) for bit in range(1, planes)]
    ).reshape(experts, width)
    expert_ids_here = jnp.arange(experts, dtype=jnp.int32)
    order = (expert_ids_here ^ expert)[:, None] == expert_ids_here[None, :]
    router_grad = lax.dot_general(
        over_zx,
        order.astype(f32),
        (((0,), (0,)), ((), ())),
        precision=lax.Precision.HIGHEST,
        preferred_element_type=f32,
    )

    down_half = (
        down_terms(fronts[0])
        + shifted(down_before, "y", -1).astype(f32)
        + shifted(down_after, "y", 1).astype(f32)
        + shifted(down_across, "y", 2).astype(f32)
    )
    down_other = exchanged(down_half, "tower", 1)
    down_grad = jnp.where(
        tower == 0,
        jnp.concatenate([down_half, down_other], axis=1),
        jnp.concatenate([down_other, down_half], axis=1),
    )
    embed_grads = pair_grads(
        *pair_blocks, embeds.shape[1], logit_scale_log, pairwise_logit_bias, dp_index
    )
    return (tokens_grad, router_grad, down_grad, embed_grads[None])


def solution(mesh):
    towers, chips = mesh.devices.shape
    grid = Mesh(
        mesh.devices.reshape(towers, chips // (columns * line), columns, line),
        ("tower", "z", "x", "y"),
    )
    dp = ("z", "x", "y")
    rows = P(("tower",) + dp, None)
    placed = (
        rows,
        P(),
        P(),
        rows,
        P(None, dp),
        P(dp, None),
        rows,
        P("tower", dp, None),
        P(),
        P(),
    )
    return jax.shard_map(
        body,
        mesh=grid,
        in_specs=placed,
        out_specs=(rows, P(), P(dp, None), P("tower", dp, None)),
        check_vma=False,
    )
```

```python
import functools

import jax
import jax.numpy as jnp
from jax import lax
from jax.experimental import pallas as pl
from jax.experimental.pallas import tpu as pltpu
from jax.sharding import Mesh, PartitionSpec as P

epsilon = 1e-06
gelu_root = 0.7978845608028654
gelu_cubic = 0.044715

line = 4
columns = 4


def shifted(block, axis, step):
    count = lax.axis_size(axis)
    return lax.ppermute(block, axis, [(i, (i + step) % count) for i in range(count)])


def exchanged(block, axis, bit):
    count = lax.axis_size(axis)
    return lax.ppermute(block, axis, [(i, i ^ bit) for i in range(count)])


def product(left, right):
    return jnp.dot(left, right, preferred_element_type=jnp.float32)


def contract_rows(left, right):
    return lax.dot_general(
        left, right, (((0,), (0,)), ((), ())), preferred_element_type=jnp.float32
    )


def contracted_columns(left, right):
    return lax.dot_general(
        left, right, (((1,), (1,)), ((), ())), preferred_element_type=jnp.float32
    )


def gelu_pair(values):
    inner = gelu_root * (values + gelu_cubic * values * values * values)
    tangent = jnp.tanh(inner)
    slope = 0.5 * (1.0 + tangent) + 0.5 * values * (1.0 - tangent * tangent) * gelu_root * (
        1.0 + 3.0 * gelu_cubic * values * values
    )
    return 0.5 * values * (1.0 + tangent), slope


def local_call(kernel, out_shape, operands, vmem, flops=1, **options):
    return pl.pallas_call(
        kernel,
        out_shape=out_shape,
        compiler_params=pltpu.CompilerParams(vmem_limit_bytes=vmem << 20),
        cost_estimate=pl.CostEstimate(flops=flops, bytes_accessed=1, transcendentals=0),
        **options,
    )(*operands)


def shape_of(shape, dtype):
    return jax.ShapeDtypeStruct(shape, dtype)


def slot_kernel(low_ref, high_ref, values_ref, rows_ref):
    count, half = rows_ref.shape
    ids = lax.broadcasted_iota(jnp.int32, (count, values_ref.shape[0]), 0)
    low_place = (ids == low_ref[...]).astype(jnp.bfloat16)
    high_place = (ids == high_ref[...]).astype(jnp.bfloat16)
    rows = product(low_place, values_ref[:, :half]) + product(high_place, values_ref[:, half:])
    rows_ref[...] = rows.astype(jnp.bfloat16)


def token_kernel(low_ref, high_ref, rows_ref, values_ref):
    count, half = rows_ref.shape
    ids = lax.broadcasted_iota(jnp.int32, (values_ref.shape[0], count), 1)
    rows = rows_ref[...]
    low_place = (ids == low_ref[...]).astype(jnp.bfloat16)
    high_place = (ids == high_ref[...]).astype(jnp.bfloat16)
    values_ref[:, :half] = product(low_place, rows).astype(jnp.bfloat16)
    values_ref[:, half:] = product(high_place, rows).astype(jnp.bfloat16)


def half_row(slot, capacity):
    return slot + capacity * (slot // capacity)


def taken(rows, row_of_slot, shift):
    slots, count = row_of_slot.shape[0], rows.shape[0]
    ids = lax.broadcasted_iota(jnp.int32, (slots, count), 1)
    return product((ids == row_of_slot + shift).astype(jnp.bfloat16), rows)


def feature_mean(first, second, width):
    total = jnp.sum(first, axis=1, keepdims=True) + jnp.sum(second, axis=1, keepdims=True)
    return total / width


def norm_kernel(
    capacity, rows_ref, slot_ref, gain_ref, column_ref, normed_ref, unit_ref, root_ref, gate_ref
):
    half = rows_ref.shape[1]
    width = 2 * half
    rows, row_of_slot = rows_ref[...], slot_ref[...]
    first, second = taken(rows, row_of_slot, 0), taken(rows, row_of_slot, capacity)
    mean = feature_mean(first, second, width)
    first, second = first - mean, second - mean
    root = lax.rsqrt(feature_mean(first * first, second * second, width) + epsilon)
    first, second = first * root, second * root
    unit_ref[:, :half] = first
    unit_ref[:, half:] = second
    root_ref[...] = root
    first = (first * gain_ref[0:1]).astype(jnp.bfloat16)
    second = (second * gain_ref[1:2]).astype(jnp.bfloat16)
    normed_ref[:, :half] = first
    normed_ref[:, half:] = second
    logits = jnp.sum(first.astype(jnp.float32) * column_ref[0:1], axis=1, keepdims=True) + jnp.sum(
        second.astype(jnp.float32) * column_ref[1:2], axis=1, keepdims=True
    )
    gate_ref[...] = jax.nn.sigmoid(logits)


def preact_kernel(normed_ref, first_ref, second_ref, preact_ref, turned_ref):
    half = first_ref.shape[0]
    preact = product(normed_ref[:, :half], first_ref[...]) + product(
        normed_ref[:, half:], second_ref[...]
    )
    preact_ref[...] = preact
    gelu, _ = gelu_pair(preact)
    turned_ref[...] = gelu.T.astype(jnp.bfloat16)


def gate_kernel(capacity, rows_ref, slot_ref, gate_ref, cotan_ref, output_ref):
    half = rows_ref.shape[1]
    rows, row_of_slot, gates = rows_ref[...], slot_ref[...], gate_ref[...]
    for part in range(2):
        values = taken(rows, row_of_slot, part * capacity)
        cotan_ref[:, part * half : (part + 1) * half] = values.astype(jnp.bfloat16)
        output_ref[:, part * half : (part + 1) * half] = (gates * values).astype(jnp.bfloat16)


def down_kernel(turned_ref, output_ref, first_ref, second_ref):
    half = first_ref.shape[1]
    turned = turned_ref[...]
    first_ref[...] = product(turned, output_ref[:, :half])
    second_ref[...] = product(turned, output_ref[:, half:]).astype(jnp.bfloat16)


def hidden_kernel(
    shards, output_ref, normed_ref, gate_ref, *refs
):
    preacts, pieces, refs = refs[:shards], refs[shards : 3 * shards], refs[3 * shards :]
    grad_ref, logit_ref, router_ref, weights, sems = refs
    half = weights.shape[3]
    copies = [
        [
            pltpu.make_async_copy(pieces[2 * shard + k], weights.at[shard, k], sems.at[shard, k])
            for k in range(2)
        ]
        for shard in range(shards)
    ]
    for group in copies:
        for copy in group:
            copy.start()
    gated = None
    for shard in range(shards):
        for copy in copies[shard]:
            copy.wait()
        hidden_grad = contracted_columns(
            output_ref[:, :half], weights[shard, 0]
        ) + contracted_columns(output_ref[:, half:], weights[shard, 1])
        gelu, slope = gelu_pair(preacts[shard][...])
        term = jnp.sum(
            gelu.astype(jnp.bfloat16).astype(jnp.float32) * hidden_grad, axis=1, keepdims=True
        )
        gated = term if gated is None else gated + term
        grad_ref[shard] = (hidden_grad * slope).astype(jnp.bfloat16)
    logit_grad = gated * (1.0 - gate_ref[...])
    logit_ref[...] = logit_grad
    router_ref[0:1, :] = jnp.sum(
        normed_ref[:, :half].astype(jnp.float32) * logit_grad, axis=0, keepdims=True
    )
    router_ref[1:2, :] = jnp.sum(
        normed_ref[:, half:].astype(jnp.float32) * logit_grad, axis=0, keepdims=True
    )


def back_kernel(
    capacity,
    shards,
    grad_ref,
    logit_ref,
    cotan_ref,
    unit_ref,
    root_ref,
    slot_ref,
    gain_ref,
    column_ref,
    *refs,
):
    pieces, refs = refs[: 2 * shards], refs[2 * shards :]
    rows_ref, weights, first_sum, second_sum, sems = refs
    count, half = rows_ref.shape
    width = 2 * half
    copies = [
        [
            pltpu.make_async_copy(pieces[2 * shard + k], weights.at[shard, k], sems.at[shard, k])
            for k in range(2)
        ]
        for shard in range(shards)
    ]
    for group in copies:
        for copy in group:
            copy.start()
    for shard in range(shards):
        for copy in copies[shard]:
            copy.wait()
        first = contracted_columns(grad_ref[shard], weights[shard, 0])
        second = contracted_columns(grad_ref[shard], weights[shard, 1])
        if shard == 0:
            first_sum[...], second_sum[...] = first, second
        else:
            first_sum[...] += first
            second_sum[...] += second
    logit_grad = logit_ref[...]
    gain_first, gain_second = gain_ref[0:1], gain_ref[1:2]
    first = (first_sum[...] + logit_grad * column_ref[0:1]) * gain_first
    second = (second_sum[...] + logit_grad * column_ref[1:2]) * gain_second
    unit_first, unit_second = unit_ref[:, :half], unit_ref[:, half:]
    grad_mean = feature_mean(first, second, width)
    grad_unit = feature_mean(first * unit_first, second * unit_second, width)
    root = root_ref[...]
    first = cotan_ref[:, :half].astype(jnp.float32) + root * (
        first - grad_mean - unit_first * grad_unit
    )
    second = cotan_ref[:, half:].astype(jnp.float32) + root * (
        second - grad_mean - unit_second * grad_unit
    )
    ids = lax.broadcasted_iota(jnp.int32, (count, slot_ref.shape[1]), 0)
    rows = product(
        (ids == slot_ref[...]).astype(jnp.bfloat16), first.astype(jnp.bfloat16)
    ) + product(
        (ids == slot_ref[...] + capacity).astype(jnp.bfloat16), second.astype(jnp.bfloat16)
    )
    rows_ref[...] = rows.astype(jnp.bfloat16)


def pair_loss(embeds, logit_scale_log, pairwise_logit_bias, dp_index):
    own_rows = embeds[0].astype(jnp.float32)
    local_member = (
        own_rows * lax.rsqrt(jnp.sum(own_rows * own_rows, axis=-1, keepdims=True) + epsilon)
    ).astype(jnp.bfloat16)
    other_unit = exchanged(local_member, "tower", 1)
    softness_factor = jnp.exp(logit_scale_log)
    pair_rows = local_member.shape[0]
    row_global = dp_index * pair_rows + jnp.arange(pair_rows, dtype=jnp.int32)
    panel_rows = lax.all_gather(other_unit, ("z", "x", "y"), axis=0, tiled=True)
    pair_scores = (
        softness_factor * contracted_columns(local_member, panel_rows) + pairwise_logit_bias
    )
    col_global = jnp.arange(panel_rows.shape[0], dtype=jnp.int32)
    pair_labels = jnp.where(row_global[:, None] == col_global[None, :], 1.0, -1.0).astype(
        jnp.float32
    )
    panel_weights = (
        -pair_labels * jax.nn.sigmoid(-pair_labels * pair_scores) * softness_factor
    ).astype(jnp.bfloat16)
    return product(panel_weights, panel_rows)


def body(
    tokens,
    norm_gain,
    router,
    expert_ids,
    up_weights,
    down_weights,
    cotangent,
    embeds,
    logit_scale_log,
    pairwise_logit_bias,
):
    token_total, width = tokens.shape
    hidden = up_weights.shape[1]
    experts = router.shape[1]
    capacity = 3 * token_total // (2 * experts)
    half = width // 2
    slots = experts * capacity
    tower = lax.axis_index("tower")
    expert = lax.axis_index("z") * columns + lax.axis_index("x")
    dp_index = expert * line + lax.axis_index("y")
    bf16, f32 = jnp.bfloat16, jnp.float32

    def halves(values, axis):
        return (
            lax.dynamic_slice_in_dim(values, tower * half, half, axis),
            lax.dynamic_slice_in_dim(values, (1 - tower) * half, half, axis),
        )

    up_own, down_own = halves(up_weights, 0), halves(down_weights, 1)
    up_before = shifted(up_own[0], "y", 1)
    up_after = shifted(up_own[0], "y", -1)
    down_part, up_before, up_after = lax.optimization_barrier((down_own[0], up_before, up_after))
    down_before = shifted(down_part, "y", 1)
    down_after = shifted(down_part, "y", -1)
    up_before, down_before, down_after = lax.optimization_barrier(
        (up_before, down_before, down_after)
    )
    up_across = shifted(up_before, "y", 1)
    down_across = shifted(down_after, "y", -1)

    choices = expert_ids[:, 0]
    onehot = choices[:, None] == jnp.arange(experts, dtype=jnp.int32)[None, :]
    row_ids = jnp.arange(token_total, dtype=jnp.int32)
    lower_tri = (row_ids[:, None] >= row_ids[None, :]).astype(bf16)
    running = product(lower_tri, onehot.astype(bf16))
    slot_rank = jnp.sum(running * onehot.astype(f32), axis=1).astype(jnp.int32) - 1
    low_row = choices * (2 * capacity) + slot_rank + capacity * tower
    high_row = choices * (2 * capacity) + slot_rank + capacity * (1 - tower)
    row_of_slot = half_row(jnp.arange(slots, dtype=jnp.int32), capacity)

    def slot_rows(values):
        return local_call(
            slot_kernel,
            [shape_of((2 * slots, half), bf16)],
            (low_row[None, :], high_row[None, :], values),
            16,
        )[0]

    def spread(rows):
        return lax.all_to_all(
            rows.reshape(experts, 2 * capacity, half),
            ("z", "x"),
            split_axis=0,
            concat_axis=0,
            tiled=True,
        ).reshape(2 * slots, half)

    def both(piece):
        return piece, exchanged(piece, "tower", 1)

    token_rows = spread(slot_rows(tokens))
    cotan_rows, token_rows = lax.optimization_barrier((slot_rows(cotangent), token_rows))
    cotan_rows = spread(cotan_rows)
    ups = [up_own] + [both(piece) for piece in (up_before, up_after, up_across)]
    downs = [down_own] + [both(piece) for piece in (down_before, down_after, down_across)]

    def features(values):
        return jnp.concatenate(halves(values.astype(f32)[None, :], 1), axis=0)

    gain = features(norm_gain)
    column = features(lax.dynamic_slice_in_dim(router, expert, 1, 1)[:, 0])
    normed, unit, root, gates = local_call(
        functools.partial(norm_kernel, capacity),
        [
            shape_of((slots, width), bf16),
            shape_of((slots, width), f32),
            shape_of((slots, 1), f32),
            shape_of((slots, 1), f32),
        ],
        (token_rows, row_of_slot[:, None], gain, column),
        24,
    )
    fronts = [
        local_call(
            preact_kernel,
            [shape_of((slots, hidden), f32), shape_of((hidden, slots), bf16)],
            (normed,) + up_pair,
            24,
        )
        for up_pair in ups
    ]
    cotan_rows, fronts = lax.optimization_barrier((cotan_rows, fronts))
    cotan, output = local_call(
        functools.partial(gate_kernel, capacity),
        [shape_of((slots, width), bf16)] * 2,
        (cotan_rows, row_of_slot[:, None], gates),
        24,
    )

    whole, apart = pl.BlockSpec(memory_space=pltpu.VMEM), pl.BlockSpec(memory_space=pltpu.HBM)
    shards = len(fronts)
    preact_grad, logit_grad, router_halves = local_call(
        functools.partial(hidden_kernel, shards),
        [
            shape_of((shards, slots, hidden), bf16),
            shape_of((slots, 1), f32),
            shape_of((2, half), f32),
        ],
        (
            output,
            normed,
            gates,
            *(front[0] for front in fronts),
            *(piece for pair in downs for piece in pair),
        ),
        24,
        in_specs=[whole] * (3 + shards) + [apart] * (2 * shards),
        scratch_shapes=[
            pltpu.VMEM((shards, 2, hidden, half), bf16),
            pltpu.SemaphoreType.DMA((shards, 2)),
        ],
    )

    def down_terms(front):
        first, second = local_call(
            down_kernel,
            [shape_of((hidden, half), f32), shape_of((hidden, half), bf16)],
            (front[1], output),
            12,
        )
        return first + exchanged(second, "tower", 1).astype(f32)

    down_before, down_after, down_across = (
        down_terms(front).astype(bf16) for front in fronts[1:]
    )
    preact_grad, down_before, down_after, down_across = lax.optimization_barrier(
        (preact_grad, down_before, down_after, down_across)
    )
    back_rows = local_call(
        functools.partial(back_kernel, capacity, shards),
        [shape_of((2 * slots, half), bf16)],
        (
            preact_grad,
            logit_grad,
            cotan,
            unit,
            root,
            row_of_slot[None, :],
            gain,
            column,
            *(piece for pair in ups for piece in pair),
        ),
        28,
        2 * shards * slots * width * hidden,
        in_specs=[whole] * 8 + [apart] * (2 * shards),
        scratch_shapes=[
            pltpu.VMEM((shards, 2, half, hidden), bf16),
            pltpu.VMEM((slots, half), f32),
            pltpu.VMEM((slots, half), f32),
            pltpu.SemaphoreType.DMA((shards, 2)),
        ],
    )[0]
    returned = spread(back_rows)
    tokens_grad = local_call(
        token_kernel,
        [shape_of((token_total, width), bf16)],
        (low_row[:, None], high_row[:, None], returned),
        16,
    )[0]

    router_column = jnp.where(
        tower == 0, router_halves, jnp.concatenate([router_halves[1:], router_halves[:1]])
    ).reshape(-1, 128)
    router_column = router_column + exchanged(router_column, "tower", 1)
    near, far, farther = (exchanged(router_column, "y", bit) for bit in (1, 2, 3))
    router_column = ((router_column + near) + (far + farther))[None]

    def collected(block, axis, bits):
        return jnp.concatenate([block] + [exchanged(block, axis, bit) for bit in bits])

    gathered = collected(collected(router_column, "x", (1, 2, 3)), "z", (1, 2, 3))
    gathered = collected(gathered, "z", (4,)).reshape(experts, width)
    expert_ids_here = jnp.arange(experts, dtype=jnp.int32)
    order = (expert_ids_here ^ expert)[:, None] == expert_ids_here[None, :]
    router_grad = lax.dot_general(
        gathered,
        order.astype(f32),
        (((0,), (0,)), ((), ())),
        precision=lax.Precision.HIGHEST,
        preferred_element_type=f32,
    )

    down_half = (
        down_terms(fronts[0])
        + shifted(down_before, "y", -1).astype(f32)
        + shifted(down_after, "y", 1).astype(f32)
        + shifted(down_across, "y", 2).astype(f32)
    )
    down_other = exchanged(down_half, "tower", 1)
    down_grad = jnp.where(
        tower == 0,
        jnp.concatenate([down_half, down_other], axis=1),
        jnp.concatenate([down_other, down_half], axis=1),
    )
    embed_grads = pair_loss(embeds, logit_scale_log, pairwise_logit_bias, dp_index)
    return (tokens_grad, router_grad, down_grad, embed_grads[None])


def solution(mesh):
    towers, chips = mesh.devices.shape
    grid = Mesh(
        mesh.devices.reshape(towers, chips // (columns * line), columns, line),
        ("tower", "z", "x", "y"),
    )
    dp = ("z", "x", "y")
    rows = P(("tower",) + dp, None)
    placed = (
        rows,
        P(),
        P(),
        rows,
        P(None, dp),
        P(dp, None),
        rows,
        P("tower", dp, None),
        P(),
        P(),
    )
    return jax.shard_map(
        body,
        mesh=grid,
        in_specs=placed,
        out_specs=(rows, P(), P(dp, None), P("tower", dp, None)),
        check_vma=False,
    )
```

```python
import functools

import jax
import jax.numpy as jnp
from jax import lax
from jax.experimental import pallas as pl
from jax.experimental.pallas import tpu as pltpu
from jax.sharding import Mesh, PartitionSpec as P

epsilon = 1e-06
gelu_root = 0.7978845608028654
gelu_cubic = 0.044715

line = 4
columns = 4


def shifted(block, axis, step):
    count = lax.axis_size(axis)
    return lax.ppermute(block, axis, [(i, (i + step) % count) for i in range(count)])


def exchanged(block, axis, bit):
    count = lax.axis_size(axis)
    return lax.ppermute(block, axis, [(i, i ^ bit) for i in range(count)])


def product(left, right):
    return jnp.dot(left, right, preferred_element_type=jnp.float32)


def contract_rows(left, right):
    return lax.dot_general(
        left, right, (((0,), (0,)), ((), ())), preferred_element_type=jnp.float32
    )


def contracted_columns(left, right):
    return lax.dot_general(
        left, right, (((1,), (1,)), ((), ())), preferred_element_type=jnp.float32
    )


def gelu_pair(values):
    inner = gelu_root * (values + gelu_cubic * values * values * values)
    tangent = jnp.tanh(inner)
    slope = 0.5 * (1.0 + tangent) + 0.5 * values * (1.0 - tangent * tangent) * gelu_root * (
        1.0 + 3.0 * gelu_cubic * values * values
    )
    return 0.5 * values * (1.0 + tangent), slope


def local_call(kernel, out_shape, operands, vmem, flops=1, **options):
    return pl.pallas_call(
        kernel,
        out_shape=out_shape,
        compiler_params=pltpu.CompilerParams(vmem_limit_bytes=vmem << 20),
        cost_estimate=pl.CostEstimate(flops=flops, bytes_accessed=1, transcendentals=0),
        **options,
    )(*operands)


def shape_of(shape, dtype):
    return jax.ShapeDtypeStruct(shape, dtype)


def staged_call(run, out_shape, operands, vmem, flops=1, scalars=(), scratch=()):
    fixed, count, results = len(scalars), len(operands), len(out_shape)

    def kernel(*refs):
        numbers, refs = refs[:fixed], refs[fixed:]
        sources, refs = refs[:count], refs[count:]
        targets, refs = refs[:results], refs[results:]
        held, refs = refs[:count], refs[count:]
        out, refs = refs[:results], refs[results:]
        in_sems, out_sems, rest = refs[0], refs[1], refs[2:]
        fetched = [
            pltpu.make_async_copy(sources[i], held[i], in_sems.at[i]) for i in range(count)
        ]
        sent = [
            pltpu.make_async_copy(out[j], targets[j], out_sems.at[j]) for j in range(results)
        ]
        for copy in fetched:
            copy.start()
        arrived = set()

        def need(i):
            if i not in arrived:
                fetched[i].wait()
                arrived.add(i)
            return held[i]

        run(need, out, lambda j: sent[j].start(), *numbers, *rest)
        for copy in sent:
            copy.wait()

    apart = pl.BlockSpec(memory_space=pltpu.HBM)
    return local_call(
        kernel,
        out_shape,
        (*scalars, *operands),
        vmem,
        flops,
        in_specs=[pl.BlockSpec(memory_space=pltpu.SMEM)] * fixed + [apart] * count,
        out_specs=[apart] * results,
        scratch_shapes=[pltpu.VMEM(v.shape, v.dtype) for v in operands]
        + [pltpu.VMEM(v.shape, v.dtype) for v in out_shape]
        + [pltpu.SemaphoreType.DMA((count,)), pltpu.SemaphoreType.DMA((results,))]
        + list(scratch),
    )


def slot_step(capacity, experts, need, out, send, tower_ref):
    count, half = out[0].shape
    tower = tower_ref[0]
    choices = need(0)[...]
    total = choices.shape[0]
    onehot = choices == lax.broadcasted_iota(jnp.int32, (total, experts), 1)
    lower_tri = lax.broadcasted_iota(jnp.int32, (total, total), 0) >= lax.broadcasted_iota(
        jnp.int32, (total, total), 1
    )
    running = product(lower_tri.astype(jnp.bfloat16), onehot.astype(jnp.bfloat16))
    rank = jnp.sum(jnp.where(onehot, running, 0.0), axis=1, keepdims=True) - 1.0
    first_row = choices.astype(jnp.float32) * (2.0 * capacity) + rank
    first_row = jnp.broadcast_to(first_row, (total, 128)).T[0:1].astype(jnp.int32)
    low_row = first_row + capacity * tower
    high_row = first_row + capacity * (1 - tower)
    out[2][0:1] = low_row
    out[2][1:2] = high_row
    send(2)
    ids = lax.broadcasted_iota(jnp.int32, (count, total), 0)
    low_place = (ids == low_row).astype(jnp.bfloat16)
    high_place = (ids == high_row).astype(jnp.bfloat16)
    for k in range(2):
        values = need(1 + k)
        rows = product(low_place, values[:, :half]) + product(high_place, values[:, half:])
        out[k][...] = rows.astype(jnp.bfloat16)
        send(k)


def token_step(need, out, send):
    rows_of = need(0)
    rows = need(1)[...]
    count, half = rows.shape
    total = out[0].shape[0]
    ids = lax.broadcasted_iota(jnp.int32, (count, total), 0)
    for part in range(2):
        place = (ids == rows_of[part : part + 1]).astype(jnp.float32).T.astype(jnp.bfloat16)
        out[0][:, part * half : (part + 1) * half] = product(place, rows).astype(jnp.bfloat16)
    send(0)


def taken(rows, slot_of_row, slots):
    ids = lax.broadcasted_iota(jnp.int32, (slots, rows.shape[0]), 0)
    return product((ids == slot_of_row).astype(jnp.bfloat16), rows)


def feature_mean(first, second, width):
    total = jnp.sum(first, axis=1, keepdims=True) + jnp.sum(second, axis=1, keepdims=True)
    return total / width


def spread_lanes(column):
    return jnp.broadcast_to(column, (column.shape[0], 128))


def front(normed, up_first, up_second, out, send, base):
    half = up_first.shape[0]
    preact = product(normed[:, :half], up_first[...]) + product(
        normed[:, half:], up_second[...]
    )
    gelu, slope = gelu_pair(preact)
    out[base][...] = slope
    send(base)
    out[base + 1][...] = gelu.astype(jnp.bfloat16)
    send(base + 1)
    out[base + 2][...] = gelu.T.astype(jnp.bfloat16)
    send(base + 2)


def norm_step(shards, need, out, send):
    slots, width = out[0].shape
    half = width // 2
    maps, rows = need(0), need(1)[...]
    first, second = (taken(rows, maps[part : part + 1], slots) for part in range(2))
    mean = feature_mean(first, second, width)
    first, second = first - mean, second - mean
    root = lax.rsqrt(feature_mean(first * first, second * second, width) + epsilon)
    first, second = first * root, second * root
    out[1][:, :half] = first
    out[1][:, half:] = second
    send(1)
    gain, column = need(2), need(3)
    first = (first * gain[0:1]).astype(jnp.bfloat16)
    second = (second * gain[1:2]).astype(jnp.bfloat16)
    out[0][:, :half] = first
    out[0][:, half:] = second
    send(0)
    logits = jnp.sum(first.astype(jnp.float32) * column[0:1], axis=1, keepdims=True) + jnp.sum(
        second.astype(jnp.float32) * column[1:2], axis=1, keepdims=True
    )
    out[2][0] = spread_lanes(root)
    out[2][1] = spread_lanes(jax.nn.sigmoid(logits))
    send(2)
    for shard in range(shards):
        front(out[0], need(4 + 2 * shard), need(5 + 2 * shard), out, send, 3 + 3 * shard)


def front_step(need, out, send):
    front(need(0), need(1), need(2), out, send, 0)


def gate_step(need, out, send):
    slots, width = out[0].shape
    half = width // 2
    maps, rows = need(0), need(1)[...]
    gates = need(2)[1][:, 0:1]
    for part in range(2):
        values = taken(rows, maps[part : part + 1], slots)
        out[0][:, part * half : (part + 1) * half] = values.astype(jnp.bfloat16)
        out[1][:, part * half : (part + 1) * half] = (gates * values).astype(jnp.bfloat16)
    send(0)
    send(1)
    for term in range((len(out) - 2) // 2):
        down_term(need(3 + term), out[1], out, send, 2 + 2 * term)


def down_term(turned, output, out, send, base):
    half = out[base].shape[1]
    out[base + 1][...] = product(turned[...], output[:, half:]).astype(jnp.bfloat16)
    send(base + 1)
    out[base][...] = product(turned[...], output[:, :half])
    send(base)


def down_step(need, out, send):
    down_term(need(0), need(1), out, send, 0)


def hidden_step(shards, need, out, send):
    output = need(0)
    half = output.shape[1] // 2
    gated = None
    for shard in range(shards):
        base = 3 + 4 * shard
        hidden_grad = contracted_columns(
            output[:, :half], need(base + 2)[...]
        ) + contracted_columns(output[:, half:], need(base + 3)[...])
        term = jnp.sum(
            need(base + 1)[...].astype(jnp.float32) * hidden_grad, axis=1, keepdims=True
        )
        gated = term if gated is None else gated + term
        out[2 + shard][...] = (hidden_grad * need(base)[...]).astype(jnp.bfloat16)
        send(2 + shard)
    logit_grad = gated * (1.0 - need(1)[1][:, 0:1])
    out[0][...] = spread_lanes(logit_grad)
    send(0)
    normed = need(2)
    for part in range(2):
        out[1][part : part + 1] = jnp.sum(
            normed[:, part * half : (part + 1) * half].astype(jnp.float32) * logit_grad,
            axis=0,
            keepdims=True,
        )
    send(1)


def back_step(shards, need, out, send, first_sum, second_sum):
    count, half = out[0].shape
    width = 2 * half
    for shard in range(shards):
        grad = need(3 * shard)[...]
        first = contracted_columns(grad, need(3 * shard + 1)[...])
        second = contracted_columns(grad, need(3 * shard + 2)[...])
        if shard == 0:
            first_sum[...], second_sum[...] = first, second
        else:
            first_sum[...] += first
            second_sum[...] += second
    base = 3 * shards
    logit_grad = need(base)[:, 0:1]
    unit, cotan, root = need(base + 1), need(base + 2), need(base + 3)[0][:, 0:1]
    row_of_slot, gain, column = need(base + 4), need(base + 5), need(base + 6)
    first = (first_sum[...] + logit_grad * column[0:1]) * gain[0:1]
    second = (second_sum[...] + logit_grad * column[1:2]) * gain[1:2]
    unit_first, unit_second = unit[:, :half], unit[:, half:]
    grad_mean = feature_mean(first, second, width)
    grad_unit = feature_mean(first * unit_first, second * unit_second, width)
    first = cotan[:, :half].astype(jnp.float32) + root * (
        first - grad_mean - unit_first * grad_unit
    )
    second = cotan[:, half:].astype(jnp.float32) + root * (
        second - grad_mean - unit_second * grad_unit
    )
    ids = lax.broadcasted_iota(jnp.int32, (count, row_of_slot.shape[1]), 0)
    rows = product(
        (ids == row_of_slot[0:1]).astype(jnp.bfloat16), first.astype(jnp.bfloat16)
    ) + product((ids == row_of_slot[1:2]).astype(jnp.bfloat16), second.astype(jnp.bfloat16))
    out[0][...] = rows.astype(jnp.bfloat16)
    send(0)


def joined_kernel(tower_ref, own_ref, other_ref, whole_ref):
    half = own_ref.shape[1]
    own_at = pl.multiple_of(tower_ref[0] * half, 128)
    other_at = pl.multiple_of((1 - tower_ref[0]) * half, 128)
    whole_ref[:, pl.ds(own_at, half)] = own_ref[...]
    whole_ref[:, pl.ds(other_at, half)] = other_ref[...]


def pair_loss(embeds, logit_scale_log, pairwise_logit_bias, dp_index):
    own_rows = embeds[0].astype(jnp.float32)
    local_member = (
        own_rows * lax.rsqrt(jnp.sum(own_rows * own_rows, axis=-1, keepdims=True) + epsilon)
    ).astype(jnp.bfloat16)
    other_unit = exchanged(local_member, "tower", 1)
    softness_factor = jnp.exp(logit_scale_log)
    pair_rows = local_member.shape[0]
    row_global = dp_index * pair_rows + jnp.arange(pair_rows, dtype=jnp.int32)
    panel_rows = lax.all_gather(other_unit, ("z", "x", "y"), axis=0, tiled=True)
    pair_scores = (
        softness_factor * contracted_columns(local_member, panel_rows) + pairwise_logit_bias
    )
    col_global = jnp.arange(panel_rows.shape[0], dtype=jnp.int32)
    pair_labels = jnp.where(row_global[:, None] == col_global[None, :], 1.0, -1.0).astype(
        jnp.float32
    )
    panel_weights = (
        -pair_labels * jax.nn.sigmoid(-pair_labels * pair_scores) * softness_factor
    ).astype(jnp.bfloat16)
    return product(panel_weights, panel_rows)


def body(
    tokens,
    norm_gain,
    router,
    expert_ids,
    up_weights,
    down_weights,
    cotangent,
    embeds,
    logit_scale_log,
    pairwise_logit_bias,
):
    token_total, width = tokens.shape
    hidden = up_weights.shape[1]
    experts = router.shape[1]
    capacity = 3 * token_total // (2 * experts)
    half = width // 2
    slots = experts * capacity
    tower = lax.axis_index("tower")
    expert = lax.axis_index("z") * columns + lax.axis_index("x")
    dp_index = expert * line + lax.axis_index("y")
    bf16, f32 = jnp.bfloat16, jnp.float32

    def halves(values, axis):
        return (
            lax.dynamic_slice_in_dim(values, tower * half, half, axis),
            lax.dynamic_slice_in_dim(values, (1 - tower) * half, half, axis),
        )

    up_own, down_own = halves(up_weights, 0), halves(down_weights, 1)
    up_before = shifted(up_own[0], "y", 1)
    up_after = shifted(up_own[0], "y", -1)
    down_part, up_before, up_after = lax.optimization_barrier((down_own[0], up_before, up_after))
    down_before = shifted(down_part, "y", 1)
    down_after = shifted(down_part, "y", -1)

    tower_word = tower.astype(jnp.int32).reshape(1)
    sent_ids = jnp.arange(2 * slots, dtype=jnp.int32)
    slot_of_sent = sent_ids // (2 * capacity) * capacity + sent_ids % capacity
    in_first = sent_ids % (2 * capacity) < capacity
    slot_maps = jnp.stack(
        [jnp.where(in_first, slot_of_sent, -1), jnp.where(in_first, -1, slot_of_sent)]
    )
    slot_ids = jnp.arange(slots, dtype=jnp.int32)
    first_row = slot_ids // capacity * (2 * capacity) + slot_ids % capacity
    row_maps = jnp.stack([first_row, first_row + capacity])

    def spread(rows):
        return lax.all_to_all(
            rows.reshape(experts, 2 * capacity, half),
            ("z", "x"),
            split_axis=0,
            concat_axis=0,
            tiled=True,
        ).reshape(2 * slots, half)

    def both(piece):
        return piece, exchanged(piece, "tower", 1)

    token_rows, cotan_rows, token_maps = staged_call(
        functools.partial(slot_step, capacity, experts),
        [shape_of((2 * slots, half), bf16)] * 2 + [shape_of((2, token_total), jnp.int32)],
        (expert_ids, tokens, cotangent),
        16,
        scalars=(tower_word,),
    )
    token_rows = spread(token_rows)
    cotan_rows, token_rows, down_before, down_after = lax.optimization_barrier(
        (cotan_rows, token_rows, down_before, down_after)
    )
    cotan_rows = spread(cotan_rows)
    up_across = shifted(up_before, "y", 1)
    down_across = shifted(down_after, "y", -1)
    ups = [up_own] + [both(piece) for piece in (up_before, up_after, up_across)]
    downs = [down_own] + [both(piece) for piece in (down_before, down_after, down_across)]

    def features(values):
        return jnp.concatenate(halves(values.astype(f32)[None, :], 1), axis=0)

    gain = features(norm_gain)
    column = features(lax.dynamic_slice_in_dim(router, expert, 1, 1)[:, 0])
    shards, near = len(ups), len(ups) - 1
    front_shapes = [
        shape_of((slots, hidden), f32),
        shape_of((slots, hidden), bf16),
        shape_of((hidden, slots), bf16),
    ]
    term_shapes = [shape_of((hidden, half), f32), shape_of((hidden, half), bf16)]
    normed, unit, scales, *near_fronts = staged_call(
        functools.partial(norm_step, near),
        [shape_of((slots, width), bf16), shape_of((slots, width), f32)]
        + [shape_of((2, slots, 128), f32)]
        + front_shapes * near,
        (slot_maps, token_rows, gain, column, *(p for pair in ups[:near] for p in pair)),
        32,
    )
    fronts = [near_fronts[3 * k : 3 * k + 3] for k in range(near)]
    fronts.append(staged_call(front_step, front_shapes, (normed,) + ups[near], 16))
    cotan_rows, across_turned = lax.optimization_barrier((cotan_rows, fronts[near][2]))
    cotan, output, *terms = staged_call(
        gate_step,
        [shape_of((slots, width), bf16)] * 2 + term_shapes * near,
        (slot_maps, cotan_rows, scales, fronts[1][2], fronts[2][2], across_turned),
        28,
    )
    logit_grad, router_halves, *preact_grads = staged_call(
        functools.partial(hidden_step, shards),
        [shape_of((slots, 128), f32), shape_of((2, half), f32)]
        + [shape_of((slots, hidden), bf16)] * shards,
        (output, scales, normed)
        + tuple(p for k in range(shards) for p in (*fronts[k][:2], *downs[k])),
        28,
    )

    def tower_sum(first, second):
        return first + exchanged(second, "tower", 1).astype(f32)

    down_before, down_after, down_across = (
        tower_sum(*terms[2 * term : 2 * term + 2]).astype(bf16) for term in range(near)
    )
    logit_grad, down_before, down_after, down_across = lax.optimization_barrier(
        (logit_grad, down_before, down_after, down_across)
    )
    down_before = shifted(down_before, "y", -1)
    down_after = shifted(down_after, "y", 1)
    down_across = shifted(down_across, "y", 2)
    back_rows = staged_call(
        functools.partial(back_step, shards),
        [shape_of((2 * slots, half), bf16)],
        tuple(p for k in range(shards) for p in (preact_grads[k], *ups[k]))
        + (logit_grad, unit, cotan, scales, row_maps, gain, column),
        32,
        2 * shards * slots * width * hidden,
        scratch=[pltpu.VMEM((slots, half), f32), pltpu.VMEM((slots, half), f32)],
    )[0]
    back_rows, router_halves = lax.optimization_barrier((back_rows, router_halves))
    returned = spread(back_rows)
    tokens_grad = staged_call(
        token_step, [shape_of((token_total, width), bf16)], (token_maps, returned), 12
    )[0]

    router_column = jnp.where(
        tower == 0, router_halves, jnp.concatenate([router_halves[1:], router_halves[:1]])
    ).reshape(-1, 128)
    router_column = (router_column + exchanged(router_column, "tower", 1))[None]

    router_column = router_column + exchanged(router_column, "y", 1)
    gathered = router_column + exchanged(router_column, "y", 2)
    for axis, bits in (("x", (1, 2)), ("z", (1, 2, 4))):
        for bit in bits:
            gathered = jnp.concatenate([gathered, exchanged(gathered, axis, bit)])
    gathered = gathered.reshape(experts, width)
    embed_grads = pair_loss(embeds, logit_scale_log, pairwise_logit_bias, dp_index)
    down_before, down_after, down_across, embed_grads = lax.optimization_barrier(
        (down_before, down_after, down_across, embed_grads)
    )
    expert_ids_here = jnp.arange(experts, dtype=jnp.int32)
    order = (expert_ids_here ^ expert)[:, None] == expert_ids_here[None, :]
    router_grad = lax.dot_general(
        gathered,
        order.astype(f32),
        (((0,), (0,)), ((), ())),
        precision=lax.Precision.HIGHEST,
        preferred_element_type=f32,
    )

    own_terms = staged_call(down_step, term_shapes, (fronts[0][2], output), 16)
    down_half = (
        tower_sum(*own_terms)
        + down_before.astype(f32)
        + down_after.astype(f32)
        + down_across.astype(f32)
    )
    down_other = exchanged(down_half, "tower", 1)
    whole = pl.BlockSpec(memory_space=pltpu.VMEM)
    down_grad = local_call(
        joined_kernel,
        [shape_of((hidden, width), f32)],
        (tower_word, down_half, down_other),
        16,
        in_specs=[pl.BlockSpec(memory_space=pltpu.SMEM), whole, whole],
    )[0]
    return (tokens_grad, router_grad, down_grad, embed_grads[None])


def solution(mesh):
    towers, chips = mesh.devices.shape
    grid = Mesh(
        mesh.devices.reshape(towers, chips // (columns * line), columns, line),
        ("tower", "z", "x", "y"),
    )
    dp = ("z", "x", "y")
    rows = P(("tower",) + dp, None)
    placed = (
        rows,
        P(),
        P(),
        rows,
        P(None, dp),
        P(dp, None),
        rows,
        P("tower", dp, None),
        P(),
        P(),
    )
    return jax.shard_map(
        body,
        mesh=grid,
        in_specs=placed,
        out_specs=(rows, P(), P(dp, None), P("tower", dp, None)),
        check_vma=False,
    )
```

```python
import functools

import jax
import jax.numpy as jnp
from jax import lax
from jax.experimental import pallas as pl
from jax.experimental.pallas import tpu as pltpu
from jax.sharding import Mesh, PartitionSpec as P

epsilon = 1e-06
gelu_root = 0.7978845608028654
gelu_cubic = 0.044715

line = 4
columns = 4


def shifted(block, axis, step):
    count = lax.axis_size(axis)
    return lax.ppermute(block, axis, [(i, (i + step) % count) for i in range(count)])


def exchanged(block, axis, bit):
    count = lax.axis_size(axis)
    return lax.ppermute(block, axis, [(i, i ^ bit) for i in range(count)])


def product(left, right):
    return jnp.dot(left, right, preferred_element_type=jnp.float32)


def contract_rows(left, right):
    return lax.dot_general(
        left, right, (((0,), (0,)), ((), ())), preferred_element_type=jnp.float32
    )


def contracted_columns(left, right):
    return lax.dot_general(
        left, right, (((1,), (1,)), ((), ())), preferred_element_type=jnp.float32
    )


def gelu_pair(values):
    inner = gelu_root * (values + gelu_cubic * values * values * values)
    tangent = jnp.tanh(inner)
    slope = 0.5 * (1.0 + tangent) + 0.5 * values * (1.0 - tangent * tangent) * gelu_root * (
        1.0 + 3.0 * gelu_cubic * values * values
    )
    return 0.5 * values * (1.0 + tangent), slope


def local_call(kernel, out_shape, operands, vmem, flops=1, **options):
    return pl.pallas_call(
        kernel,
        out_shape=out_shape,
        compiler_params=pltpu.CompilerParams(vmem_limit_bytes=vmem << 20),
        cost_estimate=pl.CostEstimate(flops=flops, bytes_accessed=1, transcendentals=0),
        **options,
    )(*operands)


def shape_of(shape, dtype):
    return jax.ShapeDtypeStruct(shape, dtype)


def staged_call(run, out_shape, operands, vmem, flops=1, scalars=(), scratch=()):
    fixed, count, results = len(scalars), len(operands), len(out_shape)

    def kernel(*refs):
        numbers, refs = refs[:fixed], refs[fixed:]
        sources, refs = refs[:count], refs[count:]
        targets, refs = refs[:results], refs[results:]
        held, refs = refs[:count], refs[count:]
        out, refs = refs[:results], refs[results:]
        in_sems, out_sems, rest = refs[0], refs[1], refs[2:]
        fetched = [
            pltpu.make_async_copy(sources[i], held[i], in_sems.at[i]) for i in range(count)
        ]
        sent = [
            pltpu.make_async_copy(out[j], targets[j], out_sems.at[j]) for j in range(results)
        ]
        for copy in fetched:
            copy.start()
        arrived = set()

        def need(i):
            if i not in arrived:
                fetched[i].wait()
                arrived.add(i)
            return held[i]

        run(need, out, lambda j: sent[j].start(), *numbers, *rest)
        for copy in sent:
            copy.wait()

    apart = pl.BlockSpec(memory_space=pltpu.HBM)
    pinned = [pltpu.with_memory_space_constraint(v, pltpu.HBM) for v in operands]
    return local_call(
        kernel,
        [pltpu.HBM(v.shape, v.dtype) for v in out_shape],
        (*scalars, *pinned),
        vmem,
        flops,
        in_specs=[pl.BlockSpec(memory_space=pltpu.SMEM)] * fixed + [apart] * count,
        out_specs=[apart] * results,
        scratch_shapes=[pltpu.VMEM(v.shape, v.dtype) for v in operands]
        + [pltpu.VMEM(v.shape, v.dtype) for v in out_shape]
        + [pltpu.SemaphoreType.DMA((count,)), pltpu.SemaphoreType.DMA((results,))]
        + list(scratch),
    )


def slot_step(capacity, experts, need, out, send, tower_ref):
    count, half = out[0].shape
    tower = tower_ref[0]
    choices = need(0)[...]
    total = choices.shape[0]
    onehot = choices == lax.broadcasted_iota(jnp.int32, (total, experts), 1)
    lower_tri = lax.broadcasted_iota(jnp.int32, (total, total), 0) >= lax.broadcasted_iota(
        jnp.int32, (total, total), 1
    )
    running = product(lower_tri.astype(jnp.bfloat16), onehot.astype(jnp.bfloat16))
    rank = jnp.sum(jnp.where(onehot, running, 0.0), axis=1, keepdims=True) - 1.0
    first_row = choices.astype(jnp.float32) * (2.0 * capacity) + rank
    first_row = jnp.broadcast_to(first_row, (total, 128)).T[0:1].astype(jnp.int32)
    low_row = first_row + capacity * tower
    high_row = first_row + capacity * (1 - tower)
    out[2][0:1] = low_row
    out[2][1:2] = high_row
    send(2)
    ids = lax.broadcasted_iota(jnp.int32, (count, total), 0)
    low_place = (ids == low_row).astype(jnp.bfloat16)
    high_place = (ids == high_row).astype(jnp.bfloat16)
    for k in range(2):
        values = need(1 + k)
        rows = product(low_place, values[:, :half]) + product(high_place, values[:, half:])
        out[k][...] = rows.astype(jnp.bfloat16)
        send(k)


def token_step(need, out, send):
    rows_of = need(0)
    rows = need(1)[...]
    count, half = rows.shape
    total = out[0].shape[0]
    ids = lax.broadcasted_iota(jnp.int32, (count, total), 0)
    for part in range(2):
        place = (ids == rows_of[part : part + 1]).astype(jnp.float32).T.astype(jnp.bfloat16)
        out[0][:, part * half : (part + 1) * half] = product(place, rows).astype(jnp.bfloat16)
    send(0)


def taken(rows, slot_of_row, slots):
    ids = lax.broadcasted_iota(jnp.int32, (slots, rows.shape[0]), 0)
    return product((ids == slot_of_row).astype(jnp.bfloat16), rows)


def feature_mean(first, second, width):
    total = jnp.sum(first, axis=1, keepdims=True) + jnp.sum(second, axis=1, keepdims=True)
    return total / width


def spread_lanes(column):
    return jnp.broadcast_to(column, (column.shape[0], 128))


def front(normed, up_first, up_second, out, send, base):
    half = up_first.shape[0]
    preact = product(normed[:, :half], up_first[...]) + product(
        normed[:, half:], up_second[...]
    )
    gelu, slope = gelu_pair(preact)
    out[base][...] = slope.astype(jnp.bfloat16)
    send(base)
    out[base + 1][...] = gelu.astype(jnp.bfloat16)
    send(base + 1)
    out[base + 2][...] = gelu.T.astype(jnp.bfloat16)
    send(base + 2)


def norm_step(shards, need, out, send):
    slots, width = out[0].shape
    half = width // 2
    maps, rows = need(0), need(1)[...]
    first, second = (taken(rows, maps[part : part + 1], slots) for part in range(2))
    mean = feature_mean(first, second, width)
    first, second = first - mean, second - mean
    root = lax.rsqrt(feature_mean(first * first, second * second, width) + epsilon)
    first, second = first * root, second * root
    out[1][:, :half] = first.astype(jnp.bfloat16)
    out[1][:, half:] = second.astype(jnp.bfloat16)
    send(1)
    gain, column = need(2), need(3)
    first = (first * gain[0:1]).astype(jnp.bfloat16)
    second = (second * gain[1:2]).astype(jnp.bfloat16)
    out[0][:, :half] = first
    out[0][:, half:] = second
    send(0)
    logits = jnp.sum(first.astype(jnp.float32) * column[0:1], axis=1, keepdims=True) + jnp.sum(
        second.astype(jnp.float32) * column[1:2], axis=1, keepdims=True
    )
    out[2][0] = spread_lanes(root)
    out[2][1] = spread_lanes(jax.nn.sigmoid(logits))
    send(2)
    for shard in range(shards):
        front(out[0], need(4 + 2 * shard), need(5 + 2 * shard), out, send, 3 + 3 * shard)


def front_step(need, out, send):
    front(need(0), need(1), need(2), out, send, 0)


def gate_step(need, out, send):
    slots, width = out[0].shape
    half = width // 2
    maps, rows = need(0), need(1)[...]
    gates = need(2)[1][:, 0:1]
    for part in range(2):
        values = taken(rows, maps[part : part + 1], slots)
        out[0][:, part * half : (part + 1) * half] = values.astype(jnp.bfloat16)
        out[1][:, part * half : (part + 1) * half] = (gates * values).astype(jnp.bfloat16)
    send(0)
    send(1)
    for term in range((len(out) - 2) // 2):
        down_term(need(3 + term), out[1], out, send, 2 + 2 * term)


def down_term(turned, output, out, send, base):
    half = out[base].shape[1]
    out[base + 1][...] = product(turned[...], output[:, half:]).astype(jnp.bfloat16)
    send(base + 1)
    out[base][...] = product(turned[...], output[:, :half]).astype(out[base].dtype)
    send(base)


def down_step(need, out, send):
    down_term(need(0), need(1), out, send, 0)


def hidden_step(shards, need, out, send):
    output = need(0)
    half = output.shape[1] // 2
    gated = None
    for shard in range(shards):
        base = 3 + 4 * shard
        hidden_grad = contracted_columns(
            output[:, :half], need(base + 2)[...]
        ) + contracted_columns(output[:, half:], need(base + 3)[...])
        term = jnp.sum(
            need(base + 1)[...].astype(jnp.float32) * hidden_grad, axis=1, keepdims=True
        )
        gated = term if gated is None else gated + term
        out[2 + shard][...] = (hidden_grad * need(base)[...].astype(jnp.float32)).astype(jnp.bfloat16)
        send(2 + shard)
    logit_grad = gated * (1.0 - need(1)[1][:, 0:1])
    out[0][...] = spread_lanes(logit_grad)
    send(0)
    normed = need(2)
    for part in range(2):
        out[1][part : part + 1] = jnp.sum(
            normed[:, part * half : (part + 1) * half].astype(jnp.float32) * logit_grad,
            axis=0,
            keepdims=True,
        )
    send(1)


def back_step(shards, need, out, send, first_sum, second_sum):
    count, half = out[0].shape
    width = 2 * half
    for shard in range(shards):
        grad = need(3 * shard)[...]
        first = contracted_columns(grad, need(3 * shard + 1)[...])
        second = contracted_columns(grad, need(3 * shard + 2)[...])
        if shard == 0:
            first_sum[...], second_sum[...] = first, second
        else:
            first_sum[...] += first
            second_sum[...] += second
    base = 3 * shards
    logit_grad = need(base)[:, 0:1]
    unit, cotan, root = need(base + 1), need(base + 2), need(base + 3)[0][:, 0:1]
    row_of_slot, gain, column = need(base + 4), need(base + 5), need(base + 6)
    first = (first_sum[...] + logit_grad * column[0:1]) * gain[0:1]
    second = (second_sum[...] + logit_grad * column[1:2]) * gain[1:2]
    unit_first = unit[:, :half].astype(jnp.float32)
    unit_second = unit[:, half:].astype(jnp.float32)
    grad_mean = feature_mean(first, second, width)
    grad_unit = feature_mean(first * unit_first, second * unit_second, width)
    first = cotan[:, :half].astype(jnp.float32) + root * (
        first - grad_mean - unit_first * grad_unit
    )
    second = cotan[:, half:].astype(jnp.float32) + root * (
        second - grad_mean - unit_second * grad_unit
    )
    ids = lax.broadcasted_iota(jnp.int32, (count, row_of_slot.shape[1]), 0)
    rows = product(
        (ids == row_of_slot[0:1]).astype(jnp.bfloat16), first.astype(jnp.bfloat16)
    ) + product((ids == row_of_slot[1:2]).astype(jnp.bfloat16), second.astype(jnp.bfloat16))
    out[0][...] = rows.astype(jnp.bfloat16)
    send(0)


def joined_kernel(tower_ref, own_ref, other_ref, whole_ref):
    half = own_ref.shape[1]
    own_at = pl.multiple_of(tower_ref[0] * half, 128)
    other_at = pl.multiple_of((1 - tower_ref[0]) * half, 128)
    whole_ref[:, pl.ds(own_at, half)] = own_ref[...]
    whole_ref[:, pl.ds(other_at, half)] = other_ref[...]


def pair_loss(embeds, logit_scale_log, pairwise_logit_bias, dp_index):
    own_rows = embeds[0].astype(jnp.float32)
    local_member = (
        own_rows * lax.rsqrt(jnp.sum(own_rows * own_rows, axis=-1, keepdims=True) + epsilon)
    ).astype(jnp.bfloat16)
    other_unit = exchanged(local_member, "tower", 1)
    softness_factor = jnp.exp(logit_scale_log)
    pair_rows = local_member.shape[0]
    row_global = dp_index * pair_rows + jnp.arange(pair_rows, dtype=jnp.int32)
    panel_rows = lax.all_gather(other_unit, ("z", "x", "y"), axis=0, tiled=True)
    pair_scores = (
        softness_factor * contracted_columns(local_member, panel_rows) + pairwise_logit_bias
    )
    col_global = jnp.arange(panel_rows.shape[0], dtype=jnp.int32)
    pair_labels = jnp.where(row_global[:, None] == col_global[None, :], 1.0, -1.0).astype(
        jnp.float32
    )
    panel_weights = (
        -pair_labels * jax.nn.sigmoid(-pair_labels * pair_scores) * softness_factor
    ).astype(jnp.bfloat16)
    return product(panel_weights, panel_rows)


def body(
    tokens,
    norm_gain,
    router,
    expert_ids,
    up_weights,
    down_weights,
    cotangent,
    embeds,
    logit_scale_log,
    pairwise_logit_bias,
):
    token_total, width = tokens.shape
    hidden = up_weights.shape[1]
    experts = router.shape[1]
    capacity = 3 * token_total // (2 * experts)
    half = width // 2
    slots = experts * capacity
    tower = lax.axis_index("tower")
    expert = lax.axis_index("z") * columns + lax.axis_index("x")
    dp_index = expert * line + lax.axis_index("y")
    bf16, f32 = jnp.bfloat16, jnp.float32

    def halves(values, axis):
        return (
            lax.dynamic_slice_in_dim(values, tower * half, half, axis),
            lax.dynamic_slice_in_dim(values, (1 - tower) * half, half, axis),
        )

    up_own, down_own = halves(up_weights, 0), halves(down_weights, 1)
    up_before = shifted(up_own[0], "y", 1)
    up_after = shifted(up_own[0], "y", -1)
    down_before = shifted(down_own[0], "y", 1)
    down_after = shifted(down_own[0], "y", -1)

    tower_word = tower.astype(jnp.int32).reshape(1)
    sent_ids = jnp.arange(2 * slots, dtype=jnp.int32)
    slot_of_sent = sent_ids // (2 * capacity) * capacity + sent_ids % capacity
    in_first = sent_ids % (2 * capacity) < capacity
    slot_maps = jnp.stack(
        [jnp.where(in_first, slot_of_sent, -1), jnp.where(in_first, -1, slot_of_sent)]
    )
    slot_ids = jnp.arange(slots, dtype=jnp.int32)
    first_row = slot_ids // capacity * (2 * capacity) + slot_ids % capacity
    row_maps = jnp.stack([first_row, first_row + capacity])

    def spread(rows):
        return lax.all_to_all(
            rows.reshape(experts, 2 * capacity, half),
            ("z", "x"),
            split_axis=0,
            concat_axis=0,
            tiled=True,
        ).reshape(2 * slots, half)

    def both(piece):
        return piece, exchanged(piece, "tower", 1)

    token_rows, cotan_rows, token_maps = staged_call(
        functools.partial(slot_step, capacity, experts),
        [shape_of((2 * slots, half), bf16)] * 2 + [shape_of((2, token_total), jnp.int32)],
        (expert_ids, tokens, cotangent),
        16,
        scalars=(tower_word,),
    )
    token_rows, up_before, up_after = lax.optimization_barrier((token_rows, up_before, up_after))
    token_rows = spread(token_rows)
    cotan_rows, token_rows = lax.optimization_barrier((cotan_rows, token_rows))
    cotan_rows = spread(cotan_rows)
    up_across = shifted(up_before, "y", 1)
    down_across = shifted(down_after, "y", -1)
    ups = [up_own] + [both(piece) for piece in (up_before, up_after, up_across)]
    downs = [down_own] + [both(piece) for piece in (down_before, down_after, down_across)]

    def features(values):
        return jnp.concatenate(halves(values.astype(f32)[None, :], 1), axis=0)

    gain = features(norm_gain)
    column = features(lax.dynamic_slice_in_dim(router, expert, 1, 1)[:, 0])
    shards, near = len(ups), len(ups) - 1
    front_shapes = [
        shape_of((slots, hidden), bf16),
        shape_of((slots, hidden), bf16),
        shape_of((hidden, slots), bf16),
    ]
    term_shapes = [shape_of((hidden, half), bf16)] * 2
    own_shapes = [shape_of((hidden, half), f32), shape_of((hidden, half), bf16)]
    normed, unit, scales, *near_fronts = staged_call(
        functools.partial(norm_step, near),
        [shape_of((slots, width), bf16)] * 2
        + [shape_of((2, slots, 128), f32)]
        + front_shapes * near,
        (slot_maps, token_rows, gain, column, *(p for pair in ups[:near] for p in pair)),
        32,
    )
    fronts = [near_fronts[3 * k : 3 * k + 3] for k in range(near)]
    fronts.append(staged_call(front_step, front_shapes, (normed,) + ups[near], 16))
    cotan_rows, across_turned = lax.optimization_barrier((cotan_rows, fronts[near][2]))
    cotan, output, *terms = staged_call(
        gate_step,
        [shape_of((slots, width), bf16)] * 2 + term_shapes * near,
        (slot_maps, cotan_rows, scales, fronts[1][2], fronts[2][2], across_turned),
        28,
    )
    logit_grad, router_halves, *preact_grads = staged_call(
        functools.partial(hidden_step, shards),
        [shape_of((slots, 128), f32), shape_of((2, half), f32)]
        + [shape_of((slots, hidden), bf16)] * shards,
        (output, scales, normed)
        + tuple(p for k in range(shards) for p in (*fronts[k][:2], *downs[k])),
        28,
    )

    def tower_sum(first, second):
        return first.astype(f32) + exchanged(second, "tower", 1).astype(f32)

    down_before, down_after, down_across = (
        tower_sum(*terms[2 * term : 2 * term + 2]).astype(bf16) for term in range(near)
    )
    router_column = jnp.where(
        tower == 0, router_halves, jnp.concatenate([router_halves[1:], router_halves[:1]])
    ).reshape(-1, 128)
    router_column = router_column + exchanged(router_column, "tower", 1)
    router_column, down_before, down_after, down_across = lax.optimization_barrier(
        (router_column, down_before, down_after, down_across)
    )
    near, far, farther = (exchanged(router_column, "y", bit) for bit in (1, 2, 3))
    router_column = (router_column + near) + (far + farther)
    down_before = shifted(down_before, "y", -1)
    down_after = shifted(down_after, "y", 1)
    down_across = shifted(down_across, "y", 2)
    logit_grad, router_column = lax.optimization_barrier((logit_grad, router_column))

    def collected(block, axis, bits):
        return jnp.concatenate([block] + [exchanged(block, axis, bit) for bit in bits])

    gathered = collected(router_column, "x", (1, 2, 3))
    back_rows = staged_call(
        functools.partial(back_step, shards),
        [shape_of((2 * slots, half), bf16)],
        tuple(p for k in range(shards) for p in (preact_grads[k], *ups[k]))
        + (logit_grad, unit, cotan, scales, row_maps, gain, column),
        32,
        2 * shards * slots * width * hidden,
        scratch=[pltpu.VMEM((slots, half), f32), pltpu.VMEM((slots, half), f32)],
    )[0]
    back_rows, gathered = lax.optimization_barrier((back_rows, gathered))
    returned = spread(back_rows)
    tokens_grad = staged_call(
        token_step, [shape_of((token_total, width), bf16)], (token_maps, returned), 12
    )[0]

    gathered = collected(collected(gathered, "z", (1, 2, 3)), "z", (4,))
    gathered = gathered.reshape(experts, width)
    embed_grads = pair_loss(embeds, logit_scale_log, pairwise_logit_bias, dp_index)
    down_before, down_after, down_across, embed_grads = lax.optimization_barrier(
        (down_before, down_after, down_across, embed_grads)
    )
    expert_ids_here = jnp.arange(experts, dtype=jnp.int32)
    order = (expert_ids_here ^ expert)[:, None] == expert_ids_here[None, :]
    router_grad = lax.dot_general(
        gathered,
        order.astype(f32),
        (((0,), (0,)), ((), ())),
        precision=lax.Precision.HIGHEST,
        preferred_element_type=f32,
    )

    own_terms = staged_call(down_step, own_shapes, (fronts[0][2], output), 16)
    down_half = (
        tower_sum(*own_terms)
        + down_before.astype(f32)
        + down_after.astype(f32)
        + down_across.astype(f32)
    )
    down_other = exchanged(down_half, "tower", 1)
    whole = pl.BlockSpec(memory_space=pltpu.VMEM)
    down_grad = local_call(
        joined_kernel,
        [shape_of((hidden, width), f32)],
        (tower_word, down_half, down_other),
        16,
        in_specs=[pl.BlockSpec(memory_space=pltpu.SMEM), whole, whole],
    )[0]
    return (tokens_grad, router_grad, down_grad, embed_grads[None])


def solution(mesh):
    towers, chips = mesh.devices.shape
    grid = Mesh(
        mesh.devices.reshape(towers, chips // (columns * line), columns, line),
        ("tower", "z", "x", "y"),
    )
    dp = ("z", "x", "y")
    rows = P(("tower",) + dp, None)
    placed = (
        rows,
        P(),
        P(),
        rows,
        P(None, dp),
        P(dp, None),
        rows,
        P("tower", dp, None),
        P(),
        P(),
    )
    return jax.shard_map(
        body,
        mesh=grid,
        in_specs=placed,
        out_specs=(rows, P(), P(dp, None), P("tower", dp, None)),
        check_vma=False,
    )
```

```python
import functools

import jax
import jax.numpy as jnp
from jax import lax
from jax.experimental import pallas as pl
from jax.experimental.pallas import tpu as pltpu
from jax.sharding import Mesh, PartitionSpec as P

epsilon = 1e-06
gelu_root = 0.7978845608028654
gelu_cubic = 0.044715

line = 4
columns = 4


def shifted(block, axis, step):
    count = lax.axis_size(axis)
    return lax.ppermute(block, axis, [(i, (i + step) % count) for i in range(count)])


def exchanged(block, axis, bit):
    count = lax.axis_size(axis)
    return lax.ppermute(block, axis, [(i, i ^ bit) for i in range(count)])


def product(left, right):
    return jnp.dot(left, right, preferred_element_type=jnp.float32)


def contract_rows(left, right):
    return lax.dot_general(
        left, right, (((0,), (0,)), ((), ())), preferred_element_type=jnp.float32
    )


def contracted_columns(left, right):
    return lax.dot_general(
        left, right, (((1,), (1,)), ((), ())), preferred_element_type=jnp.float32
    )


def gelu_pair(values):
    inner = gelu_root * (values + gelu_cubic * values * values * values)
    tangent = jnp.tanh(inner)
    slope = 0.5 * (1.0 + tangent) + 0.5 * values * (1.0 - tangent * tangent) * gelu_root * (
        1.0 + 3.0 * gelu_cubic * values * values
    )
    return 0.5 * values * (1.0 + tangent), slope


def local_call(kernel, out_shape, operands, vmem, flops=1, **options):
    return pl.pallas_call(
        kernel,
        out_shape=out_shape,
        compiler_params=pltpu.CompilerParams(vmem_limit_bytes=vmem << 20),
        cost_estimate=pl.CostEstimate(flops=flops, bytes_accessed=1, transcendentals=0),
        **options,
    )(*operands)


def shape_of(shape, dtype):
    return jax.ShapeDtypeStruct(shape, dtype)


def staged_call(run, out_shape, operands, vmem, flops=1, scalars=(), scratch=()):
    fixed, count, results = len(scalars), len(operands), len(out_shape)

    def kernel(*refs):
        numbers, refs = refs[:fixed], refs[fixed:]
        sources, refs = refs[:count], refs[count:]
        targets, refs = refs[:results], refs[results:]
        held, refs = refs[:count], refs[count:]
        out, refs = refs[:results], refs[results:]
        in_sems, out_sems, rest = refs[0], refs[1], refs[2:]
        fetched = [
            pltpu.make_async_copy(sources[i], held[i], in_sems.at[i]) for i in range(count)
        ]
        sent = [
            pltpu.make_async_copy(out[j], targets[j], out_sems.at[j]) for j in range(results)
        ]
        for copy in fetched:
            copy.start()
        arrived = set()

        def need(i):
            if i not in arrived:
                fetched[i].wait()
                arrived.add(i)
            return held[i]

        run(need, out, lambda j: sent[j].start(), *numbers, *rest)
        for copy in sent:
            copy.wait()

    apart = pl.BlockSpec(memory_space=pltpu.HBM)
    pinned = [pltpu.with_memory_space_constraint(v, pltpu.HBM) for v in operands]
    return local_call(
        kernel,
        [pltpu.HBM(v.shape, v.dtype) for v in out_shape],
        (*scalars, *pinned),
        vmem,
        flops,
        in_specs=[pl.BlockSpec(memory_space=pltpu.SMEM)] * fixed + [apart] * count,
        out_specs=[apart] * results,
        scratch_shapes=[pltpu.VMEM(v.shape, v.dtype) for v in operands]
        + [pltpu.VMEM(v.shape, v.dtype) for v in out_shape]
        + [pltpu.SemaphoreType.DMA((count,)), pltpu.SemaphoreType.DMA((results,))]
        + list(scratch),
    )


def slot_step(capacity, experts, return_rows, need, out, send, tower_ref):
    count, half = out[0].shape
    tower = tower_ref[0]
    choices = need(0)[...]
    total = choices.shape[0]
    onehot = choices == lax.broadcasted_iota(jnp.int32, (total, experts), 1)
    lower_tri = lax.broadcasted_iota(jnp.int32, (total, total), 0) >= lax.broadcasted_iota(
        jnp.int32, (total, total), 1
    )
    running = product(lower_tri.astype(jnp.bfloat16), onehot.astype(jnp.bfloat16))
    rank = jnp.sum(jnp.where(onehot, running, 0.0), axis=1, keepdims=True) - 1.0
    first_row = choices.astype(jnp.float32) * (2.0 * capacity) + rank
    first_row = jnp.broadcast_to(first_row, (total, 128)).T[0:1].astype(jnp.int32)
    low_row = first_row + capacity * tower
    high_row = first_row + capacity * (1 - tower)
    more = choices.astype(jnp.float32) * jnp.float32(return_rows - 2 * capacity)
    more = jnp.broadcast_to(more, (total, 128)).T[0:1].astype(jnp.int32)
    out[2][0:1] = low_row + more
    out[2][1:2] = high_row + more
    send(2)
    ids = lax.broadcasted_iota(jnp.int32, (count, total), 0)
    low_place = (ids == low_row).astype(jnp.bfloat16)
    high_place = (ids == high_row).astype(jnp.bfloat16)
    for k in range(2):
        values = need(1 + k)
        rows = product(low_place, values[:, :half]) + product(high_place, values[:, half:])
        out[k][...] = rows.astype(jnp.bfloat16)
        send(k)


def token_step(experts, column_row, need, out, send):
    rows_of = need(0)
    rows = need(1)[...]
    count, half = rows.shape
    total = out[0].shape[0]
    ids = lax.broadcasted_iota(jnp.int32, (count, total), 0)
    for part in range(2):
        place = (ids == rows_of[part : part + 1]).astype(jnp.float32).T.astype(jnp.bfloat16)
        out[0][:, part * half : (part + 1) * half] = product(place, rows).astype(jnp.bfloat16)
    send(0)
    words = rows.astype(jnp.float32).reshape(experts, count // experts, half)
    for part in range(2):
        sums = words[:, column_row + part, :] + words[:, column_row + 2 + part, :]
        out[1][part * half : (part + 1) * half, :] = sums.T
    send(1)


def taken(rows, slot_of_row, slots):
    ids = lax.broadcasted_iota(jnp.int32, (slots, rows.shape[0]), 0)
    return product((ids == slot_of_row).astype(jnp.bfloat16), rows)


def feature_mean(first, second, width):
    total = jnp.sum(first, axis=1, keepdims=True) + jnp.sum(second, axis=1, keepdims=True)
    return total / width


def spread_lanes(column):
    return jnp.broadcast_to(column, (column.shape[0], 128))


def front(normed, up_first, up_second, out, send, base):
    half = up_first.shape[0]
    preact = product(normed[:, :half], up_first[...]) + product(
        normed[:, half:], up_second[...]
    )
    gelu, slope = gelu_pair(preact)
    out[base][...] = slope.astype(jnp.bfloat16)
    send(base)
    out[base + 1][...] = gelu.astype(jnp.bfloat16)
    send(base + 1)
    out[base + 2][...] = gelu.T.astype(jnp.bfloat16)
    send(base + 2)


def norm_step(shards, need, out, send):
    slots, width = out[0].shape
    half = width // 2
    maps, rows = need(0), need(1)[...]
    first, second = (taken(rows, maps[part : part + 1], slots) for part in range(2))
    mean = feature_mean(first, second, width)
    first, second = first - mean, second - mean
    root = lax.rsqrt(feature_mean(first * first, second * second, width) + epsilon)
    first, second = first * root, second * root
    out[1][:, :half] = first.astype(jnp.bfloat16)
    out[1][:, half:] = second.astype(jnp.bfloat16)
    send(1)
    gain, column = need(2), need(3)
    first = (first * gain[0:1]).astype(jnp.bfloat16)
    second = (second * gain[1:2]).astype(jnp.bfloat16)
    out[0][:, :half] = first
    out[0][:, half:] = second
    send(0)
    logits = jnp.sum(first.astype(jnp.float32) * column[0:1], axis=1, keepdims=True) + jnp.sum(
        second.astype(jnp.float32) * column[1:2], axis=1, keepdims=True
    )
    out[2][0] = spread_lanes(root)
    out[2][1] = spread_lanes(jax.nn.sigmoid(logits))
    send(2)
    for shard in range(shards):
        front(out[0], need(4 + 2 * shard), need(5 + 2 * shard), out, send, 3 + 3 * shard)


def front_step(need, out, send):
    front(need(0), need(1), need(2), out, send, 0)


def gate_step(need, out, send):
    slots, width = out[0].shape
    half = width // 2
    maps, rows = need(0), need(1)[...]
    gates = need(2)[1][:, 0:1]
    for part in range(2):
        values = taken(rows, maps[part : part + 1], slots)
        out[0][:, part * half : (part + 1) * half] = values.astype(jnp.bfloat16)
        out[1][:, part * half : (part + 1) * half] = (gates * values).astype(jnp.bfloat16)
    send(0)
    send(1)
    for term in range((len(out) - 2) // 2):
        down_term(need(3 + term), out[1], out, send, 2 + 2 * term)


def down_term(turned, output, out, send, base):
    half = out[base].shape[1]
    out[base + 1][...] = product(turned[...], output[:, half:]).astype(jnp.bfloat16)
    send(base + 1)
    out[base][...] = product(turned[...], output[:, :half]).astype(out[base].dtype)
    send(base)


def down_step(need, out, send):
    down_term(need(0), need(1), out, send, 0)


def hidden_step(shards, need, out, send):
    output = need(0)
    half = output.shape[1] // 2
    gated = None
    for shard in range(shards):
        base = 3 + 4 * shard
        hidden_grad = contracted_columns(
            output[:, :half], need(base + 2)[...]
        ) + contracted_columns(output[:, half:], need(base + 3)[...])
        term = jnp.sum(
            need(base + 1)[...].astype(jnp.float32) * hidden_grad, axis=1, keepdims=True
        )
        gated = term if gated is None else gated + term
        out[2 + shard][...] = (hidden_grad * need(base)[...].astype(jnp.float32)).astype(jnp.bfloat16)
        send(2 + shard)
    logit_grad = gated * (1.0 - need(1)[1][:, 0:1])
    out[0][...] = spread_lanes(logit_grad)
    send(0)
    normed = need(2)
    for part in range(2):
        out[1][part : part + 1] = jnp.sum(
            normed[:, part * half : (part + 1) * half].astype(jnp.float32) * logit_grad,
            axis=0,
            keepdims=True,
        )
    send(1)


def back_step(shards, experts, need, out, send, first_sum, second_sum):
    count, half = out[0].shape
    width = 2 * half
    for shard in range(shards):
        grad = need(3 * shard)[...]
        first = contracted_columns(grad, need(3 * shard + 1)[...])
        second = contracted_columns(grad, need(3 * shard + 2)[...])
        if shard == 0:
            first_sum[...], second_sum[...] = first, second
        else:
            first_sum[...] += first
            second_sum[...] += second
    base = 3 * shards
    logit_grad = need(base)[:, 0:1]
    unit, cotan, root = need(base + 1), need(base + 2), need(base + 3)[0][:, 0:1]
    row_of_slot, gain, column = need(base + 4), need(base + 5), need(base + 6)
    first = (first_sum[...] + logit_grad * column[0:1]) * gain[0:1]
    second = (second_sum[...] + logit_grad * column[1:2]) * gain[1:2]
    unit_first = unit[:, :half].astype(jnp.float32)
    unit_second = unit[:, half:].astype(jnp.float32)
    grad_mean = feature_mean(first, second, width)
    grad_unit = feature_mean(first * unit_first, second * unit_second, width)
    first = cotan[:, :half].astype(jnp.float32) + root * (
        first - grad_mean - unit_first * grad_unit
    )
    second = cotan[:, half:].astype(jnp.float32) + root * (
        second - grad_mean - unit_second * grad_unit
    )
    ids = lax.broadcasted_iota(jnp.int32, (count, row_of_slot.shape[1]), 0)
    rows = product(
        (ids == row_of_slot[0:1]).astype(jnp.bfloat16), first.astype(jnp.bfloat16)
    ) + product((ids == row_of_slot[1:2]).astype(jnp.bfloat16), second.astype(jnp.bfloat16))
    words = need(base + 7)[...]
    high = words.astype(jnp.bfloat16)
    low = (words - high.astype(jnp.float32)).astype(jnp.bfloat16)
    tail = jnp.concatenate(
        [high.astype(jnp.float32), low.astype(jnp.float32), jnp.zeros((4, half), jnp.float32)]
    )
    per_expert = count // experts
    rows = jnp.concatenate(
        [
            rows.reshape(experts, per_expert, half)[:, : per_expert - 8],
            jnp.broadcast_to(tail[None], (experts, 8, half)),
        ],
        axis=1,
    )
    out[0][...] = rows.reshape(count, half).astype(jnp.bfloat16)
    send(0)


def joined_kernel(tower_ref, own_ref, other_ref, whole_ref):
    half = own_ref.shape[1]
    own_at = pl.multiple_of(tower_ref[0] * half, 128)
    other_at = pl.multiple_of((1 - tower_ref[0]) * half, 128)
    whole_ref[:, pl.ds(own_at, half)] = own_ref[...]
    whole_ref[:, pl.ds(other_at, half)] = other_ref[...]


def pair_rows(embeds):
    own_rows = embeds[0].astype(jnp.float32)
    local_member = (
        own_rows * lax.rsqrt(jnp.sum(own_rows * own_rows, axis=-1, keepdims=True) + epsilon)
    ).astype(jnp.bfloat16)
    other_unit = exchanged(local_member, "tower", 1)
    return local_member, lax.all_gather(other_unit, ("z", "x", "y"), axis=0, tiled=True)


def pair_grads(local_member, panel_rows, logit_scale_log, pairwise_logit_bias, dp_index):
    softness_factor = jnp.exp(logit_scale_log)
    row_count = local_member.shape[0]
    row_global = dp_index * row_count + jnp.arange(row_count, dtype=jnp.int32)
    pair_scores = (
        softness_factor * contracted_columns(local_member, panel_rows) + pairwise_logit_bias
    )
    col_global = jnp.arange(panel_rows.shape[0], dtype=jnp.int32)
    pair_labels = jnp.where(row_global[:, None] == col_global[None, :], 1.0, -1.0).astype(
        jnp.float32
    )
    panel_weights = (
        -pair_labels * jax.nn.sigmoid(-pair_labels * pair_scores) * softness_factor
    ).astype(jnp.bfloat16)
    return product(panel_weights, panel_rows)


def body(
    tokens,
    norm_gain,
    router,
    expert_ids,
    up_weights,
    down_weights,
    cotangent,
    embeds,
    logit_scale_log,
    pairwise_logit_bias,
):
    token_total, width = tokens.shape
    hidden = up_weights.shape[1]
    experts = router.shape[1]
    capacity = 3 * token_total // (2 * experts)
    half = width // 2
    slots = experts * capacity
    tower = lax.axis_index("tower")
    expert = lax.axis_index("z") * columns + lax.axis_index("x")
    dp_index = expert * line + lax.axis_index("y")
    bf16, f32 = jnp.bfloat16, jnp.float32

    def halves(values, axis):
        return (
            lax.dynamic_slice_in_dim(values, tower * half, half, axis),
            lax.dynamic_slice_in_dim(values, (1 - tower) * half, half, axis),
        )

    up_own, down_own = halves(up_weights, 0), halves(down_weights, 1)
    head = half // 10
    head_before = shifted(up_own[0][:head], "y", 1)
    head_after = shifted(up_own[0][:head], "y", -1)
    rest, head_before, head_after = lax.optimization_barrier(
        (up_own[0][head:], head_before, head_after)
    )
    rest_before, rest_after = shifted(rest, "y", 1), shifted(rest, "y", -1)
    down_part, rest_before, rest_after = lax.optimization_barrier(
        (down_own[0], rest_before, rest_after)
    )
    down_before = shifted(down_part, "y", 1)
    down_after = shifted(down_part, "y", -1)

    tower_word = tower.astype(jnp.int32).reshape(1)
    return_rows = 2 * capacity + 8
    sent_ids = jnp.arange(2 * slots, dtype=jnp.int32)
    slot_of_sent = sent_ids // (2 * capacity) * capacity + sent_ids % capacity
    in_first = sent_ids % (2 * capacity) < capacity
    slot_maps = jnp.stack(
        [jnp.where(in_first, slot_of_sent, -1), jnp.where(in_first, -1, slot_of_sent)]
    )
    slot_ids = jnp.arange(slots, dtype=jnp.int32)
    first_row = slot_ids // capacity * return_rows + slot_ids % capacity
    row_maps = jnp.stack([first_row, first_row + capacity])

    def spread(rows):
        return lax.all_to_all(
            rows.reshape(experts, -1, half),
            ("z", "x"),
            split_axis=0,
            concat_axis=0,
            tiled=True,
        ).reshape(-1, half)

    def both(piece):
        return piece, exchanged(piece, "tower", 1)

    tower_word, head_before, head_after = lax.optimization_barrier(
        (tower_word, head_before, head_after)
    )
    token_rows, cotan_rows, token_maps = staged_call(
        functools.partial(slot_step, capacity, experts, return_rows),
        [shape_of((2 * slots, half), bf16)] * 2 + [shape_of((2, token_total), jnp.int32)],
        (expert_ids, tokens, cotangent),
        16,
        scalars=(tower_word,),
    )
    token_rows = spread(token_rows)
    up_before = jnp.concatenate([head_before, rest_before])
    up_after = jnp.concatenate([head_after, rest_after])
    cotan_rows, token_rows, up_before, down_before, down_after = lax.optimization_barrier(
        (cotan_rows, token_rows, up_before, down_before, down_after)
    )
    cotan_rows = spread(cotan_rows)
    up_across = shifted(up_before, "y", 1)
    down_across = shifted(down_after, "y", -1)
    ups = [up_own] + [both(piece) for piece in (up_before, up_after, up_across)]
    downs = [down_own] + [both(piece) for piece in (down_before, down_after, down_across)]

    def features(values):
        return jnp.concatenate(halves(values.astype(f32)[None, :], 1), axis=0)

    gain = features(norm_gain)
    column = features(lax.dynamic_slice_in_dim(router, expert, 1, 1)[:, 0])
    shards, near = len(ups), len(ups) - 1
    front_shapes = [
        shape_of((slots, hidden), bf16),
        shape_of((slots, hidden), bf16),
        shape_of((hidden, slots), bf16),
    ]
    term_shapes = [shape_of((hidden, half), bf16)] * 2
    own_shapes = [shape_of((hidden, half), f32), shape_of((hidden, half), bf16)]
    normed, unit, scales, *near_fronts = staged_call(
        functools.partial(norm_step, near),
        [shape_of((slots, width), bf16)] * 2
        + [shape_of((2, slots, 128), f32)]
        + front_shapes * near,
        (slot_maps, token_rows, gain, column, *(p for pair in ups[:near] for p in pair)),
        32,
    )
    fronts = [near_fronts[3 * k : 3 * k + 3] for k in range(near)]
    fronts.append(staged_call(front_step, front_shapes, (normed,) + ups[near], 16))
    cotan_rows, across_turned = lax.optimization_barrier((cotan_rows, fronts[near][2]))
    cotan, output, *terms = staged_call(
        gate_step,
        [shape_of((slots, width), bf16)] * 2 + term_shapes * near,
        (slot_maps, cotan_rows, scales, fronts[1][2], fronts[2][2], across_turned),
        28,
    )
    logit_grad, router_halves, *preact_grads = staged_call(
        functools.partial(hidden_step, shards),
        [shape_of((slots, 128), f32), shape_of((2, half), f32)]
        + [shape_of((slots, hidden), bf16)] * shards,
        (output, scales, normed)
        + tuple(p for k in range(shards) for p in (*fronts[k][:2], *downs[k])),
        28,
    )

    def tower_sum(first, second):
        return first.astype(f32) + exchanged(second, "tower", 1).astype(f32)

    down_before, down_after, down_across = (
        tower_sum(*terms[2 * term : 2 * term + 2]).astype(bf16) for term in range(near)
    )
    router_column = jnp.where(
        tower == 0, router_halves, jnp.concatenate([router_halves[1:], router_halves[:1]])
    )
    router_column = router_column + exchanged(router_column, "tower", 1)
    near, far, farther = (exchanged(router_column, "y", bit) for bit in (1, 2, 3))
    router_column = (router_column + near) + (far + farther)
    router_column, down_before, down_after, down_across = lax.optimization_barrier(
        (router_column, down_before, down_after, down_across)
    )
    down_before = shifted(down_before, "y", -1)
    down_after = shifted(down_after, "y", 1)
    down_across = shifted(down_across, "y", 2)
    back_rows = staged_call(
        functools.partial(back_step, shards, experts),
        [shape_of((experts * return_rows, half), bf16)],
        tuple(p for k in range(shards) for p in (preact_grads[k], *ups[k]))
        + (logit_grad, unit, cotan, scales, row_maps, gain, column, router_column),
        32,
        16 * shards * slots * width * hidden,
        scratch=[pltpu.VMEM((slots, half), f32), pltpu.VMEM((slots, half), f32)],
    )[0]
    returned = spread(back_rows)
    tokens_grad, router_grad = staged_call(
        functools.partial(token_step, experts, 2 * capacity),
        [shape_of((token_total, width), bf16), shape_of((width, experts), f32)],
        (token_maps, returned),
        20,
    )

    local_member, panel_rows = pair_rows(embeds)
    panel_rows, output, down_before, down_after = lax.optimization_barrier(
        (panel_rows, output, down_before, down_after)
    )
    embed_grads = pair_grads(
        local_member, panel_rows, logit_scale_log, pairwise_logit_bias, dp_index
    )
    embed_grads, down_across = lax.optimization_barrier((embed_grads, down_across))
    own_terms = staged_call(down_step, own_shapes, (fronts[0][2], output), 16)
    down_half = (
        tower_sum(*own_terms)
        + down_before.astype(f32)
        + down_after.astype(f32)
        + down_across.astype(f32)
    )
    down_other = exchanged(down_half, "tower", 1)
    whole = pl.BlockSpec(memory_space=pltpu.VMEM)
    down_grad = local_call(
        joined_kernel,
        [shape_of((hidden, width), f32)],
        (tower_word, down_half, down_other),
        16,
        in_specs=[pl.BlockSpec(memory_space=pltpu.SMEM), whole, whole],
    )[0]
    return (tokens_grad, router_grad, down_grad, embed_grads[None])


def solution(mesh):
    towers, chips = mesh.devices.shape
    grid = Mesh(
        mesh.devices.reshape(towers, chips // (columns * line), columns, line),
        ("tower", "z", "x", "y"),
    )
    dp = ("z", "x", "y")
    rows = P(("tower",) + dp, None)
    placed = (
        rows,
        P(),
        P(),
        rows,
        P(None, dp),
        P(dp, None),
        rows,
        P("tower", dp, None),
        P(),
        P(),
    )
    return jax.shard_map(
        body,
        mesh=grid,
        in_specs=placed,
        out_specs=(rows, P(), P(dp, None), P("tower", dp, None)),
        check_vma=False,
    )
```

```python
import functools

import jax
import jax.numpy as jnp
from jax import lax
from jax.experimental import pallas as pl
from jax.experimental.pallas import tpu as pltpu
from jax.sharding import Mesh, PartitionSpec as P

epsilon = 1e-06
gelu_root = 0.7978845608028654
gelu_cubic = 0.044715

line = 4
columns = 4


def shifted(block, axis, step):
    count = lax.axis_size(axis)
    return lax.ppermute(block, axis, [(i, (i + step) % count) for i in range(count)])


def exchanged(block, axis, bit):
    count = lax.axis_size(axis)
    return lax.ppermute(block, axis, [(i, i ^ bit) for i in range(count)])


def product(left, right):
    return jnp.dot(left, right, preferred_element_type=jnp.float32)


def contract_rows(left, right):
    return lax.dot_general(
        left, right, (((0,), (0,)), ((), ())), preferred_element_type=jnp.float32
    )


def contracted_columns(left, right):
    return lax.dot_general(
        left, right, (((1,), (1,)), ((), ())), preferred_element_type=jnp.float32
    )


def gelu_pair(values):
    inner = gelu_root * (values + gelu_cubic * values * values * values)
    tangent = jnp.tanh(inner)
    slope = 0.5 * (1.0 + tangent) + 0.5 * values * (1.0 - tangent * tangent) * gelu_root * (
        1.0 + 3.0 * gelu_cubic * values * values
    )
    return 0.5 * values * (1.0 + tangent), slope


def local_call(kernel, out_shape, operands, vmem, flops=1, **options):
    return pl.pallas_call(
        kernel,
        out_shape=out_shape,
        compiler_params=pltpu.CompilerParams(vmem_limit_bytes=vmem << 20),
        cost_estimate=pl.CostEstimate(flops=flops, bytes_accessed=1, transcendentals=0),
        **options,
    )(*operands)


def shape_of(shape, dtype):
    return jax.ShapeDtypeStruct(shape, dtype)


def staged_call(run, out_shape, operands, vmem, flops=1, scalars=(), scratch=()):
    fixed, count, results = len(scalars), len(operands), len(out_shape)

    def kernel(*refs):
        numbers, refs = refs[:fixed], refs[fixed:]
        sources, refs = refs[:count], refs[count:]
        targets, refs = refs[:results], refs[results:]
        held, refs = refs[:count], refs[count:]
        out, refs = refs[:results], refs[results:]
        in_sems, out_sems, rest = refs[0], refs[1], refs[2:]
        fetched = [
            pltpu.make_async_copy(sources[i], held[i], in_sems.at[i]) for i in range(count)
        ]
        sent = [
            pltpu.make_async_copy(out[j], targets[j], out_sems.at[j]) for j in range(results)
        ]
        for copy in fetched:
            copy.start()
        arrived = set()

        def need(i):
            if i not in arrived:
                fetched[i].wait()
                arrived.add(i)
            return held[i]

        run(need, out, lambda j: sent[j].start(), *numbers, *rest)
        for copy in sent:
            copy.wait()

    apart = pl.BlockSpec(memory_space=pltpu.HBM)
    pinned = [pltpu.with_memory_space_constraint(v, pltpu.HBM) for v in operands]
    return local_call(
        kernel,
        [pltpu.HBM(v.shape, v.dtype) for v in out_shape],
        (*scalars, *pinned),
        vmem,
        flops,
        in_specs=[pl.BlockSpec(memory_space=pltpu.SMEM)] * fixed + [apart] * count,
        out_specs=[apart] * results,
        scratch_shapes=[pltpu.VMEM(v.shape, v.dtype) for v in operands]
        + [pltpu.VMEM(v.shape, v.dtype) for v in out_shape]
        + [pltpu.SemaphoreType.DMA((count,)), pltpu.SemaphoreType.DMA((results,))]
        + list(scratch),
    )


def slot_step(capacity, experts, return_rows, need, out, send, tower_ref):
    count, half = out[0].shape
    tower = tower_ref[0]
    choices = need(0)[...]
    total = choices.shape[0]
    onehot = choices == lax.broadcasted_iota(jnp.int32, (total, experts), 1)
    lower_tri = lax.broadcasted_iota(jnp.int32, (total, total), 0) >= lax.broadcasted_iota(
        jnp.int32, (total, total), 1
    )
    running = product(lower_tri.astype(jnp.bfloat16), onehot.astype(jnp.bfloat16))
    rank = jnp.sum(jnp.where(onehot, running, 0.0), axis=1, keepdims=True) - 1.0
    first_row = choices.astype(jnp.float32) * (2.0 * capacity) + rank
    first_row = jnp.broadcast_to(first_row, (total, 128)).T[0:1].astype(jnp.int32)
    low_row = first_row + capacity * tower
    high_row = first_row + capacity * (1 - tower)
    more = choices.astype(jnp.float32) * jnp.float32(return_rows - 2 * capacity)
    more = jnp.broadcast_to(more, (total, 128)).T[0:1].astype(jnp.int32)
    out[2][0:1] = low_row + more
    out[2][1:2] = high_row + more
    send(2)
    ids = lax.broadcasted_iota(jnp.int32, (count, total), 0)
    low_place = (ids == low_row).astype(jnp.bfloat16)
    high_place = (ids == high_row).astype(jnp.bfloat16)
    for k in range(2):
        values = need(1 + k)
        rows = product(low_place, values[:, :half]) + product(high_place, values[:, half:])
        out[k][...] = rows.astype(jnp.bfloat16)
        send(k)


def token_step(experts, column_row, need, out, send):
    rows_of = need(0)
    rows = need(1)[...]
    count, half = rows.shape
    total = out[0].shape[0]
    ids = lax.broadcasted_iota(jnp.int32, (count, total), 0)
    for part in range(2):
        place = (ids == rows_of[part : part + 1]).astype(jnp.float32).T.astype(jnp.bfloat16)
        out[0][:, part * half : (part + 1) * half] = product(place, rows).astype(jnp.bfloat16)
    send(0)
    words = rows.astype(jnp.float32).reshape(experts, count // experts, half)
    for part in range(2):
        sums = words[:, column_row + part, :] + words[:, column_row + 2 + part, :]
        out[1][part * half : (part + 1) * half, :] = sums.T
    send(1)


def taken(rows, slot_of_row, slots):
    ids = lax.broadcasted_iota(jnp.int32, (slots, rows.shape[0]), 0)
    return product((ids == slot_of_row).astype(jnp.bfloat16), rows)


def feature_mean(first, second, width):
    total = jnp.sum(first, axis=1, keepdims=True) + jnp.sum(second, axis=1, keepdims=True)
    return total / width


def spread_lanes(column):
    return jnp.broadcast_to(column, (column.shape[0], 128))


def front(normed, up_first, up_second, out, send, base):
    half = up_first.shape[0]
    preact = product(normed[:, :half], up_first[...]) + product(
        normed[:, half:], up_second[...]
    )
    gelu, slope = gelu_pair(preact)
    out[base][...] = slope.astype(jnp.bfloat16)
    send(base)
    out[base + 1][...] = gelu.astype(jnp.bfloat16)
    send(base + 1)
    out[base + 2][...] = gelu.T.astype(jnp.bfloat16)
    send(base + 2)


def norm_step(shards, need, out, send):
    slots, width = out[0].shape
    half = width // 2
    maps, rows = need(0), need(1)[...]
    first, second = (taken(rows, maps[part : part + 1], slots) for part in range(2))
    mean = feature_mean(first, second, width)
    first, second = first - mean, second - mean
    root = lax.rsqrt(feature_mean(first * first, second * second, width) + epsilon)
    first, second = first * root, second * root
    out[1][:, :half] = first.astype(jnp.bfloat16)
    out[1][:, half:] = second.astype(jnp.bfloat16)
    send(1)
    gain, column = need(2), need(3)
    first = (first * gain[0:1]).astype(jnp.bfloat16)
    second = (second * gain[1:2]).astype(jnp.bfloat16)
    out[0][:, :half] = first
    out[0][:, half:] = second
    send(0)
    logits = jnp.sum(first.astype(jnp.float32) * column[0:1], axis=1, keepdims=True) + jnp.sum(
        second.astype(jnp.float32) * column[1:2], axis=1, keepdims=True
    )
    out[2][0] = spread_lanes(root)
    out[2][1] = spread_lanes(jax.nn.sigmoid(logits))
    send(2)
    for shard in range(shards):
        front(out[0], need(4 + 2 * shard), need(5 + 2 * shard), out, send, 3 + 3 * shard)


def front_step(need, out, send):
    front(need(0), need(1), need(2), out, send, 0)


def gate_step(need, out, send):
    slots, width = out[0].shape
    half = width // 2
    maps, rows = need(0), need(1)[...]
    gates = need(2)[1][:, 0:1]
    for part in range(2):
        values = taken(rows, maps[part : part + 1], slots)
        out[0][:, part * half : (part + 1) * half] = values.astype(jnp.bfloat16)
        out[1][:, part * half : (part + 1) * half] = (gates * values).astype(jnp.bfloat16)
    send(0)
    send(1)
    for term in range((len(out) - 2) // 2):
        down_term(need(3 + term), out[1], out, send, 2 + 2 * term)


def down_term(turned, output, out, send, base):
    half = out[base].shape[1]
    out[base + 1][...] = product(turned[...], output[:, half:]).astype(jnp.bfloat16)
    send(base + 1)
    out[base][...] = product(turned[...], output[:, :half]).astype(out[base].dtype)
    send(base)


def hidden_step(shards, need, out, send):
    output = need(0)
    half = output.shape[1] // 2
    gated = None
    for shard in range(shards):
        base = 3 + 4 * shard
        hidden_grad = contracted_columns(
            output[:, :half], need(base + 2)[...]
        ) + contracted_columns(output[:, half:], need(base + 3)[...])
        term = jnp.sum(
            need(base + 1)[...].astype(jnp.float32) * hidden_grad, axis=1, keepdims=True
        )
        gated = term if gated is None else gated + term
        out[2 + shard][...] = (hidden_grad * need(base)[...].astype(jnp.float32)).astype(jnp.bfloat16)
        send(2 + shard)
    logit_grad = gated * (1.0 - need(1)[1][:, 0:1])
    out[0][...] = spread_lanes(logit_grad)
    send(0)
    normed = need(2)
    for part in range(2):
        out[1][part : part + 1] = jnp.sum(
            normed[:, part * half : (part + 1) * half].astype(jnp.float32) * logit_grad,
            axis=0,
            keepdims=True,
        )
    send(1)


def back_step(shards, experts, need, out, send, first_sum, second_sum):
    count, half = out[0].shape
    width = 2 * half
    for shard in range(shards):
        grad = need(3 * shard)[...]
        first = contracted_columns(grad, need(3 * shard + 1)[...])
        second = contracted_columns(grad, need(3 * shard + 2)[...])
        if shard == 0:
            first_sum[...], second_sum[...] = first, second
        else:
            first_sum[...] += first
            second_sum[...] += second
    base = 3 * shards
    logit_grad = need(base)[:, 0:1]
    unit, cotan, root = need(base + 1), need(base + 2), need(base + 3)[0][:, 0:1]
    row_of_slot, gain, column = need(base + 4), need(base + 5), need(base + 6)
    first = (first_sum[...] + logit_grad * column[0:1]) * gain[0:1]
    second = (second_sum[...] + logit_grad * column[1:2]) * gain[1:2]
    unit_first = unit[:, :half].astype(jnp.float32)
    unit_second = unit[:, half:].astype(jnp.float32)
    grad_mean = feature_mean(first, second, width)
    grad_unit = feature_mean(first * unit_first, second * unit_second, width)
    first = cotan[:, :half].astype(jnp.float32) + root * (
        first - grad_mean - unit_first * grad_unit
    )
    second = cotan[:, half:].astype(jnp.float32) + root * (
        second - grad_mean - unit_second * grad_unit
    )
    ids = lax.broadcasted_iota(jnp.int32, (count, row_of_slot.shape[1]), 0)
    rows = product(
        (ids == row_of_slot[0:1]).astype(jnp.bfloat16), first.astype(jnp.bfloat16)
    ) + product((ids == row_of_slot[1:2]).astype(jnp.bfloat16), second.astype(jnp.bfloat16))
    words = need(base + 7)[...]
    high = words.astype(jnp.bfloat16)
    low = (words - high.astype(jnp.float32)).astype(jnp.bfloat16)
    tail = jnp.concatenate(
        [high.astype(jnp.float32), low.astype(jnp.float32), jnp.zeros((4, half), jnp.float32)]
    )
    per_expert = count // experts
    rows = jnp.concatenate(
        [
            rows.reshape(experts, per_expert, half)[:, : per_expert - 8],
            jnp.broadcast_to(tail[None], (experts, 8, half)),
        ],
        axis=1,
    )
    out[0][...] = rows.reshape(count, half).astype(jnp.bfloat16)
    send(0)


def joined_kernel(tower_ref, own_ref, other_ref, whole_ref):
    half = own_ref.shape[1]
    own_at = pl.multiple_of(tower_ref[0] * half, 128)
    other_at = pl.multiple_of((1 - tower_ref[0]) * half, 128)
    whole_ref[:, pl.ds(own_at, half)] = own_ref[...]
    whole_ref[:, pl.ds(other_at, half)] = other_ref[...]


def pair_rows(embeds):
    own_rows = embeds[0].astype(jnp.float32)
    local_member = (
        own_rows * lax.rsqrt(jnp.sum(own_rows * own_rows, axis=-1, keepdims=True) + epsilon)
    ).astype(jnp.bfloat16)
    other_unit = exchanged(local_member, "tower", 1)
    return local_member, lax.all_gather(other_unit, ("z", "x", "y"), axis=0, tiled=True)


def pair_grads(local_member, panel_rows, logit_scale_log, pairwise_logit_bias, dp_index):
    softness_factor = jnp.exp(logit_scale_log)
    row_count = local_member.shape[0]
    row_global = dp_index * row_count + jnp.arange(row_count, dtype=jnp.int32)
    pair_scores = (
        softness_factor * contracted_columns(local_member, panel_rows) + pairwise_logit_bias
    )
    col_global = jnp.arange(panel_rows.shape[0], dtype=jnp.int32)
    pair_labels = jnp.where(row_global[:, None] == col_global[None, :], 1.0, -1.0).astype(
        jnp.float32
    )
    panel_weights = (
        -pair_labels * jax.nn.sigmoid(-pair_labels * pair_scores) * softness_factor
    ).astype(jnp.bfloat16)
    return product(panel_weights, panel_rows)


def body(
    tokens,
    norm_gain,
    router,
    expert_ids,
    up_weights,
    down_weights,
    cotangent,
    embeds,
    logit_scale_log,
    pairwise_logit_bias,
):
    token_total, width = tokens.shape
    hidden = up_weights.shape[1]
    experts = router.shape[1]
    capacity = 3 * token_total // (2 * experts)
    half = width // 2
    slots = experts * capacity
    tower = lax.axis_index("tower")
    expert = lax.axis_index("z") * columns + lax.axis_index("x")
    dp_index = expert * line + lax.axis_index("y")
    bf16, f32 = jnp.bfloat16, jnp.float32

    def halves(values, axis):
        return (
            lax.dynamic_slice_in_dim(values, tower * half, half, axis),
            lax.dynamic_slice_in_dim(values, (1 - tower) * half, half, axis),
        )

    up_own, down_own = halves(up_weights, 0), halves(down_weights, 1)
    up_before, up_after = shifted(up_own[0], "y", 1), shifted(up_own[0], "y", -1)
    down_part, up_before, up_after = lax.optimization_barrier((down_own[0], up_before, up_after))
    down_before, down_after = shifted(down_part, "y", 1), shifted(down_part, "y", -1)
    up_before, down_before, down_after = lax.optimization_barrier(
        (up_before, down_before, down_after)
    )
    up_across, down_across = shifted(up_before, "y", 1), shifted(down_after, "y", -1)

    tower_word = tower.astype(jnp.int32).reshape(1)
    return_rows = 2 * capacity + 8
    sent_ids = jnp.arange(2 * slots, dtype=jnp.int32)
    slot_of_sent = sent_ids // (2 * capacity) * capacity + sent_ids % capacity
    in_first = sent_ids % (2 * capacity) < capacity
    slot_maps = jnp.stack(
        [jnp.where(in_first, slot_of_sent, -1), jnp.where(in_first, -1, slot_of_sent)]
    )
    slot_ids = jnp.arange(slots, dtype=jnp.int32)
    first_row = slot_ids // capacity * return_rows + slot_ids % capacity
    row_maps = jnp.stack([first_row, first_row + capacity])

    def spread(rows):
        return lax.all_to_all(
            rows.reshape(experts, -1, half),
            ("z", "x"),
            split_axis=0,
            concat_axis=0,
            tiled=True,
        ).reshape(-1, half)

    def both(piece):
        return piece, exchanged(piece, "tower", 1)

    token_rows, cotan_rows, token_maps = staged_call(
        functools.partial(slot_step, capacity, experts, return_rows),
        [shape_of((2 * slots, half), bf16)] * 2 + [shape_of((2, token_total), jnp.int32)],
        (expert_ids, tokens, cotangent),
        16,
        scalars=(tower_word,),
    )
    token_rows = spread(token_rows)
    cotan_rows, token_rows = lax.optimization_barrier((cotan_rows, token_rows))
    cotan_rows = spread(cotan_rows)
    ups = [up_own] + [both(piece) for piece in (up_before, up_after, up_across)]
    downs = [down_own] + [both(piece) for piece in (down_before, down_after, down_across)]

    def features(values):
        return jnp.concatenate(halves(values.astype(f32)[None, :], 1), axis=0)

    gain = features(norm_gain)
    column = features(lax.dynamic_slice_in_dim(router, expert, 1, 1)[:, 0])
    shards, near = len(ups), len(ups) - 1
    front_shapes = [
        shape_of((slots, hidden), bf16),
        shape_of((slots, hidden), bf16),
        shape_of((hidden, slots), bf16),
    ]
    term_shapes = [shape_of((hidden, half), bf16)] * 2
    own_shapes = [shape_of((hidden, half), f32), shape_of((hidden, half), bf16)]
    token_rows, _, _ = lax.optimization_barrier((token_rows, down_before, down_after))
    normed, unit, scales, *near_fronts = staged_call(
        functools.partial(norm_step, near),
        [shape_of((slots, width), bf16)] * 2
        + [shape_of((2, slots, 128), f32)]
        + front_shapes * near,
        (slot_maps, token_rows, gain, column, *(p for pair in ups[:near] for p in pair)),
        32,
        1 << 35,
    )
    fronts = [near_fronts[3 * k : 3 * k + 3] for k in range(near)]
    fronts.append(staged_call(front_step, front_shapes, (normed,) + ups[near], 16))
    cotan_rows, across_turned = lax.optimization_barrier((cotan_rows, fronts[near][2]))
    cotan, output, *terms = staged_call(
        gate_step,
        [shape_of((slots, width), bf16)] * 2 + term_shapes * near + own_shapes,
        (slot_maps, cotan_rows, scales, fronts[1][2], fronts[2][2], across_turned, fronts[0][2]),
        32,
    )
    logit_grad, router_halves, *preact_grads = staged_call(
        functools.partial(hidden_step, shards),
        [shape_of((slots, 128), f32), shape_of((2, half), f32)]
        + [shape_of((slots, hidden), bf16)] * shards,
        (output, scales, normed)
        + tuple(p for k in range(shards) for p in (*fronts[k][:2], *downs[k])),
        28,
    )

    def tower_sum(first, second):
        return first.astype(f32) + exchanged(second, "tower", 1).astype(f32)

    down_before, down_after, down_across = (
        tower_sum(*terms[2 * term : 2 * term + 2]).astype(bf16) for term in range(near)
    )
    router_column = jnp.where(
        tower == 0, router_halves, jnp.concatenate([router_halves[1:], router_halves[:1]])
    )
    router_column = router_column + exchanged(router_column, "tower", 1)
    beside, beyond, farthest = (exchanged(router_column, "y", bit) for bit in (1, 2, 3))
    router_column = (router_column + beside) + (beyond + farthest)
    router_column, down_before, down_after, down_across = lax.optimization_barrier(
        (router_column, down_before, down_after, down_across)
    )
    down_before = shifted(down_before, "y", -1)
    down_after = shifted(down_after, "y", 1)
    down_across = shifted(down_across, "y", 2)
    back_rows = staged_call(
        functools.partial(back_step, shards, experts),
        [shape_of((experts * return_rows, half), bf16)],
        tuple(p for k in range(shards) for p in (preact_grads[k], *ups[k]))
        + (logit_grad, unit, cotan, scales, row_maps, gain, column, router_column),
        32,
        16 * shards * slots * width * hidden,
        scratch=[pltpu.VMEM((slots, half), f32), pltpu.VMEM((slots, half), f32)],
    )[0]
    returned = spread(back_rows)
    local_member, panel_rows = pair_rows(embeds)
    panel_rows, down_before = lax.optimization_barrier((panel_rows, down_before))
    embed_grads = pair_grads(
        local_member, panel_rows, logit_scale_log, pairwise_logit_bias, dp_index
    )
    embed_grads, token_maps = lax.optimization_barrier((embed_grads, token_maps))
    tokens_grad, router_grad = staged_call(
        functools.partial(token_step, experts, 2 * capacity),
        [shape_of((token_total, width), bf16), shape_of((width, experts), f32)],
        (token_maps, returned),
        20,
    )

    down_half = (
        tower_sum(*terms[2 * near :])
        + down_before.astype(f32)
        + down_after.astype(f32)
        + down_across.astype(f32)
    )
    down_other = exchanged(down_half, "tower", 1)
    whole = pl.BlockSpec(memory_space=pltpu.VMEM)
    down_grad = local_call(
        joined_kernel,
        [shape_of((hidden, width), f32)],
        (tower_word, down_half, down_other),
        16,
        in_specs=[pl.BlockSpec(memory_space=pltpu.SMEM), whole, whole],
    )[0]
    return (tokens_grad, router_grad, down_grad, embed_grads[None])


def solution(mesh):
    towers, chips = mesh.devices.shape
    grid = Mesh(
        mesh.devices.reshape(towers, chips // (columns * line), columns, line),
        ("tower", "z", "x", "y"),
    )
    dp = ("z", "x", "y")
    rows = P(("tower",) + dp, None)
    placed = (
        rows,
        P(),
        P(),
        rows,
        P(None, dp),
        P(dp, None),
        rows,
        P("tower", dp, None),
        P(),
        P(),
    )
    return jax.shard_map(
        body,
        mesh=grid,
        in_specs=placed,
        out_specs=(rows, P(), P(dp, None), P("tower", dp, None)),
        check_vma=False,
    )
```

```python
import functools

import jax
import jax.numpy as jnp
from jax import lax
from jax.experimental import pallas as pl
from jax.experimental.pallas import tpu as pltpu
from jax.sharding import Mesh, PartitionSpec as P

epsilon = 1e-06
gelu_root = 0.7978845608028654
gelu_cubic = 0.044715

line = 4
columns = 4


def shifted(block, axis, step):
    count = lax.axis_size(axis)
    return lax.ppermute(block, axis, [(i, (i + step) % count) for i in range(count)])


def exchanged(block, axis, bit):
    count = lax.axis_size(axis)
    return lax.ppermute(block, axis, [(i, i ^ bit) for i in range(count)])


def product(left, right):
    return jnp.dot(left, right, preferred_element_type=jnp.float32)


def contract_rows(left, right):
    return lax.dot_general(
        left, right, (((0,), (0,)), ((), ())), preferred_element_type=jnp.float32
    )


def contracted_columns(left, right):
    return lax.dot_general(
        left, right, (((1,), (1,)), ((), ())), preferred_element_type=jnp.float32
    )


def gelu_pair(values):
    inner = gelu_root * (values + gelu_cubic * values * values * values)
    tangent = jnp.tanh(inner)
    slope = 0.5 * (1.0 + tangent) + 0.5 * values * (1.0 - tangent * tangent) * gelu_root * (
        1.0 + 3.0 * gelu_cubic * values * values
    )
    return 0.5 * values * (1.0 + tangent), slope


def local_call(kernel, out_shape, operands, vmem, flops=1, **options):
    return pl.pallas_call(
        kernel,
        out_shape=out_shape,
        compiler_params=pltpu.CompilerParams(vmem_limit_bytes=vmem << 20),
        cost_estimate=pl.CostEstimate(flops=flops, bytes_accessed=1, transcendentals=0),
        **options,
    )(*operands)


def shape_of(shape, dtype):
    return jax.ShapeDtypeStruct(shape, dtype)


def staged_call(run, out_shape, operands, vmem, flops=1, scalars=(), scratch=()):
    fixed, count, results = len(scalars), len(operands), len(out_shape)

    def kernel(*refs):
        numbers, refs = refs[:fixed], refs[fixed:]
        sources, refs = refs[:count], refs[count:]
        targets, refs = refs[:results], refs[results:]
        held, refs = refs[:count], refs[count:]
        out, refs = refs[:results], refs[results:]
        in_sems, out_sems, rest = refs[0], refs[1], refs[2:]
        fetched = [
            pltpu.make_async_copy(sources[i], held[i], in_sems.at[i]) for i in range(count)
        ]
        sent = [
            pltpu.make_async_copy(out[j], targets[j], out_sems.at[j]) for j in range(results)
        ]
        for copy in fetched:
            copy.start()
        arrived = set()

        def need(i):
            if i not in arrived:
                fetched[i].wait()
                arrived.add(i)
            return held[i]

        run(need, out, lambda j: sent[j].start(), *numbers, *rest)
        for copy in sent:
            copy.wait()

    apart = pl.BlockSpec(memory_space=pltpu.HBM)
    pinned = [pltpu.with_memory_space_constraint(v, pltpu.HBM) for v in operands]
    return local_call(
        kernel,
        [pltpu.HBM(v.shape, v.dtype) for v in out_shape],
        (*scalars, *pinned),
        vmem,
        flops,
        in_specs=[pl.BlockSpec(memory_space=pltpu.SMEM)] * fixed + [apart] * count,
        out_specs=[apart] * results,
        scratch_shapes=[pltpu.VMEM(v.shape, v.dtype) for v in operands]
        + [pltpu.VMEM(v.shape, v.dtype) for v in out_shape]
        + [pltpu.SemaphoreType.DMA((count,)), pltpu.SemaphoreType.DMA((results,))]
        + list(scratch),
    )


def slot_step(capacity, experts, return_rows, need, out, send, tower_ref):
    count, half = out[0].shape
    tower = tower_ref[0]
    choices = need(0)[...]
    total = choices.shape[0]
    onehot = choices == lax.broadcasted_iota(jnp.int32, (total, experts), 1)
    lower_tri = lax.broadcasted_iota(jnp.int32, (total, total), 0) >= lax.broadcasted_iota(
        jnp.int32, (total, total), 1
    )
    running = product(lower_tri.astype(jnp.bfloat16), onehot.astype(jnp.bfloat16))
    rank = jnp.sum(jnp.where(onehot, running, 0.0), axis=1, keepdims=True) - 1.0
    first_row = choices.astype(jnp.float32) * (2.0 * capacity) + rank
    first_row = jnp.broadcast_to(first_row, (total, 128)).T[0:1].astype(jnp.int32)
    low_row = first_row + capacity * tower
    high_row = first_row + capacity * (1 - tower)
    more = choices.astype(jnp.float32) * jnp.float32(return_rows - 2 * capacity)
    more = jnp.broadcast_to(more, (total, 128)).T[0:1].astype(jnp.int32)
    out[2][0:1] = low_row + more
    out[2][1:2] = high_row + more
    send(2)
    ids = lax.broadcasted_iota(jnp.int32, (count, total), 0)
    low_place = (ids == low_row).astype(jnp.bfloat16)
    high_place = (ids == high_row).astype(jnp.bfloat16)
    for k in range(2):
        values = need(1 + k)
        rows = product(low_place, values[:, :half]) + product(high_place, values[:, half:])
        out[k][...] = rows.astype(jnp.bfloat16)
        send(k)


def token_step(experts, column_row, need, out, send):
    rows_of = need(0)
    rows = need(1)[...]
    count, half = rows.shape
    total = out[0].shape[0]
    ids = lax.broadcasted_iota(jnp.int32, (count, total), 0)
    for part in range(2):
        place = (ids == rows_of[part : part + 1]).astype(jnp.float32).T.astype(jnp.bfloat16)
        out[0][:, part * half : (part + 1) * half] = product(place, rows).astype(jnp.bfloat16)
    send(0)
    words = rows.astype(jnp.float32).reshape(experts, count // experts, half)
    for part in range(2):
        sums = words[:, column_row + part, :] + words[:, column_row + 2 + part, :]
        out[1][:, part * half : (part + 1) * half] = sums
    send(1)


def taken(rows, slot_of_row, slots):
    ids = lax.broadcasted_iota(jnp.int32, (slots, rows.shape[0]), 0)
    return product((ids == slot_of_row).astype(jnp.bfloat16), rows)


def feature_mean(first, second, width):
    total = jnp.sum(first, axis=1, keepdims=True) + jnp.sum(second, axis=1, keepdims=True)
    return total / width


def spread_lanes(column):
    return jnp.broadcast_to(column, (column.shape[0], 128))


def front(normed, up_first, up_second, out, send, base):
    half = up_first.shape[0]
    preact = product(normed[:, :half], up_first[...]) + product(
        normed[:, half:], up_second[...]
    )
    gelu, slope = gelu_pair(preact)
    out[base][...] = slope.astype(jnp.bfloat16)
    send(base)
    out[base + 1][...] = gelu.astype(jnp.bfloat16)
    send(base + 1)
    out[base + 2][...] = gelu.T.astype(jnp.bfloat16)
    send(base + 2)


def norm_step(shards, need, out, send):
    slots, width = out[0].shape
    half = width // 2
    maps, rows = need(0), need(1)[...]
    first, second = (taken(rows, maps[part : part + 1], slots) for part in range(2))
    mean = feature_mean(first, second, width)
    first, second = first - mean, second - mean
    root = lax.rsqrt(feature_mean(first * first, second * second, width) + epsilon)
    first, second = first * root, second * root
    out[1][:, :half] = first.astype(jnp.bfloat16)
    out[1][:, half:] = second.astype(jnp.bfloat16)
    send(1)
    gain, column = need(2), need(3)
    first = (first * gain[0:1]).astype(jnp.bfloat16)
    second = (second * gain[1:2]).astype(jnp.bfloat16)
    out[0][:, :half] = first
    out[0][:, half:] = second
    send(0)
    logits = jnp.sum(first.astype(jnp.float32) * column[0:1], axis=1, keepdims=True) + jnp.sum(
        second.astype(jnp.float32) * column[1:2], axis=1, keepdims=True
    )
    out[2][0] = spread_lanes(root)
    out[2][1] = spread_lanes(jax.nn.sigmoid(logits))
    send(2)
    for shard in range(shards):
        front(out[0], need(4 + 2 * shard), need(5 + 2 * shard), out, send, 3 + 3 * shard)


def front_step(need, out, send):
    front(need(0), need(1), need(2), out, send, 0)


def gate_step(need, out, send):
    slots, width = out[0].shape
    half = width // 2
    maps, rows = need(0), need(1)[...]
    gates = need(2)[1][:, 0:1]
    for part in range(2):
        values = taken(rows, maps[part : part + 1], slots)
        out[0][:, part * half : (part + 1) * half] = values.astype(jnp.bfloat16)
        out[1][:, part * half : (part + 1) * half] = (gates * values).astype(jnp.bfloat16)
    send(0)
    send(1)
    for term in range((len(out) - 2) // 2):
        down_term(need(3 + term), out[1], out, send, 2 + 2 * term)


def down_term(turned, output, out, send, base):
    half = out[base].shape[1]
    out[base + 1][...] = product(turned[...], output[:, half:]).astype(jnp.bfloat16)
    send(base + 1)
    out[base][...] = product(turned[...], output[:, :half]).astype(out[base].dtype)
    send(base)


def hidden_step(shards, need, out, send):
    output = need(0)
    half = output.shape[1] // 2
    gated = None
    for shard in range(shards):
        base = 3 + 4 * shard
        hidden_grad = contracted_columns(
            output[:, :half], need(base + 2)[...]
        ) + contracted_columns(output[:, half:], need(base + 3)[...])
        term = jnp.sum(
            need(base + 1)[...].astype(jnp.float32) * hidden_grad, axis=1, keepdims=True
        )
        gated = term if gated is None else gated + term
        out[2 + shard][...] = (hidden_grad * need(base)[...].astype(jnp.float32)).astype(jnp.bfloat16)
        send(2 + shard)
    logit_grad = gated * (1.0 - need(1)[1][:, 0:1])
    out[0][...] = spread_lanes(logit_grad)
    send(0)
    normed = need(2)
    for part in range(2):
        out[1][part : part + 1] = jnp.sum(
            normed[:, part * half : (part + 1) * half].astype(jnp.float32) * logit_grad,
            axis=0,
            keepdims=True,
        )
    send(1)


def back_step(shards, need, out, send, first_sum, second_sum):
    count, half = out[0].shape
    width = 2 * half
    for shard in range(shards):
        grad = need(3 * shard)[...]
        first = contracted_columns(grad, need(3 * shard + 1)[...])
        second = contracted_columns(grad, need(3 * shard + 2)[...])
        if shard == 0:
            first_sum[...], second_sum[...] = first, second
        else:
            first_sum[...] += first
            second_sum[...] += second
    base = 3 * shards
    logit_grad = need(base)[:, 0:1]
    unit, cotan, root = need(base + 1), need(base + 2), need(base + 3)[0][:, 0:1]
    row_of_slot, gain, column = need(base + 4), need(base + 5), need(base + 6)
    first = (first_sum[...] + logit_grad * column[0:1]) * gain[0:1]
    second = (second_sum[...] + logit_grad * column[1:2]) * gain[1:2]
    unit_first = unit[:, :half].astype(jnp.float32)
    unit_second = unit[:, half:].astype(jnp.float32)
    grad_mean = feature_mean(first, second, width)
    grad_unit = feature_mean(first * unit_first, second * unit_second, width)
    first = cotan[:, :half].astype(jnp.float32) + root * (
        first - grad_mean - unit_first * grad_unit
    )
    second = cotan[:, half:].astype(jnp.float32) + root * (
        second - grad_mean - unit_second * grad_unit
    )
    ids = lax.broadcasted_iota(jnp.int32, (count, row_of_slot.shape[1]), 0)
    rows = product(
        (ids == row_of_slot[0:1]).astype(jnp.bfloat16), first.astype(jnp.bfloat16)
    ) + product((ids == row_of_slot[1:2]).astype(jnp.bfloat16), second.astype(jnp.bfloat16))
    out[0][...] = rows.astype(jnp.bfloat16)
    send(0)


def tail_kernel(column_ref, rows_ref, into_ref, tail, sem):
    experts, more, half = tail.shape
    words = column_ref[...]
    high = words.astype(jnp.bfloat16).astype(jnp.float32)
    block = jnp.concatenate([high, words - high, jnp.zeros((more - 4, half), jnp.float32)])
    tail[...] = jnp.broadcast_to(block[None], tail.shape).astype(jnp.bfloat16)
    copy = pltpu.make_async_copy(tail, into_ref.at[:, pl.ds(into_ref.shape[1] - more, more)], sem)
    copy.start()
    copy.wait()


def joined_kernel(tower_ref, own_ref, other_ref, whole_ref):
    half = own_ref.shape[1]
    own_at = pl.multiple_of(tower_ref[0] * half, 128)
    other_at = pl.multiple_of((1 - tower_ref[0]) * half, 128)
    whole_ref[:, pl.ds(own_at, half)] = own_ref[...]
    whole_ref[:, pl.ds(other_at, half)] = other_ref[...]


def pair_rows(embeds):
    own_rows = embeds[0].astype(jnp.float32)
    local_member = (
        own_rows * lax.rsqrt(jnp.sum(own_rows * own_rows, axis=-1, keepdims=True) + epsilon)
    ).astype(jnp.bfloat16)
    return local_member, exchanged(local_member, "tower", 1)


def pair_grads(local_member, panel_rows, logit_scale_log, pairwise_logit_bias, dp_index):
    softness_factor = jnp.exp(logit_scale_log)
    row_count = local_member.shape[0]
    row_global = dp_index * row_count + jnp.arange(row_count, dtype=jnp.int32)
    pair_scores = (
        softness_factor * contracted_columns(local_member, panel_rows) + pairwise_logit_bias
    )
    col_global = jnp.arange(panel_rows.shape[0], dtype=jnp.int32)
    pair_labels = jnp.where(row_global[:, None] == col_global[None, :], 1.0, -1.0).astype(
        jnp.float32
    )
    panel_weights = (
        -pair_labels * jax.nn.sigmoid(-pair_labels * pair_scores) * softness_factor
    ).astype(jnp.bfloat16)
    return product(panel_weights, panel_rows)


def body(
    tokens,
    norm_gain,
    router,
    expert_ids,
    up_weights,
    down_weights,
    cotangent,
    embeds,
    logit_scale_log,
    pairwise_logit_bias,
):
    token_total, width = tokens.shape
    hidden = up_weights.shape[1]
    experts = router.shape[1]
    capacity = 3 * token_total // (2 * experts)
    half = width // 2
    slots = experts * capacity
    tower = lax.axis_index("tower")
    expert = lax.axis_index("z") * columns + lax.axis_index("x")
    dp_index = expert * line + lax.axis_index("y")
    bf16, f32 = jnp.bfloat16, jnp.float32

    def halves(values, axis):
        return (
            lax.dynamic_slice_in_dim(values, tower * half, half, axis),
            lax.dynamic_slice_in_dim(values, (1 - tower) * half, half, axis),
        )

    up_own, down_own = halves(up_weights, 0), halves(down_weights, 1)
    up_before, up_after = shifted(up_own[0], "y", 1), shifted(up_own[0], "y", -1)
    down_part, up_before, up_after = lax.optimization_barrier((down_own[0], up_before, up_after))
    down_before, down_after = shifted(down_part, "y", 1), shifted(down_part, "y", -1)
    up_before, down_before, down_after = lax.optimization_barrier(
        (up_before, down_before, down_after)
    )
    up_across, down_across = shifted(up_before, "y", 1), shifted(down_after, "y", -1)

    tower_word = tower.astype(jnp.int32).reshape(1)
    return_rows = 2 * capacity + 8
    sent_ids = jnp.arange(2 * slots, dtype=jnp.int32)
    slot_of_sent = sent_ids // (2 * capacity) * capacity + sent_ids % capacity
    in_first = sent_ids % (2 * capacity) < capacity
    slot_maps = jnp.stack(
        [jnp.where(in_first, slot_of_sent, -1), jnp.where(in_first, -1, slot_of_sent)]
    )
    slot_ids = jnp.arange(slots, dtype=jnp.int32)
    first_row = slot_ids // capacity * return_rows + slot_ids % capacity
    row_maps = jnp.stack([first_row, first_row + capacity])

    def spread(rows):
        return lax.all_to_all(
            rows.reshape(experts, -1, half),
            ("z", "x"),
            split_axis=0,
            concat_axis=0,
            tiled=True,
        ).reshape(-1, half)

    def both(piece):
        return piece, exchanged(piece, "tower", 1)

    token_rows, cotan_rows, token_maps = staged_call(
        functools.partial(slot_step, capacity, experts, return_rows),
        [shape_of((2 * slots, half), bf16)] * 2 + [shape_of((2, token_total), jnp.int32)],
        (expert_ids, tokens, cotangent),
        16,
        scalars=(tower_word,),
    )
    local_member, other_member = pair_rows(embeds)
    token_rows, other_member = lax.optimization_barrier((token_rows, other_member))
    panel_rows = lax.all_gather(other_member, ("z", "x", "y"), axis=0, tiled=True)
    token_rows = spread(token_rows)
    cotan_rows, token_rows = lax.optimization_barrier((cotan_rows, token_rows))
    cotan_rows = spread(cotan_rows)
    ups = [up_own] + [both(piece) for piece in (up_before, up_after, up_across)]
    downs = [down_own] + [both(piece) for piece in (down_before, down_after, down_across)]

    def features(values):
        return jnp.concatenate(halves(values.astype(f32)[None, :], 1), axis=0)

    gain = features(norm_gain)
    column = features(lax.dynamic_slice_in_dim(router, expert, 1, 1)[:, 0])
    shards, near = len(ups), len(ups) - 1
    front_shapes = [
        shape_of((slots, hidden), bf16),
        shape_of((slots, hidden), bf16),
        shape_of((hidden, slots), bf16),
    ]
    term_shapes = [shape_of((hidden, half), bf16)] * 2
    own_shapes = [shape_of((hidden, half), f32), shape_of((hidden, half), bf16)]
    token_rows, _, _ = lax.optimization_barrier((token_rows, down_before, down_after))
    normed, unit, scales, *near_fronts = staged_call(
        functools.partial(norm_step, near),
        [shape_of((slots, width), bf16)] * 2
        + [shape_of((2, slots, 128), f32)]
        + front_shapes * near,
        (slot_maps, token_rows, gain, column, *(p for pair in ups[:near] for p in pair)),
        32,
        1 << 34,
    )
    fronts = [near_fronts[3 * k : 3 * k + 3] for k in range(near)]
    fronts.append(staged_call(front_step, front_shapes, (normed,) + ups[near], 16))
    cotan_rows, across_turned = lax.optimization_barrier((cotan_rows, fronts[near][2]))
    cotan, output, *terms = staged_call(
        gate_step,
        [shape_of((slots, width), bf16)] * 2 + term_shapes * near + own_shapes,
        (slot_maps, cotan_rows, scales, fronts[1][2], fronts[2][2], across_turned, fronts[0][2]),
        32,
    )
    logit_grad, router_halves, *preact_grads = staged_call(
        functools.partial(hidden_step, shards),
        [shape_of((slots, 128), f32), shape_of((2, half), f32)]
        + [shape_of((slots, hidden), bf16)] * shards,
        (output, scales, normed)
        + tuple(p for k in range(shards) for p in (*fronts[k][:2], *downs[k])),
        28,
    )

    def tower_sum(first, second):
        return first.astype(f32) + exchanged(second, "tower", 1).astype(f32)

    down_before, down_after, down_across = (
        tower_sum(*terms[2 * term : 2 * term + 2]).astype(bf16) for term in range(near)
    )
    router_column = jnp.where(
        tower == 0, router_halves, jnp.concatenate([router_halves[1:], router_halves[:1]])
    )
    router_column = router_column + exchanged(router_column, "tower", 1)
    logit_grad, router_column, down_before, down_after, down_across = lax.optimization_barrier(
        (logit_grad, router_column, down_before, down_after, down_across)
    )
    down_before = shifted(down_before, "y", -1)
    down_after = shifted(down_after, "y", 1)
    down_across = shifted(down_across, "y", 2)
    beside, beyond, farthest = (exchanged(router_column, "y", bit) for bit in (1, 2, 3))
    router_column = (router_column + beside) + (beyond + farthest)
    back_rows = staged_call(
        functools.partial(back_step, shards),
        [shape_of((experts * return_rows, half), bf16)],
        tuple(p for k in range(shards) for p in (preact_grads[k], *ups[k]))
        + (logit_grad, unit, cotan, scales, row_maps, gain, column),
        32,
        16 * shards * slots * width * hidden,
        scratch=[pltpu.VMEM((slots, half), f32), pltpu.VMEM((slots, half), f32)],
    )[0]
    back_rows = local_call(
        tail_kernel,
        [pltpu.HBM((experts, return_rows, half), bf16)],
        (
            router_column,
            pltpu.with_memory_space_constraint(
                back_rows.reshape(experts, return_rows, half), pltpu.HBM
            ),
        ),
        8,
        in_specs=[
            pl.BlockSpec(memory_space=pltpu.VMEM),
            pl.BlockSpec(memory_space=pltpu.HBM),
        ],
        out_specs=[pl.BlockSpec(memory_space=pltpu.HBM)],
        input_output_aliases={1: 0},
        scratch_shapes=[
            pltpu.VMEM((experts, return_rows - 2 * capacity, half), bf16),
            pltpu.SemaphoreType.DMA,
        ],
    )[0]
    returned = spread(back_rows)
    panel_rows, down_before = lax.optimization_barrier((panel_rows, down_before))
    embed_grads = pair_grads(
        local_member, panel_rows, logit_scale_log, pairwise_logit_bias, dp_index
    )
    embed_grads, token_maps = lax.optimization_barrier((embed_grads, token_maps))
    tokens_grad, router_rows = staged_call(
        functools.partial(token_step, experts, 2 * capacity),
        [shape_of((token_total, width), bf16), shape_of((experts, width), f32)],
        (token_maps, returned),
        20,
    )

    down_half = (
        tower_sum(*terms[2 * near :])
        + down_before.astype(f32)
        + down_after.astype(f32)
        + down_across.astype(f32)
    )
    down_other = exchanged(down_half, "tower", 1)
    whole = pl.BlockSpec(memory_space=pltpu.VMEM)
    down_grad = local_call(
        joined_kernel,
        [shape_of((hidden, width), f32)],
        (tower_word, down_half, down_other),
        16,
        in_specs=[pl.BlockSpec(memory_space=pltpu.SMEM), whole, whole],
    )[0]
    return (tokens_grad, router_rows.T, down_grad, embed_grads[None])


def solution(mesh):
    towers, chips = mesh.devices.shape
    grid = Mesh(
        mesh.devices.reshape(towers, chips // (columns * line), columns, line),
        ("tower", "z", "x", "y"),
    )
    dp = ("z", "x", "y")
    rows = P(("tower",) + dp, None)
    placed = (
        rows,
        P(),
        P(),
        rows,
        P(None, dp),
        P(dp, None),
        rows,
        P("tower", dp, None),
        P(),
        P(),
    )
    return jax.shard_map(
        body,
        mesh=grid,
        in_specs=placed,
        out_specs=(rows, P(), P(dp, None), P("tower", dp, None)),
        check_vma=False,
    )
```

```python
import functools

import jax
import jax.numpy as jnp
from jax import lax
from jax.experimental import pallas as pl
from jax.experimental.pallas import tpu as pltpu
from jax.sharding import Mesh, PartitionSpec as P

epsilon = 1e-06
gelu_root = 0.7978845608028654
gelu_cubic = 0.044715

line = 4
columns = 4


def shifted(block, axis, step):
    count = lax.axis_size(axis)
    return lax.ppermute(block, axis, [(i, (i + step) % count) for i in range(count)])


def exchanged(block, axis, bit):
    count = lax.axis_size(axis)
    return lax.ppermute(block, axis, [(i, i ^ bit) for i in range(count)])


def product(left, right):
    return jnp.dot(left, right, preferred_element_type=jnp.float32)


def contract_rows(left, right):
    return lax.dot_general(
        left, right, (((0,), (0,)), ((), ())), preferred_element_type=jnp.float32
    )


def contracted_columns(left, right):
    return lax.dot_general(
        left, right, (((1,), (1,)), ((), ())), preferred_element_type=jnp.float32
    )


def gelu_pair(values):
    inner = gelu_root * (values + gelu_cubic * values * values * values)
    tangent = jnp.tanh(inner)
    slope = 0.5 * (1.0 + tangent) + 0.5 * values * (1.0 - tangent * tangent) * gelu_root * (
        1.0 + 3.0 * gelu_cubic * values * values
    )
    return 0.5 * values * (1.0 + tangent), slope


def local_call(kernel, out_shape, operands, vmem, flops=1, **options):
    return pl.pallas_call(
        kernel,
        out_shape=out_shape,
        compiler_params=pltpu.CompilerParams(vmem_limit_bytes=vmem << 20),
        cost_estimate=pl.CostEstimate(flops=flops, bytes_accessed=1, transcendentals=0),
        **options,
    )(*operands)


def shape_of(shape, dtype):
    return jax.ShapeDtypeStruct(shape, dtype)


def staged_call(run, out_shape, operands, vmem, flops=1, scalars=(), scratch=(), joint=()):
    fixed, count, results = len(scalars), len(operands), len(out_shape)
    joint = dict(joint)
    places, buffers = [], []
    for i, value in enumerate(operands):
        if i - 1 in joint:
            places.append((len(buffers) - 1, 1))
        else:
            shape = list(value.shape)
            if i in joint:
                shape[joint[i]] *= 2
            places.append((len(buffers), 0))
            buffers.append(pltpu.VMEM(tuple(shape), value.dtype))

    def kernel(*refs):
        numbers, refs = refs[:fixed], refs[fixed:]
        sources, refs = refs[:count], refs[count:]
        targets, refs = refs[:results], refs[results:]
        held, refs = refs[: len(buffers)], refs[len(buffers) :]
        out, refs = refs[:results], refs[results:]
        in_sems, out_sems, rest = refs[0], refs[1], refs[2:]

        def target(i):
            at, part = places[i]
            first = i - part
            if first not in joint:
                return held[at]
            extent = sources[i].shape[joint[first]]
            window = pl.ds(part * extent, extent)
            return held[at].at[window] if joint[first] == 0 else held[at].at[:, window]

        fetched = [
            pltpu.make_async_copy(sources[i], target(i), in_sems.at[i]) for i in range(count)
        ]
        sent = [
            pltpu.make_async_copy(out[j], targets[j], out_sems.at[j]) for j in range(results)
        ]
        for copy in fetched:
            copy.start()
        arrived = set()

        def need(i):
            if i not in arrived:
                fetched[i].wait()
                if i in joint:
                    fetched[i + 1].wait()
                arrived.add(i)
            return held[places[i][0]]

        run(need, out, lambda j: sent[j].start(), *numbers, *rest)
        for copy in sent:
            copy.wait()

    apart = pl.BlockSpec(memory_space=pltpu.HBM)
    pinned = [pltpu.with_memory_space_constraint(v, pltpu.HBM) for v in operands]
    return local_call(
        kernel,
        [pltpu.HBM(v.shape, v.dtype) for v in out_shape],
        (*scalars, *pinned),
        vmem,
        flops,
        in_specs=[pl.BlockSpec(memory_space=pltpu.SMEM)] * fixed + [apart] * count,
        out_specs=[apart] * results,
        scratch_shapes=buffers
        + [pltpu.VMEM(v.shape, v.dtype) for v in out_shape]
        + [pltpu.SemaphoreType.DMA((count,)), pltpu.SemaphoreType.DMA((results,))]
        + list(scratch),
    )


def slot_step(capacity, experts, return_rows, need, out, send, tower_ref):
    tower = tower_ref[0]
    choices = need(0)[...]
    total = choices.shape[0]
    onehot = choices == lax.broadcasted_iota(jnp.int32, (total, experts), 1)
    lower_tri = lax.broadcasted_iota(jnp.int32, (total, total), 0) >= lax.broadcasted_iota(
        jnp.int32, (total, total), 1
    )
    running = product(lower_tri.astype(jnp.bfloat16), onehot.astype(jnp.bfloat16))
    rank = jnp.sum(jnp.where(onehot, running, 0.0), axis=1, keepdims=True) - 1.0
    first_row = choices.astype(jnp.float32) * (2.0 * capacity) + rank
    first_row = jnp.broadcast_to(first_row, (total, 128)).T[0:1].astype(jnp.int32)
    low_row = first_row + capacity * tower
    high_row = first_row + capacity * (1 - tower)
    more = choices.astype(jnp.float32) * jnp.float32(return_rows - 2 * capacity)
    more = jnp.broadcast_to(more, (total, 128)).T[0:1].astype(jnp.int32)
    out[1][0:1] = low_row
    out[1][1:2] = high_row
    out[1][2:3] = low_row + more
    out[1][3:4] = high_row + more
    send(1)
    placed(low_row, high_row, need(1), out, send)


def placed(low_row, high_row, values, out, send):
    count, half = out[0].shape
    ids = lax.broadcasted_iota(jnp.int32, (count, values.shape[0]), 0)
    low_place = (ids == low_row).astype(jnp.bfloat16)
    high_place = (ids == high_row).astype(jnp.bfloat16)
    rows = product(low_place, values[:, :half]) + product(high_place, values[:, half:])
    out[0][...] = rows.astype(jnp.bfloat16)
    send(0)


def place_step(need, out, send):
    maps = need(0)
    placed(maps[0:1], maps[1:2], need(1), out, send)


def token_step(experts, column_row, need, out, send):
    rows_of = need(0)
    rows = need(1)[...]
    count, half = rows.shape
    total = out[0].shape[0]
    ids = lax.broadcasted_iota(jnp.int32, (count, total), 0)
    for part in range(2):
        place = (ids == rows_of[2 + part : 3 + part]).astype(jnp.float32).T.astype(jnp.bfloat16)
        out[0][:, part * half : (part + 1) * half] = product(place, rows).astype(jnp.bfloat16)
    send(0)
    words = rows.astype(jnp.float32).reshape(experts, count // experts, half)
    for part in range(2):
        sums = words[:, column_row + part, :] + words[:, column_row + 2 + part, :]
        out[1][:, part * half : (part + 1) * half] = sums
    send(1)


def taken(rows, slot_of_row, slots):
    ids = lax.broadcasted_iota(jnp.int32, (slots, rows.shape[0]), 0)
    return product((ids == slot_of_row).astype(jnp.bfloat16), rows)


def feature_mean(first, second, width):
    total = jnp.sum(first, axis=1, keepdims=True) + jnp.sum(second, axis=1, keepdims=True)
    return total / width


def spread_lanes(column):
    return jnp.broadcast_to(column, (column.shape[0], 128))


def front(normed, up_pair, out, send, base):
    preact = product(normed[...], up_pair[...])
    gelu, slope = gelu_pair(preact)
    out[base][...] = slope.astype(jnp.bfloat16)
    send(base)
    out[base + 1][...] = gelu.astype(jnp.bfloat16)
    send(base + 1)
    out[base + 2][...] = gelu.T.astype(jnp.bfloat16)
    send(base + 2)


def norm_step(shards, need, out, send):
    slots, width = out[0].shape
    half = width // 2
    maps, rows = need(0), need(1)[...]
    first, second = (taken(rows, maps[part : part + 1], slots) for part in range(2))
    mean = feature_mean(first, second, width)
    first, second = first - mean, second - mean
    root = lax.rsqrt(feature_mean(first * first, second * second, width) + epsilon)
    first, second = first * root, second * root
    out[1][:, :half] = first.astype(jnp.bfloat16)
    out[1][:, half:] = second.astype(jnp.bfloat16)
    send(1)
    gain, column = need(2), need(3)
    first = (first * gain[0:1]).astype(jnp.bfloat16)
    second = (second * gain[1:2]).astype(jnp.bfloat16)
    out[0][:, :half] = first
    out[0][:, half:] = second
    send(0)
    logits = jnp.sum(first.astype(jnp.float32) * column[0:1], axis=1, keepdims=True) + jnp.sum(
        second.astype(jnp.float32) * column[1:2], axis=1, keepdims=True
    )
    out[2][0] = spread_lanes(root)
    out[2][1] = spread_lanes(jax.nn.sigmoid(logits))
    send(2)
    for shard in range(shards):
        front(out[0], need(4 + 2 * shard), out, send, 3 + 3 * shard)


def front_step(need, out, send):
    front(need(0), need(1), out, send, 0)


def gate_step(need, out, send):
    slots, width = out[0].shape
    half = width // 2
    maps, rows = need(0), need(1)[...]
    gates = need(2)[1][:, 0:1]
    for part in range(2):
        values = taken(rows, maps[part : part + 1], slots)
        out[0][:, part * half : (part + 1) * half] = values.astype(jnp.bfloat16)
        out[1][:, part * half : (part + 1) * half] = (gates * values).astype(jnp.bfloat16)
    send(0)
    send(1)
    for term in range((len(out) - 2) // 2):
        down_term(need(3 + term), out[1], out, send, 2 + 2 * term)


def down_term(turned, output, out, send, base):
    half = out[base].shape[1]
    terms = product(turned[...], output[...])
    out[base + 1][...] = terms[:, half:].astype(jnp.bfloat16)
    send(base + 1)
    out[base][...] = terms[:, :half].astype(out[base].dtype)
    send(base)


def hidden_step(shards, need, out, send, tower_ref):
    output = need(0)
    half = output.shape[1] // 2
    gated = None
    for shard in range(shards):
        base = 1 + 4 * shard
        hidden_grad = contracted_columns(output[...], need(base)[...])
        term = jnp.sum(
            need(base + 3)[...].astype(jnp.float32) * hidden_grad, axis=1, keepdims=True
        )
        gated = term if gated is None else gated + term
        out[2 + shard][...] = (hidden_grad * need(base + 2)[...].astype(jnp.float32)).astype(jnp.bfloat16)
        send(2 + shard)
    base = 1 + 4 * shards
    logit_grad = gated * (1.0 - need(base)[1][:, 0:1])
    out[0][...] = spread_lanes(logit_grad)
    send(0)
    normed = need(base + 1)
    sums = [
        jnp.sum(
            normed[:, part * half : (part + 1) * half].astype(jnp.float32) * logit_grad,
            axis=0,
            keepdims=True,
        )
        for part in range(2)
    ]
    in_order = tower_ref[0] == 0
    out[1][0:1] = jnp.where(in_order, sums[0], sums[1])
    out[1][1:2] = jnp.where(in_order, sums[1], sums[0])
    send(1)


def back_step(shards, need, out, send, total):
    count, half = out[0].shape
    width = 2 * half
    for shard in range(shards):
        grad = need(3 * shard)[...]
        term = contracted_columns(grad, need(3 * shard + 1)[...])
        if shard == 0:
            total[...] = term
        else:
            total[...] += term
    base = 3 * shards
    logit_grad = need(base)[:, 0:1]
    unit, cotan, root = need(base + 1), need(base + 2), need(base + 3)[0][:, 0:1]
    row_of_slot, gain, column = need(base + 4), need(base + 5), need(base + 6)
    first = (total[:, :half] + logit_grad * column[0:1]) * gain[0:1]
    second = (total[:, half:] + logit_grad * column[1:2]) * gain[1:2]
    unit_first = unit[:, :half].astype(jnp.float32)
    unit_second = unit[:, half:].astype(jnp.float32)
    grad_mean = feature_mean(first, second, width)
    grad_unit = feature_mean(first * unit_first, second * unit_second, width)
    first = cotan[:, :half].astype(jnp.float32) + root * (
        first - grad_mean - unit_first * grad_unit
    )
    second = cotan[:, half:].astype(jnp.float32) + root * (
        second - grad_mean - unit_second * grad_unit
    )
    ids = lax.broadcasted_iota(jnp.int32, (count, row_of_slot.shape[1]), 0)
    rows = product(
        (ids == row_of_slot[0:1]).astype(jnp.bfloat16), first.astype(jnp.bfloat16)
    ) + product((ids == row_of_slot[1:2]).astype(jnp.bfloat16), second.astype(jnp.bfloat16))
    out[0][...] = rows.astype(jnp.bfloat16)
    send(0)


def tail_kernel(column_ref, rows_ref, into_ref, tail, sem):
    experts, more, half = tail.shape
    words = column_ref[...]
    high = words.astype(jnp.bfloat16).astype(jnp.float32)
    block = jnp.concatenate([high, words - high, jnp.zeros((more - 4, half), jnp.float32)])
    tail[...] = jnp.broadcast_to(block[None], tail.shape).astype(jnp.bfloat16)
    copy = pltpu.make_async_copy(tail, into_ref.at[:, pl.ds(into_ref.shape[1] - more, more)], sem)
    copy.start()
    copy.wait()


def joined_kernel(tower_ref, own_ref, other_ref, whole_ref):
    half = own_ref.shape[1]
    own_at = pl.multiple_of(tower_ref[0] * half, 128)
    other_at = pl.multiple_of((1 - tower_ref[0]) * half, 128)
    whole_ref[:, pl.ds(own_at, half)] = own_ref[...]
    whole_ref[:, pl.ds(other_at, half)] = other_ref[...]


def pair_rows(embeds):
    own_rows = embeds[0].astype(jnp.float32)
    local_member = (
        own_rows * lax.rsqrt(jnp.sum(own_rows * own_rows, axis=-1, keepdims=True) + epsilon)
    ).astype(jnp.bfloat16)
    return local_member, exchanged(local_member, "tower", 1)


def pair_grads(local_member, panel_rows, logit_scale_log, pairwise_logit_bias, dp_index):
    softness_factor = jnp.exp(logit_scale_log)
    row_count = local_member.shape[0]
    row_global = dp_index * row_count + jnp.arange(row_count, dtype=jnp.int32)
    pair_scores = (
        softness_factor * contracted_columns(local_member, panel_rows) + pairwise_logit_bias
    )
    col_global = jnp.arange(panel_rows.shape[0], dtype=jnp.int32)
    pair_labels = jnp.where(row_global[:, None] == col_global[None, :], 1.0, -1.0).astype(
        jnp.float32
    )
    panel_weights = (
        -pair_labels * jax.nn.sigmoid(-pair_labels * pair_scores) * softness_factor
    ).astype(jnp.bfloat16)
    return product(panel_weights, panel_rows)


def body(
    tokens,
    norm_gain,
    router,
    expert_ids,
    up_weights,
    down_weights,
    cotangent,
    embeds,
    logit_scale_log,
    pairwise_logit_bias,
):
    token_total, width = tokens.shape
    hidden = up_weights.shape[1]
    experts = router.shape[1]
    capacity = 3 * token_total // (2 * experts)
    half = width // 2
    slots = experts * capacity
    tower = lax.axis_index("tower")
    expert = lax.axis_index("z") * columns + lax.axis_index("x")
    dp_index = expert * line + lax.axis_index("y")
    bf16, f32 = jnp.bfloat16, jnp.float32

    def halves(values, axis):
        return (
            lax.dynamic_slice_in_dim(values, tower * half, half, axis),
            lax.dynamic_slice_in_dim(values, (1 - tower) * half, half, axis),
        )

    up_own, down_own = halves(up_weights, 0), halves(down_weights, 1)
    up_before, up_after = shifted(up_own[0], "y", 1), shifted(up_own[0], "y", -1)

    tower_word = tower.astype(jnp.int32).reshape(1)
    return_rows = 2 * capacity + 8
    sent_ids = jnp.arange(2 * slots, dtype=jnp.int32)
    slot_of_sent = sent_ids // (2 * capacity) * capacity + sent_ids % capacity
    in_first = sent_ids % (2 * capacity) < capacity
    slot_maps = jnp.stack(
        [jnp.where(in_first, slot_of_sent, -1), jnp.where(in_first, -1, slot_of_sent)]
    )
    slot_ids = jnp.arange(slots, dtype=jnp.int32)
    first_row = slot_ids // capacity * return_rows + slot_ids % capacity
    row_maps = jnp.stack([first_row, first_row + capacity])

    def spread(rows):
        return lax.all_to_all(
            rows.reshape(experts, -1, half),
            ("z", "x"),
            split_axis=0,
            concat_axis=0,
            tiled=True,
        ).reshape(-1, half)

    def both(piece):
        return piece, exchanged(piece, "tower", 1)

    token_rows, token_maps = staged_call(
        functools.partial(slot_step, capacity, experts, return_rows),
        [shape_of((2 * slots, half), bf16), shape_of((4, token_total), jnp.int32)],
        (expert_ids, tokens),
        16,
        scalars=(tower_word,),
    )
    late_maps, up_before, up_after = lax.optimization_barrier((token_maps, up_before, up_after))
    cotan_rows = staged_call(
        place_step, [shape_of((2 * slots, half), bf16)], (late_maps, cotangent), 16
    )[0]
    down_part, up_before, up_after, cotan_rows = lax.optimization_barrier(
        (down_own[0], up_before, up_after, cotan_rows)
    )
    down_before, down_after = shifted(down_part, "y", 1), shifted(down_part, "y", -1)
    up_before, down_before, down_after = lax.optimization_barrier(
        (up_before, down_before, down_after)
    )
    up_across, down_across = shifted(up_before, "y", 1), shifted(down_after, "y", -1)

    local_member, other_member = pair_rows(embeds)
    token_rows, other_member = lax.optimization_barrier((token_rows, other_member))
    panel_rows = lax.all_gather(other_member, ("z", "x", "y"), axis=0, tiled=True)
    token_rows = spread(token_rows)
    cotan_rows, token_rows = lax.optimization_barrier((cotan_rows, token_rows))
    cotan_rows = spread(cotan_rows)
    ups = [up_own] + [both(piece) for piece in (up_before, up_after, up_across)]
    downs = [down_own] + [both(piece) for piece in (down_before, down_after, down_across)]

    def features(values):
        return jnp.concatenate(halves(values.astype(f32)[None, :], 1), axis=0)

    gain = features(norm_gain)
    column = features(lax.dynamic_slice_in_dim(router, expert, 1, 1)[:, 0])
    shards, near = len(ups), len(ups) - 1
    front_shapes = [
        shape_of((slots, hidden), bf16),
        shape_of((slots, hidden), bf16),
        shape_of((hidden, slots), bf16),
    ]
    term_shapes = [shape_of((hidden, half), bf16)] * 2
    own_shapes = [shape_of((hidden, half), f32), shape_of((hidden, half), bf16)]
    token_rows, _, _ = lax.optimization_barrier((token_rows, down_before, down_after))
    normed, unit, scales, *near_fronts = staged_call(
        functools.partial(norm_step, near),
        [shape_of((slots, width), bf16)] * 2
        + [shape_of((2, slots, 128), f32)]
        + front_shapes * near,
        (slot_maps, token_rows, gain, column, *(p for pair in ups[:near] for p in pair)),
        32,
        1 << 34,
        joint=[(4 + 2 * k, 0) for k in range(near)],
    )
    fronts = [near_fronts[3 * k : 3 * k + 3] for k in range(near)]
    fronts.append(staged_call(front_step, front_shapes, (normed,) + ups[near], 16, joint=[(1, 0)]))
    cotan_rows, across_turned = lax.optimization_barrier((cotan_rows, fronts[near][2]))
    cotan, output, *terms = staged_call(
        gate_step,
        [shape_of((slots, width), bf16)] * 2 + term_shapes * near + own_shapes,
        (slot_maps, cotan_rows, scales, fronts[1][2], fronts[2][2], across_turned, fronts[0][2]),
        32,
    )
    logit_grad, router_halves, *preact_grads = staged_call(
        functools.partial(hidden_step, shards),
        [shape_of((slots, 128), f32), shape_of((2, half), f32)]
        + [shape_of((slots, hidden), bf16)] * shards,
        (output, *(p for k in range(shards) for p in (*downs[k], *fronts[k][:2])), scales, normed),
        28,
        scalars=(tower_word,),
        joint=[(1 + 4 * k, 1) for k in range(shards)],
    )

    def tower_sum(first, second):
        return first.astype(f32) + exchanged(second, "tower", 1).astype(f32)

    down_before, down_after, down_across = (
        tower_sum(*terms[2 * term : 2 * term + 2]).astype(bf16) for term in range(near)
    )
    router_column = router_halves
    router_column = router_column + exchanged(router_column, "tower", 1)
    logit_grad, router_column, down_before, down_after, down_across = lax.optimization_barrier(
        (logit_grad, router_column, down_before, down_after, down_across)
    )
    down_before = shifted(down_before, "y", -1)
    down_after = shifted(down_after, "y", 1)
    down_across = shifted(down_across, "y", 2)
    beside, beyond, farthest = (exchanged(router_column, "y", bit) for bit in (1, 2, 3))
    router_column = (router_column + beside) + (beyond + farthest)
    back_rows = staged_call(
        functools.partial(back_step, shards),
        [shape_of((experts * return_rows, half), bf16)],
        tuple(p for k in range(shards) for p in (preact_grads[k], *ups[k]))
        + (logit_grad, unit, cotan, scales, row_maps, gain, column),
        32,
        16 * shards * slots * width * hidden,
        scratch=[pltpu.VMEM((slots, width), f32)],
        joint=[(3 * k + 1, 0) for k in range(shards)],
    )[0]
    back_rows = local_call(
        tail_kernel,
        [pltpu.HBM((experts, return_rows, half), bf16)],
        (
            router_column,
            pltpu.with_memory_space_constraint(
                back_rows.reshape(experts, return_rows, half), pltpu.HBM
            ),
        ),
        8,
        in_specs=[
            pl.BlockSpec(memory_space=pltpu.VMEM),
            pl.BlockSpec(memory_space=pltpu.HBM),
        ],
        out_specs=[pl.BlockSpec(memory_space=pltpu.HBM)],
        input_output_aliases={1: 0},
        scratch_shapes=[
            pltpu.VMEM((experts, return_rows - 2 * capacity, half), bf16),
            pltpu.SemaphoreType.DMA,
        ],
    )[0]
    returned = spread(back_rows)
    panel_rows, down_before = lax.optimization_barrier((panel_rows, down_before))
    embed_grads = pair_grads(
        local_member, panel_rows, logit_scale_log, pairwise_logit_bias, dp_index
    )
    down_half = (
        tower_sum(*terms[2 * near :])
        + down_before.astype(f32)
        + down_after.astype(f32)
        + down_across.astype(f32)
    )
    down_other = exchanged(down_half, "tower", 1)
    whole = pl.BlockSpec(memory_space=pltpu.VMEM)
    down_grad = local_call(
        joined_kernel,
        [shape_of((hidden, width), f32)],
        (tower_word, down_half, down_other),
        16,
        in_specs=[pl.BlockSpec(memory_space=pltpu.SMEM), whole, whole],
    )[0]
    embed_grads, token_maps, down_grad = lax.optimization_barrier(
        (embed_grads, token_maps, down_grad)
    )
    tokens_grad, router_rows = staged_call(
        functools.partial(token_step, experts, 2 * capacity),
        [shape_of((token_total, width), bf16), shape_of((experts, width), f32)],
        (token_maps, returned),
        20,
    )
    return (tokens_grad, router_rows.T, down_grad, embed_grads[None])


def solution(mesh):
    towers, chips = mesh.devices.shape
    grid = Mesh(
        mesh.devices.reshape(towers, chips // (columns * line), columns, line),
        ("tower", "z", "x", "y"),
    )
    dp = ("z", "x", "y")
    rows = P(("tower",) + dp, None)
    placed = (
        rows,
        P(),
        P(),
        rows,
        P(None, dp),
        P(dp, None),
        rows,
        P("tower", dp, None),
        P(),
        P(),
    )
    return jax.shard_map(
        body,
        mesh=grid,
        in_specs=placed,
        out_specs=(rows, P(), P(dp, None), P("tower", dp, None)),
        check_vma=False,
    )
```

```python
import functools

import jax
import jax.numpy as jnp
from jax import lax
from jax.experimental import pallas as pl
from jax.experimental.pallas import tpu as pltpu
from jax.sharding import Mesh, PartitionSpec as P

epsilon = 1e-06
gelu_root = 0.7978845608028654
gelu_cubic = 0.044715

line = 4
columns = 4


def shifted(block, axis, step):
    count = lax.axis_size(axis)
    return lax.ppermute(block, axis, [(i, (i + step) % count) for i in range(count)])


def exchanged(block, axis, bit):
    count = lax.axis_size(axis)
    return lax.ppermute(block, axis, [(i, i ^ bit) for i in range(count)])


def product(left, right):
    return jnp.dot(left, right, preferred_element_type=jnp.float32)


def contract_rows(left, right):
    return lax.dot_general(
        left, right, (((0,), (0,)), ((), ())), preferred_element_type=jnp.float32
    )


def contracted_columns(left, right):
    return lax.dot_general(
        left, right, (((1,), (1,)), ((), ())), preferred_element_type=jnp.float32
    )


def gelu_pair(values):
    inner = gelu_root * (values + gelu_cubic * values * values * values)
    tangent = jnp.tanh(inner)
    slope = 0.5 * (1.0 + tangent) + 0.5 * values * (1.0 - tangent * tangent) * gelu_root * (
        1.0 + 3.0 * gelu_cubic * values * values
    )
    return 0.5 * values * (1.0 + tangent), slope


def local_call(kernel, out_shape, operands, vmem, flops=1, **options):
    return pl.pallas_call(
        kernel,
        out_shape=out_shape,
        compiler_params=pltpu.CompilerParams(vmem_limit_bytes=vmem << 20),
        cost_estimate=pl.CostEstimate(flops=flops, bytes_accessed=1, transcendentals=0),
        **options,
    )(*operands)


def shape_of(shape, dtype):
    return jax.ShapeDtypeStruct(shape, dtype)


def staged_call(run, out_shape, operands, vmem, flops=1, scalars=(), scratch=(), joint=()):
    fixed, count, results = len(scalars), len(operands), len(out_shape)
    joint = dict(joint)
    places, buffers = [], []
    for i, value in enumerate(operands):
        if i - 1 in joint:
            places.append((len(buffers) - 1, 1))
        else:
            shape = list(value.shape)
            if i in joint:
                shape[joint[i]] *= 2
            places.append((len(buffers), 0))
            buffers.append(pltpu.VMEM(tuple(shape), value.dtype))

    def kernel(*refs):
        numbers, refs = refs[:fixed], refs[fixed:]
        sources, refs = refs[:count], refs[count:]
        targets, refs = refs[:results], refs[results:]
        held, refs = refs[: len(buffers)], refs[len(buffers) :]
        out, refs = refs[:results], refs[results:]
        in_sems, out_sems, rest = refs[0], refs[1], refs[2:]

        def target(i):
            at, part = places[i]
            first = i - part
            if first not in joint:
                return held[at]
            extent = sources[i].shape[joint[first]]
            window = pl.ds(part * extent, extent)
            return held[at].at[window] if joint[first] == 0 else held[at].at[:, window]

        fetched = [
            pltpu.make_async_copy(sources[i], target(i), in_sems.at[i]) for i in range(count)
        ]
        sent = [
            pltpu.make_async_copy(out[j], targets[j], out_sems.at[j]) for j in range(results)
        ]
        for copy in fetched:
            copy.start()
        arrived = set()

        def need(i):
            if i not in arrived:
                fetched[i].wait()
                if i in joint:
                    fetched[i + 1].wait()
                arrived.add(i)
            return held[places[i][0]]

        run(need, out, lambda j: sent[j].start(), *numbers, *rest)
        for copy in sent:
            copy.wait()

    apart = pl.BlockSpec(memory_space=pltpu.HBM)
    pinned = [pltpu.with_memory_space_constraint(v, pltpu.HBM) for v in operands]
    return local_call(
        kernel,
        [pltpu.HBM(v.shape, v.dtype) for v in out_shape],
        (*scalars, *pinned),
        vmem,
        flops,
        in_specs=[pl.BlockSpec(memory_space=pltpu.SMEM)] * fixed + [apart] * count,
        out_specs=[apart] * results,
        scratch_shapes=buffers
        + [pltpu.VMEM(v.shape, v.dtype) for v in out_shape]
        + [pltpu.SemaphoreType.DMA((count,)), pltpu.SemaphoreType.DMA((results,))]
        + list(scratch),
    )


def slot_step(capacity, experts, return_rows, need, out, send, tower_ref):
    tower = tower_ref[0]
    choices = need(0)[...]
    total = choices.shape[0]
    onehot = choices == lax.broadcasted_iota(jnp.int32, (total, experts), 1)
    lower_tri = lax.broadcasted_iota(jnp.int32, (total, total), 0) >= lax.broadcasted_iota(
        jnp.int32, (total, total), 1
    )
    running = product(lower_tri.astype(jnp.bfloat16), onehot.astype(jnp.bfloat16))
    rank = jnp.sum(jnp.where(onehot, running, 0.0), axis=1, keepdims=True) - 1.0
    first_row = choices.astype(jnp.float32) * (2.0 * capacity) + rank
    first_row = jnp.broadcast_to(first_row, (total, 128)).T[0:1].astype(jnp.int32)
    low_row = first_row + capacity * tower
    high_row = first_row + capacity * (1 - tower)
    more = choices.astype(jnp.float32) * jnp.float32(return_rows - 2 * capacity)
    more = jnp.broadcast_to(more, (total, 128)).T[0:1].astype(jnp.int32)
    out[1][0:1] = low_row
    out[1][1:2] = high_row
    out[1][2:3] = low_row + more
    out[1][3:4] = high_row + more
    send(1)
    placed(low_row, high_row, need(1), out, send)


def placed(low_row, high_row, values, out, send):
    count, half = out[0].shape
    ids = lax.broadcasted_iota(jnp.int32, (count, values.shape[0]), 0)
    low_place = (ids == low_row).astype(jnp.bfloat16)
    high_place = (ids == high_row).astype(jnp.bfloat16)
    rows = product(low_place, values[:, :half]) + product(high_place, values[:, half:])
    out[0][...] = rows.astype(jnp.bfloat16)
    send(0)


def place_step(need, out, send):
    maps = need(0)
    placed(maps[0:1], maps[1:2], need(1), out, send)


def token_step(experts, column_row, need, out, send):
    rows_of = need(0)
    rows = need(1)[...]
    count, half = rows.shape
    total = out[0].shape[0]
    ids = lax.broadcasted_iota(jnp.int32, (count, total), 0)
    for part in range(2):
        place = (ids == rows_of[2 + part : 3 + part]).astype(jnp.float32).T.astype(jnp.bfloat16)
        out[0][:, part * half : (part + 1) * half] = product(place, rows).astype(jnp.bfloat16)
    send(0)
    words = rows.astype(jnp.float32).reshape(experts, count // experts, half)
    for part in range(2):
        sums = words[:, column_row + part, :] + words[:, column_row + 2 + part, :]
        out[1][:, part * half : (part + 1) * half] = sums
    send(1)


def taken(rows, slot_of_row, slots):
    ids = lax.broadcasted_iota(jnp.int32, (slots, rows.shape[0]), 0)
    return product((ids == slot_of_row).astype(jnp.bfloat16), rows)


def feature_mean(first, second, width):
    total = jnp.sum(first, axis=1, keepdims=True) + jnp.sum(second, axis=1, keepdims=True)
    return total / width


def spread_lanes(column):
    return jnp.broadcast_to(column, (column.shape[0], 128))


def front(normed, up_pair, out, send, base):
    preact = product(normed[...], up_pair[...])
    gelu, slope = gelu_pair(preact)
    out[base][...] = slope.astype(jnp.bfloat16)
    send(base)
    out[base + 1][...] = gelu.astype(jnp.bfloat16)
    send(base + 1)
    out[base + 2][...] = gelu.T.astype(jnp.bfloat16)
    send(base + 2)


def norm_step(shards, need, out, send):
    slots, width = out[0].shape
    half = width // 2
    maps, rows = need(0), need(1)[...]
    first, second = (taken(rows, maps[part : part + 1], slots) for part in range(2))
    mean = feature_mean(first, second, width)
    first, second = first - mean, second - mean
    root = lax.rsqrt(feature_mean(first * first, second * second, width) + epsilon)
    first, second = first * root, second * root
    out[1][:, :half] = first.astype(jnp.bfloat16)
    out[1][:, half:] = second.astype(jnp.bfloat16)
    send(1)
    gain, column = need(2), need(3)
    first = (first * gain[0:1]).astype(jnp.bfloat16)
    second = (second * gain[1:2]).astype(jnp.bfloat16)
    out[0][:, :half] = first
    out[0][:, half:] = second
    send(0)
    logits = jnp.sum(first.astype(jnp.float32) * column[0:1], axis=1, keepdims=True) + jnp.sum(
        second.astype(jnp.float32) * column[1:2], axis=1, keepdims=True
    )
    out[2][0] = spread_lanes(root)
    out[2][1] = spread_lanes(jax.nn.sigmoid(logits))
    send(2)
    for shard in range(shards):
        front(out[0], need(4 + 2 * shard), out, send, 3 + 3 * shard)


def front_step(need, out, send):
    front(need(0), need(1), out, send, 0)


def gate_step(need, out, send):
    slots, width = out[0].shape
    half = width // 2
    maps, rows = need(0), need(1)[...]
    gates = need(2)[1][:, 0:1]
    for part in range(2):
        values = taken(rows, maps[part : part + 1], slots)
        out[0][:, part * half : (part + 1) * half] = values.astype(jnp.bfloat16)
        out[1][:, part * half : (part + 1) * half] = (gates * values).astype(jnp.bfloat16)
    send(0)
    send(1)
    for term in range((len(out) - 2) // 2):
        down_term(need(3 + term), out[1], out, send, 2 + 2 * term)


def down_term(turned, output, out, send, base):
    half = out[base].shape[1]
    terms = product(turned[...], output[...])
    out[base + 1][...] = terms[:, half:].astype(jnp.bfloat16)
    send(base + 1)
    out[base][...] = terms[:, :half].astype(out[base].dtype)
    send(base)


def hidden_step(shards, need, out, send, tower_ref):
    output = need(0)
    half = output.shape[1] // 2
    gated = None
    for shard in range(shards):
        base = 1 + 4 * shard
        hidden_grad = contracted_columns(output[...], need(base)[...])
        term = jnp.sum(
            need(base + 3)[...].astype(jnp.float32) * hidden_grad, axis=1, keepdims=True
        )
        gated = term if gated is None else gated + term
        out[2 + shard][...] = (hidden_grad * need(base + 2)[...].astype(jnp.float32)).astype(jnp.bfloat16)
        send(2 + shard)
    base = 1 + 4 * shards
    logit_grad = gated * (1.0 - need(base)[1][:, 0:1])
    out[0][...] = spread_lanes(logit_grad)
    send(0)
    normed = need(base + 1)
    sums = [
        jnp.sum(
            normed[:, part * half : (part + 1) * half].astype(jnp.float32) * logit_grad,
            axis=0,
            keepdims=True,
        )
        for part in range(2)
    ]
    in_order = tower_ref[0] == 0
    out[1][0:1] = jnp.where(in_order, sums[0], sums[1])
    out[1][1:2] = jnp.where(in_order, sums[1], sums[0])
    send(1)


def back_step(shards, need, out, send, total):
    count, half = out[0].shape
    width = 2 * half
    for shard in range(shards):
        grad = need(3 * shard)[...]
        term = contracted_columns(grad, need(3 * shard + 1)[...])
        if shard == 0:
            total[...] = term
        else:
            total[...] += term
    base = 3 * shards
    logit_grad = need(base)[:, 0:1]
    unit, cotan, root = need(base + 1), need(base + 2), need(base + 3)[0][:, 0:1]
    row_of_slot, gain, column = need(base + 4), need(base + 5), need(base + 6)
    first = (total[:, :half] + logit_grad * column[0:1]) * gain[0:1]
    second = (total[:, half:] + logit_grad * column[1:2]) * gain[1:2]
    unit_first = unit[:, :half].astype(jnp.float32)
    unit_second = unit[:, half:].astype(jnp.float32)
    grad_mean = feature_mean(first, second, width)
    grad_unit = feature_mean(first * unit_first, second * unit_second, width)
    first = cotan[:, :half].astype(jnp.float32) + root * (
        first - grad_mean - unit_first * grad_unit
    )
    second = cotan[:, half:].astype(jnp.float32) + root * (
        second - grad_mean - unit_second * grad_unit
    )
    ids = lax.broadcasted_iota(jnp.int32, (count, row_of_slot.shape[1]), 0)
    rows = product(
        (ids == row_of_slot[0:1]).astype(jnp.bfloat16), first.astype(jnp.bfloat16)
    ) + product((ids == row_of_slot[1:2]).astype(jnp.bfloat16), second.astype(jnp.bfloat16))
    out[0][...] = rows.astype(jnp.bfloat16)
    send(0)


def tail_kernel(column_ref, rows_ref, into_ref, tail, sem):
    experts, more, half = tail.shape
    words = column_ref[...]
    high = words.astype(jnp.bfloat16).astype(jnp.float32)
    block = jnp.concatenate([high, words - high, jnp.zeros((more - 4, half), jnp.float32)])
    tail[...] = jnp.broadcast_to(block[None], tail.shape).astype(jnp.bfloat16)
    copy = pltpu.make_async_copy(tail, into_ref.at[:, pl.ds(into_ref.shape[1] - more, more)], sem)
    copy.start()
    copy.wait()


def joined_kernel(tower_ref, own_ref, other_ref, whole_ref):
    half = own_ref.shape[1]
    own_at = pl.multiple_of(tower_ref[0] * half, 128)
    other_at = pl.multiple_of((1 - tower_ref[0]) * half, 128)
    whole_ref[:, pl.ds(own_at, half)] = own_ref[...]
    whole_ref[:, pl.ds(other_at, half)] = other_ref[...]


def pair_rows(embeds):
    own_rows = embeds[0].astype(jnp.float32)
    local_member = (
        own_rows * lax.rsqrt(jnp.sum(own_rows * own_rows, axis=-1, keepdims=True) + epsilon)
    ).astype(jnp.bfloat16)
    return local_member, exchanged(local_member, "tower", 1)


def pair_grads(local_member, panel_rows, logit_scale_log, pairwise_logit_bias, dp_index):
    softness_factor = jnp.exp(logit_scale_log)
    row_count = local_member.shape[0]
    row_global = dp_index * row_count + jnp.arange(row_count, dtype=jnp.int32)
    pair_scores = (
        softness_factor * contracted_columns(local_member, panel_rows) + pairwise_logit_bias
    )
    col_global = jnp.arange(panel_rows.shape[0], dtype=jnp.int32)
    pair_labels = jnp.where(row_global[:, None] == col_global[None, :], 1.0, -1.0).astype(
        jnp.float32
    )
    panel_weights = (
        -pair_labels * jax.nn.sigmoid(-pair_labels * pair_scores) * softness_factor
    ).astype(jnp.bfloat16)
    return product(panel_weights, panel_rows)


def body(
    tokens,
    norm_gain,
    router,
    expert_ids,
    up_weights,
    down_weights,
    cotangent,
    embeds,
    logit_scale_log,
    pairwise_logit_bias,
):
    token_total, width = tokens.shape
    hidden = up_weights.shape[1]
    experts = router.shape[1]
    capacity = 3 * token_total // (2 * experts)
    half = width // 2
    slots = experts * capacity
    tower = lax.axis_index("tower")
    expert = lax.axis_index("z") * columns + lax.axis_index("x")
    dp_index = expert * line + lax.axis_index("y")
    bf16, f32 = jnp.bfloat16, jnp.float32

    def halves(values, axis):
        return (
            lax.dynamic_slice_in_dim(values, tower * half, half, axis),
            lax.dynamic_slice_in_dim(values, (1 - tower) * half, half, axis),
        )

    up_own, down_own = halves(up_weights, 0), halves(down_weights, 1)
    up_before, up_after = shifted(up_own[0], "y", 1), shifted(up_own[0], "y", -1)

    tower_word = tower.astype(jnp.int32).reshape(1)
    return_rows = 2 * capacity + 8
    sent_ids = jnp.arange(2 * slots, dtype=jnp.int32)
    slot_of_sent = sent_ids // (2 * capacity) * capacity + sent_ids % capacity
    in_first = sent_ids % (2 * capacity) < capacity
    slot_maps = jnp.stack(
        [jnp.where(in_first, slot_of_sent, -1), jnp.where(in_first, -1, slot_of_sent)]
    )
    slot_ids = jnp.arange(slots, dtype=jnp.int32)
    first_row = slot_ids // capacity * return_rows + slot_ids % capacity
    row_maps = jnp.stack([first_row, first_row + capacity])

    def spread(rows):
        return lax.all_to_all(
            rows.reshape(experts, -1, half),
            ("z", "x"),
            split_axis=0,
            concat_axis=0,
            tiled=True,
        ).reshape(-1, half)

    def both(piece):
        return piece, exchanged(piece, "tower", 1)

    token_rows, token_maps = staged_call(
        functools.partial(slot_step, capacity, experts, return_rows),
        [shape_of((2 * slots, half), bf16), shape_of((4, token_total), jnp.int32)],
        (expert_ids, tokens),
        16,
        scalars=(tower_word,),
    )
    late_maps, up_before, up_after = lax.optimization_barrier((token_maps, up_before, up_after))
    cotan_rows = staged_call(
        place_step, [shape_of((2 * slots, half), bf16)], (late_maps, cotangent), 16
    )[0]
    down_part, up_before, up_after, cotan_rows = lax.optimization_barrier(
        (down_own[0], up_before, up_after, cotan_rows)
    )
    down_before, down_after = shifted(down_part, "y", 1), shifted(down_part, "y", -1)
    up_before, down_before, down_after = lax.optimization_barrier(
        (up_before, down_before, down_after)
    )
    up_across, down_across = shifted(up_before, "y", 1), shifted(down_after, "y", -1)

    local_member, other_member = pair_rows(embeds)
    token_rows, other_member = lax.optimization_barrier((token_rows, other_member))
    panel_rows = lax.all_gather(other_member, ("z", "x", "y"), axis=0, tiled=True)
    token_rows = spread(token_rows)
    cotan_rows, token_rows = lax.optimization_barrier((cotan_rows, token_rows))
    cotan_rows = spread(cotan_rows)
    ups = [up_own] + [both(piece) for piece in (up_before, up_after, up_across)]
    downs = [down_own] + [both(piece) for piece in (down_before, down_after, down_across)]

    def features(values):
        return jnp.concatenate(halves(values.astype(f32)[None, :], 1), axis=0)

    gain = features(norm_gain)
    column = features(lax.dynamic_slice_in_dim(router, expert, 1, 1)[:, 0])
    shards, near = len(ups), len(ups) - 1
    front_shapes = [
        shape_of((slots, hidden), bf16),
        shape_of((slots, hidden), bf16),
        shape_of((hidden, slots), bf16),
    ]
    term_shapes = [shape_of((hidden, half), bf16)] * 2
    own_shapes = [shape_of((hidden, half), f32), shape_of((hidden, half), bf16)]
    token_rows, _, _ = lax.optimization_barrier((token_rows, down_before, down_after))
    normed, unit, scales, *near_fronts = staged_call(
        functools.partial(norm_step, near),
        [shape_of((slots, width), bf16)] * 2
        + [shape_of((2, slots, 128), f32)]
        + front_shapes * near,
        (slot_maps, token_rows, gain, column, *(p for pair in ups[:near] for p in pair)),
        32,
        1 << 34,
        joint=[(4 + 2 * k, 0) for k in range(near)],
    )
    fronts = [near_fronts[3 * k : 3 * k + 3] for k in range(near)]
    fronts.append(staged_call(front_step, front_shapes, (normed,) + ups[near], 16, joint=[(1, 0)]))
    cotan_rows, across_turned = lax.optimization_barrier((cotan_rows, fronts[near][2]))
    cotan, output, *terms = staged_call(
        gate_step,
        [shape_of((slots, width), bf16)] * 2 + term_shapes * near + own_shapes,
        (slot_maps, cotan_rows, scales, fronts[1][2], fronts[2][2], across_turned, fronts[0][2]),
        32,
    )
    logit_grad, router_halves, *preact_grads = staged_call(
        functools.partial(hidden_step, shards),
        [shape_of((slots, 128), f32), shape_of((2, half), f32)]
        + [shape_of((slots, hidden), bf16)] * shards,
        (output, *(p for k in range(shards) for p in (*downs[k], *fronts[k][:2])), scales, normed),
        28,
        scalars=(tower_word,),
        joint=[(1 + 4 * k, 1) for k in range(shards)],
    )

    def half_sum(first, swapped):
        return first.astype(f32) + swapped.astype(f32)

    swapped = [exchanged(terms[2 * term + 1], "tower", 1) for term in range(shards)]
    down_across = half_sum(terms[2 * near - 2], swapped[near - 1]).astype(bf16)
    router_column = router_halves
    router_column = router_column + exchanged(router_column, "tower", 1)
    logit_grad, router_column, down_across, swapped = lax.optimization_barrier(
        (logit_grad, router_column, down_across, swapped)
    )
    down_across = shifted(down_across, "y", 2)
    beside, beyond, farthest = (exchanged(router_column, "y", bit) for bit in (1, 2, 3))
    router_column = (router_column + beside) + (beyond + farthest)
    back_rows = staged_call(
        functools.partial(back_step, shards),
        [shape_of((experts * return_rows, half), bf16)],
        tuple(p for k in range(shards) for p in (preact_grads[k], *ups[k]))
        + (logit_grad, unit, cotan, scales, row_maps, gain, column),
        32,
        16 * shards * slots * width * hidden,
        scratch=[pltpu.VMEM((slots, width), f32)],
        joint=[(3 * k + 1, 0) for k in range(shards)],
    )[0]
    back_rows = local_call(
        tail_kernel,
        [pltpu.HBM((experts, return_rows, half), bf16)],
        (
            router_column,
            pltpu.with_memory_space_constraint(
                back_rows.reshape(experts, return_rows, half), pltpu.HBM
            ),
        ),
        8,
        in_specs=[
            pl.BlockSpec(memory_space=pltpu.VMEM),
            pl.BlockSpec(memory_space=pltpu.HBM),
        ],
        out_specs=[pl.BlockSpec(memory_space=pltpu.HBM)],
        input_output_aliases={1: 0},
        scratch_shapes=[
            pltpu.VMEM((experts, return_rows - 2 * capacity, half), bf16),
            pltpu.SemaphoreType.DMA,
        ],
    )[0]
    returned = spread(back_rows)
    swapped, down_across, _ = lax.optimization_barrier((swapped, down_across, back_rows))
    down_before = shifted(half_sum(terms[0], swapped[0]).astype(bf16), "y", -1)
    down_after = shifted(half_sum(terms[2], swapped[1]).astype(bf16), "y", 1)
    panel_rows, down_before = lax.optimization_barrier((panel_rows, down_before))
    embed_grads = pair_grads(
        local_member, panel_rows, logit_scale_log, pairwise_logit_bias, dp_index
    )
    down_half = (
        half_sum(terms[2 * near], swapped[near])
        + down_before.astype(f32)
        + down_after.astype(f32)
        + down_across.astype(f32)
    )
    down_other = exchanged(down_half, "tower", 1)
    whole = pl.BlockSpec(memory_space=pltpu.VMEM)
    down_grad = local_call(
        joined_kernel,
        [shape_of((hidden, width), f32)],
        (tower_word, down_half, down_other),
        16,
        in_specs=[pl.BlockSpec(memory_space=pltpu.SMEM), whole, whole],
    )[0]
    embed_grads, token_maps = lax.optimization_barrier((embed_grads, token_maps))
    tokens_grad, router_rows = staged_call(
        functools.partial(token_step, experts, 2 * capacity),
        [shape_of((token_total, width), bf16), shape_of((experts, width), f32)],
        (token_maps, returned),
        20,
        1 << 34,
    )
    return (tokens_grad, router_rows.T, down_grad, embed_grads[None])


def solution(mesh):
    towers, chips = mesh.devices.shape
    grid = Mesh(
        mesh.devices.reshape(towers, chips // (columns * line), columns, line),
        ("tower", "z", "x", "y"),
    )
    dp = ("z", "x", "y")
    rows = P(("tower",) + dp, None)
    placed = (
        rows,
        P(),
        P(),
        rows,
        P(None, dp),
        P(dp, None),
        rows,
        P("tower", dp, None),
        P(),
        P(),
    )
    return jax.shard_map(
        body,
        mesh=grid,
        in_specs=placed,
        out_specs=(rows, P(), P(dp, None), P("tower", dp, None)),
        check_vma=False,
    )
```

```python
import functools

import jax
import jax.numpy as jnp
from jax import lax
from jax.experimental import pallas as pl
from jax.experimental.pallas import tpu as pltpu
from jax.sharding import Mesh, PartitionSpec as P

epsilon = 1e-06
gelu_root = 0.7978845608028654
gelu_cubic = 0.044715

line = 4
columns = 4


def shifted(block, axis, step):
    count = lax.axis_size(axis)
    return lax.ppermute(block, axis, [(i, (i + step) % count) for i in range(count)])


def exchanged(block, axis, bit):
    count = lax.axis_size(axis)
    return lax.ppermute(block, axis, [(i, i ^ bit) for i in range(count)])


def product(left, right):
    return jnp.dot(left, right, preferred_element_type=jnp.float32)


def contract_rows(left, right):
    return lax.dot_general(
        left, right, (((0,), (0,)), ((), ())), preferred_element_type=jnp.float32
    )


def contracted_columns(left, right):
    return lax.dot_general(
        left, right, (((1,), (1,)), ((), ())), preferred_element_type=jnp.float32
    )


def gelu_pair(values):
    inner = gelu_root * (values + gelu_cubic * values * values * values)
    tangent = jnp.tanh(inner)
    slope = 0.5 * (1.0 + tangent) + 0.5 * values * (1.0 - tangent * tangent) * gelu_root * (
        1.0 + 3.0 * gelu_cubic * values * values
    )
    return 0.5 * values * (1.0 + tangent), slope


def local_call(kernel, out_shape, operands, vmem, flops=1, **options):
    return pl.pallas_call(
        kernel,
        out_shape=out_shape,
        compiler_params=pltpu.CompilerParams(vmem_limit_bytes=vmem << 20),
        cost_estimate=pl.CostEstimate(flops=flops, bytes_accessed=1, transcendentals=0),
        **options,
    )(*operands)


def shape_of(shape, dtype):
    return jax.ShapeDtypeStruct(shape, dtype)


def staged_call(run, out_shape, operands, vmem, flops=1, scalars=(), scratch=(), joint=()):
    fixed, count, results = len(scalars), len(operands), len(out_shape)
    joint = dict(joint)
    places, buffers = [], []
    for i, value in enumerate(operands):
        if i - 1 in joint:
            places.append((len(buffers) - 1, 1))
        else:
            shape = list(value.shape)
            if i in joint:
                shape[joint[i]] *= 2
            places.append((len(buffers), 0))
            buffers.append(pltpu.VMEM(tuple(shape), value.dtype))

    def kernel(*refs):
        numbers, refs = refs[:fixed], refs[fixed:]
        sources, refs = refs[:count], refs[count:]
        targets, refs = refs[:results], refs[results:]
        held, refs = refs[: len(buffers)], refs[len(buffers) :]
        out, refs = refs[:results], refs[results:]
        in_sems, out_sems, rest = refs[0], refs[1], refs[2:]

        def target(i):
            at, part = places[i]
            first = i - part
            if first not in joint:
                return held[at]
            extent = sources[i].shape[joint[first]]
            window = pl.ds(part * extent, extent)
            return held[at].at[window] if joint[first] == 0 else held[at].at[:, window]

        fetched = [
            pltpu.make_async_copy(sources[i], target(i), in_sems.at[i]) for i in range(count)
        ]
        sent = [
            pltpu.make_async_copy(out[j], targets[j], out_sems.at[j]) for j in range(results)
        ]
        for copy in fetched:
            copy.start()
        arrived = set()

        def need(i):
            if i not in arrived:
                fetched[i].wait()
                if i in joint:
                    fetched[i + 1].wait()
                arrived.add(i)
            return held[places[i][0]]

        run(need, out, lambda j: sent[j].start(), *numbers, *rest)
        for copy in sent:
            copy.wait()

    apart = pl.BlockSpec(memory_space=pltpu.HBM)
    pinned = [pltpu.with_memory_space_constraint(v, pltpu.HBM) for v in operands]
    return local_call(
        kernel,
        [pltpu.HBM(v.shape, v.dtype) for v in out_shape],
        (*scalars, *pinned),
        vmem,
        flops,
        in_specs=[pl.BlockSpec(memory_space=pltpu.SMEM)] * fixed + [apart] * count,
        out_specs=[apart] * results,
        scratch_shapes=buffers
        + [pltpu.VMEM(v.shape, v.dtype) for v in out_shape]
        + [pltpu.SemaphoreType.DMA((count,)), pltpu.SemaphoreType.DMA((results,))]
        + list(scratch),
    )


def slot_step(capacity, experts, return_rows, need, out, send, tower_ref):
    tower = tower_ref[0]
    choices = need(0)[...]
    total = choices.shape[0]
    onehot = choices == lax.broadcasted_iota(jnp.int32, (total, experts), 1)
    lower_tri = lax.broadcasted_iota(jnp.int32, (total, total), 0) >= lax.broadcasted_iota(
        jnp.int32, (total, total), 1
    )
    running = product(lower_tri.astype(jnp.bfloat16), onehot.astype(jnp.bfloat16))
    rank = jnp.sum(jnp.where(onehot, running, 0.0), axis=1, keepdims=True) - 1.0
    first_row = choices.astype(jnp.float32) * (2.0 * capacity) + rank
    first_row = jnp.broadcast_to(first_row, (total, 128)).T[0:1].astype(jnp.int32)
    low_row = first_row + capacity * tower
    high_row = first_row + capacity * (1 - tower)
    more = choices.astype(jnp.float32) * jnp.float32(return_rows - 2 * capacity)
    more = jnp.broadcast_to(more, (total, 128)).T[0:1].astype(jnp.int32)
    out[1][0:1] = low_row
    out[1][1:2] = high_row
    out[1][2:3] = low_row + more
    out[1][3:4] = high_row + more
    send(1)
    placed(low_row, high_row, need(1), out, send)


def placed(low_row, high_row, values, out, send):
    count, half = out[0].shape
    ids = lax.broadcasted_iota(jnp.int32, (count, values.shape[0]), 0)
    low_place = (ids == low_row).astype(jnp.bfloat16)
    high_place = (ids == high_row).astype(jnp.bfloat16)
    rows = product(low_place, values[:, :half]) + product(high_place, values[:, half:])
    out[0][...] = rows.astype(jnp.bfloat16)
    send(0)


def place_step(need, out, send):
    maps = need(0)
    placed(maps[0:1], maps[1:2], need(1), out, send)


def token_step(experts, column_row, need, out, send):
    rows_of = need(0)
    rows = need(1)[...]
    count, half = rows.shape
    total = out[0].shape[0]
    ids = lax.broadcasted_iota(jnp.int32, (count, total), 0)
    for part in range(2):
        place = (ids == rows_of[2 + part : 3 + part]).astype(jnp.float32).T.astype(jnp.bfloat16)
        out[0][:, part * half : (part + 1) * half] = product(place, rows).astype(jnp.bfloat16)
    send(0)
    words = rows.astype(jnp.float32).reshape(experts, count // experts, half)
    for part in range(2):
        sums = words[:, column_row + part, :] + words[:, column_row + 2 + part, :]
        out[1][:, part * half : (part + 1) * half] = sums
    send(1)


def taken(rows, slot_of_row, slots):
    ids = lax.broadcasted_iota(jnp.int32, (slots, rows.shape[0]), 0)
    return product((ids == slot_of_row).astype(jnp.bfloat16), rows)


def feature_mean(first, second, width):
    total = jnp.sum(first, axis=1, keepdims=True) + jnp.sum(second, axis=1, keepdims=True)
    return total / width


def spread_lanes(column):
    return jnp.broadcast_to(column, (column.shape[0], 128))


def front(normed, up_pair, out, send, base):
    preact = product(normed[...], up_pair[...])
    gelu, slope = gelu_pair(preact)
    out[base][...] = slope.astype(jnp.bfloat16)
    send(base)
    out[base + 1][...] = gelu.astype(jnp.bfloat16)
    send(base + 1)
    out[base + 2][...] = gelu.T.astype(jnp.bfloat16)
    send(base + 2)


def norm_step(shards, need, out, send):
    slots, width = out[0].shape
    half = width // 2
    maps, rows = need(0), need(1)[...]
    first, second = (taken(rows, maps[part : part + 1], slots) for part in range(2))
    mean = feature_mean(first, second, width)
    first, second = first - mean, second - mean
    root = lax.rsqrt(feature_mean(first * first, second * second, width) + epsilon)
    first, second = first * root, second * root
    out[1][:, :half] = first.astype(jnp.bfloat16)
    out[1][:, half:] = second.astype(jnp.bfloat16)
    send(1)
    gain, column = need(2), need(3)
    first = (first * gain[0:1]).astype(jnp.bfloat16)
    second = (second * gain[1:2]).astype(jnp.bfloat16)
    out[0][:, :half] = first
    out[0][:, half:] = second
    send(0)
    logits = jnp.sum(first.astype(jnp.float32) * column[0:1], axis=1, keepdims=True) + jnp.sum(
        second.astype(jnp.float32) * column[1:2], axis=1, keepdims=True
    )
    out[2][0] = spread_lanes(root)
    out[2][1] = spread_lanes(jax.nn.sigmoid(logits))
    send(2)
    for shard in range(shards):
        front(out[0], need(4 + 2 * shard), out, send, 3 + 3 * shard)


def front_step(need, out, send):
    front(need(0), need(1), out, send, 0)


def gate_step(need, out, send):
    slots, width = out[0].shape
    half = width // 2
    maps, rows = need(0), need(1)[...]
    gates = need(2)[1][:, 0:1]
    for part in range(2):
        values = taken(rows, maps[part : part + 1], slots)
        out[0][:, part * half : (part + 1) * half] = values.astype(jnp.bfloat16)
        out[1][:, part * half : (part + 1) * half] = (gates * values).astype(jnp.bfloat16)
    send(0)
    send(1)
    for term in range((len(out) - 2) // 2):
        down_term(need(3 + term), out[1], out, send, 2 + 2 * term)


def down_term(turned, output, out, send, base):
    half = out[base].shape[1]
    terms = product(turned[...], output[...])
    out[base + 1][...] = terms[:, half:].astype(jnp.bfloat16)
    send(base + 1)
    out[base][...] = terms[:, :half].astype(out[base].dtype)
    send(base)


def hidden_step(shards, need, out, send, tower_ref):
    output = need(0)
    half = output.shape[1] // 2
    gated = None
    for shard in range(shards):
        base = 1 + 4 * shard
        hidden_grad = contracted_columns(output[...], need(base)[...])
        term = jnp.sum(
            need(base + 3)[...].astype(jnp.float32) * hidden_grad, axis=1, keepdims=True
        )
        gated = term if gated is None else gated + term
        out[2 + shard][...] = (hidden_grad * need(base + 2)[...].astype(jnp.float32)).astype(jnp.bfloat16)
        send(2 + shard)
    base = 1 + 4 * shards
    logit_grad = gated * (1.0 - need(base)[1][:, 0:1])
    out[0][...] = spread_lanes(logit_grad)
    send(0)
    normed = need(base + 1)
    sums = [
        jnp.sum(
            normed[:, part * half : (part + 1) * half].astype(jnp.float32) * logit_grad,
            axis=0,
            keepdims=True,
        )
        for part in range(2)
    ]
    in_order = tower_ref[0] == 0
    out[1][0:1] = jnp.where(in_order, sums[0], sums[1])
    out[1][1:2] = jnp.where(in_order, sums[1], sums[0])
    send(1)


def back_step(shards, need, out, send, total):
    count, half = out[0].shape
    width = 2 * half
    for shard in range(shards):
        grad = need(3 * shard)[...]
        term = contracted_columns(grad, need(3 * shard + 1)[...])
        if shard == 0:
            total[...] = term
        else:
            total[...] += term
    base = 3 * shards
    logit_grad = need(base)[:, 0:1]
    unit, cotan, root = need(base + 1), need(base + 2), need(base + 3)[0][:, 0:1]
    row_of_slot, gain, column = need(base + 4), need(base + 5), need(base + 6)
    first = (total[:, :half] + logit_grad * column[0:1]) * gain[0:1]
    second = (total[:, half:] + logit_grad * column[1:2]) * gain[1:2]
    unit_first = unit[:, :half].astype(jnp.float32)
    unit_second = unit[:, half:].astype(jnp.float32)
    grad_mean = feature_mean(first, second, width)
    grad_unit = feature_mean(first * unit_first, second * unit_second, width)
    first = cotan[:, :half].astype(jnp.float32) + root * (
        first - grad_mean - unit_first * grad_unit
    )
    second = cotan[:, half:].astype(jnp.float32) + root * (
        second - grad_mean - unit_second * grad_unit
    )
    ids = lax.broadcasted_iota(jnp.int32, (count, row_of_slot.shape[1]), 0)
    rows = product(
        (ids == row_of_slot[0:1]).astype(jnp.bfloat16), first.astype(jnp.bfloat16)
    ) + product((ids == row_of_slot[1:2]).astype(jnp.bfloat16), second.astype(jnp.bfloat16))
    out[0][...] = rows.astype(jnp.bfloat16)
    send(0)


def tail_kernel(column_ref, rows_ref, into_ref, tail, sem):
    experts, more, half = tail.shape
    words = column_ref[...]
    high = words.astype(jnp.bfloat16).astype(jnp.float32)
    block = jnp.concatenate([high, words - high, jnp.zeros((more - 4, half), jnp.float32)])
    tail[...] = jnp.broadcast_to(block[None], tail.shape).astype(jnp.bfloat16)
    copy = pltpu.make_async_copy(tail, into_ref.at[:, pl.ds(into_ref.shape[1] - more, more)], sem)
    copy.start()
    copy.wait()


def joined_kernel(tower_ref, own_ref, other_ref, whole_ref):
    half = own_ref.shape[1]
    own_at = pl.multiple_of(tower_ref[0] * half, 128)
    other_at = pl.multiple_of((1 - tower_ref[0]) * half, 128)
    whole_ref[:, pl.ds(own_at, half)] = own_ref[...]
    whole_ref[:, pl.ds(other_at, half)] = other_ref[...]


def pair_rows(embeds):
    own_rows = embeds[0].astype(jnp.float32)
    local_member = (
        own_rows * lax.rsqrt(jnp.sum(own_rows * own_rows, axis=-1, keepdims=True) + epsilon)
    ).astype(jnp.bfloat16)
    return local_member, exchanged(local_member, "tower", 1)


def pair_grads(local_member, panel_rows, logit_scale_log, pairwise_logit_bias, dp_index):
    softness_factor = jnp.exp(logit_scale_log)
    row_count = local_member.shape[0]
    row_global = dp_index * row_count + jnp.arange(row_count, dtype=jnp.int32)
    pair_scores = (
        softness_factor * contracted_columns(local_member, panel_rows) + pairwise_logit_bias
    )
    col_global = jnp.arange(panel_rows.shape[0], dtype=jnp.int32)
    pair_labels = jnp.where(row_global[:, None] == col_global[None, :], 1.0, -1.0).astype(
        jnp.float32
    )
    panel_weights = (
        -pair_labels * jax.nn.sigmoid(-pair_labels * pair_scores) * softness_factor
    ).astype(jnp.bfloat16)
    return product(panel_weights, panel_rows)


def body(
    tokens,
    norm_gain,
    router,
    expert_ids,
    up_weights,
    down_weights,
    cotangent,
    embeds,
    logit_scale_log,
    pairwise_logit_bias,
):
    token_total, width = tokens.shape
    hidden = up_weights.shape[1]
    experts = router.shape[1]
    capacity = 3 * token_total // (2 * experts)
    half = width // 2
    slots = experts * capacity
    tower = lax.axis_index("tower")
    expert = lax.axis_index("z") * columns + lax.axis_index("x")
    dp_index = expert * line + lax.axis_index("y")
    bf16, f32 = jnp.bfloat16, jnp.float32

    def halves(values, axis):
        return (
            lax.dynamic_slice_in_dim(values, tower * half, half, axis),
            lax.dynamic_slice_in_dim(values, (1 - tower) * half, half, axis),
        )

    up_own, down_own = halves(up_weights, 0), halves(down_weights, 1)
    up_before, up_after = shifted(up_own[0], "y", 1), shifted(up_own[0], "y", -1)

    tower_word = tower.astype(jnp.int32).reshape(1)
    return_rows = 2 * capacity + 8
    sent_ids = jnp.arange(2 * slots, dtype=jnp.int32)
    slot_of_sent = sent_ids // (2 * capacity) * capacity + sent_ids % capacity
    in_first = sent_ids % (2 * capacity) < capacity
    slot_maps = jnp.stack(
        [jnp.where(in_first, slot_of_sent, -1), jnp.where(in_first, -1, slot_of_sent)]
    )
    slot_ids = jnp.arange(slots, dtype=jnp.int32)
    first_row = slot_ids // capacity * return_rows + slot_ids % capacity
    row_maps = jnp.stack([first_row, first_row + capacity])

    def spread(rows):
        return lax.all_to_all(
            rows.reshape(experts, -1, half),
            ("z", "x"),
            split_axis=0,
            concat_axis=0,
            tiled=True,
        ).reshape(-1, half)

    def both(piece):
        return piece, exchanged(piece, "tower", 1)

    token_rows, token_maps = staged_call(
        functools.partial(slot_step, capacity, experts, return_rows),
        [shape_of((2 * slots, half), bf16), shape_of((4, token_total), jnp.int32)],
        (expert_ids, tokens),
        16,
        scalars=(tower_word,),
    )
    late_maps, up_before, up_after = lax.optimization_barrier((token_maps, up_before, up_after))
    cotan_rows = staged_call(
        place_step, [shape_of((2 * slots, half), bf16)], (late_maps, cotangent), 16
    )[0]
    down_part, up_before, up_after, cotan_rows = lax.optimization_barrier(
        (down_own[0], up_before, up_after, cotan_rows)
    )
    down_before, down_after = shifted(down_part, "y", 1), shifted(down_part, "y", -1)
    up_before, down_before, down_after = lax.optimization_barrier(
        (up_before, down_before, down_after)
    )
    up_across, down_across = shifted(up_before, "y", 1), shifted(down_after, "y", -1)

    local_member, other_member = pair_rows(embeds)
    token_rows, other_member = lax.optimization_barrier((token_rows, other_member))
    panel_rows = lax.all_gather(other_member, ("z", "x", "y"), axis=0, tiled=True)
    token_rows = spread(token_rows)
    cotan_rows, token_rows = lax.optimization_barrier((cotan_rows, token_rows))
    cotan_rows = spread(cotan_rows)
    ups = [up_own] + [both(piece) for piece in (up_before, up_after, up_across)]
    downs = [down_own] + [both(piece) for piece in (down_before, down_after, down_across)]

    def features(values):
        return jnp.concatenate(halves(values.astype(f32)[None, :], 1), axis=0)

    gain = features(norm_gain)
    column = features(lax.dynamic_slice_in_dim(router, expert, 1, 1)[:, 0])
    shards, near = len(ups), len(ups) - 1
    front_shapes = [
        shape_of((slots, hidden), bf16),
        shape_of((slots, hidden), bf16),
        shape_of((hidden, slots), bf16),
    ]
    term_shapes = [shape_of((hidden, half), bf16)] * 2
    own_shapes = [shape_of((hidden, half), f32), shape_of((hidden, half), bf16)]
    token_rows, _, _ = lax.optimization_barrier((token_rows, down_before, down_after))
    normed, unit, scales, *near_fronts = staged_call(
        functools.partial(norm_step, near),
        [shape_of((slots, width), bf16)] * 2
        + [shape_of((2, slots, 128), f32)]
        + front_shapes * near,
        (slot_maps, token_rows, gain, column, *(p for pair in ups[:near] for p in pair)),
        32,
        1 << 34,
        joint=[(4 + 2 * k, 0) for k in range(near)],
    )
    fronts = [near_fronts[3 * k : 3 * k + 3] for k in range(near)]
    fronts.append(staged_call(front_step, front_shapes, (normed,) + ups[near], 16, joint=[(1, 0)]))
    cotan_rows, across_turned = lax.optimization_barrier((cotan_rows, fronts[near][2]))
    cotan, output, *terms = staged_call(
        gate_step,
        [shape_of((slots, width), bf16)] * 2 + term_shapes * near + own_shapes,
        (slot_maps, cotan_rows, scales, fronts[1][2], fronts[2][2], across_turned, fronts[0][2]),
        32,
    )
    logit_grad, router_halves, *preact_grads = staged_call(
        functools.partial(hidden_step, shards),
        [shape_of((slots, 128), f32), shape_of((2, half), f32)]
        + [shape_of((slots, hidden), bf16)] * shards,
        (output, *(p for k in range(shards) for p in (*downs[k], *fronts[k][:2])), scales, normed),
        28,
        scalars=(tower_word,),
        joint=[(1 + 4 * k, 1) for k in range(shards)],
    )

    def half_sum(first, swapped):
        return first.astype(f32) + swapped.astype(f32)

    swapped = [exchanged(terms[2 * term + 1], "tower", 1) for term in range(shards)]
    down_across = half_sum(terms[2 * near - 2], swapped[near - 1]).astype(bf16)
    router_column = router_halves
    router_column = router_column + exchanged(router_column, "tower", 1)
    logit_grad, router_column, down_across, swapped = lax.optimization_barrier(
        (logit_grad, router_column, down_across, swapped)
    )
    down_across = shifted(down_across, "y", 2)
    beside, beyond, farthest = (exchanged(router_column, "y", bit) for bit in (1, 2, 3))
    router_column = (router_column + beside) + (beyond + farthest)
    back_rows = staged_call(
        functools.partial(back_step, shards),
        [shape_of((experts * return_rows, half), bf16)],
        tuple(p for k in range(shards) for p in (preact_grads[k], *ups[k]))
        + (logit_grad, unit, cotan, scales, row_maps, gain, column),
        32,
        16 * shards * slots * width * hidden,
        scratch=[pltpu.VMEM((slots, width), f32)],
        joint=[(3 * k + 1, 0) for k in range(shards)],
    )[0]
    back_rows = local_call(
        tail_kernel,
        [pltpu.HBM((experts, return_rows, half), bf16)],
        (
            router_column,
            pltpu.with_memory_space_constraint(
                back_rows.reshape(experts, return_rows, half), pltpu.HBM
            ),
        ),
        8,
        in_specs=[
            pl.BlockSpec(memory_space=pltpu.VMEM),
            pl.BlockSpec(memory_space=pltpu.HBM),
        ],
        out_specs=[pl.BlockSpec(memory_space=pltpu.HBM)],
        input_output_aliases={1: 0},
        scratch_shapes=[
            pltpu.VMEM((experts, return_rows - 2 * capacity, half), bf16),
            pltpu.SemaphoreType.DMA,
        ],
    )[0]
    returned = spread(back_rows)
    swapped, down_across, _ = lax.optimization_barrier((swapped, down_across, back_rows))
    down_before = shifted(half_sum(terms[0], swapped[0]).astype(bf16), "y", -1)
    down_after = shifted(half_sum(terms[2], swapped[1]).astype(bf16), "y", 1)
    panel_rows, down_across = lax.optimization_barrier((panel_rows, down_across))
    embed_grads = pair_grads(
        local_member, panel_rows, logit_scale_log, pairwise_logit_bias, dp_index
    )
    embed_grads, down_before, down_after = lax.optimization_barrier(
        (embed_grads, down_before, down_after)
    )
    down_half = (
        half_sum(terms[2 * near], swapped[near])
        + down_before.astype(f32)
        + down_after.astype(f32)
        + down_across.astype(f32)
    )
    down_other = exchanged(down_half, "tower", 1)
    whole = pl.BlockSpec(memory_space=pltpu.VMEM)
    down_grad = local_call(
        joined_kernel,
        [shape_of((hidden, width), f32)],
        (tower_word, down_half, down_other),
        16,
        in_specs=[pl.BlockSpec(memory_space=pltpu.SMEM), whole, whole],
    )[0]
    embed_grads, token_maps = lax.optimization_barrier((embed_grads, token_maps))
    tokens_grad, router_rows = staged_call(
        functools.partial(token_step, experts, 2 * capacity),
        [shape_of((token_total, width), bf16), shape_of((experts, width), f32)],
        (token_maps, returned),
        20,
        1 << 34,
    )
    return (tokens_grad, router_rows.T, down_grad, embed_grads[None])


def solution(mesh):
    towers, chips = mesh.devices.shape
    grid = Mesh(
        mesh.devices.reshape(towers, chips // (columns * line), columns, line),
        ("tower", "z", "x", "y"),
    )
    dp = ("z", "x", "y")
    rows = P(("tower",) + dp, None)
    placed = (
        rows,
        P(),
        P(),
        rows,
        P(None, dp),
        P(dp, None),
        rows,
        P("tower", dp, None),
        P(),
        P(),
    )
    return jax.shard_map(
        body,
        mesh=grid,
        in_specs=placed,
        out_specs=(rows, P(), P(dp, None), P("tower", dp, None)),
        check_vma=False,
    )
```
